32 devices in a mesh: rep: 2 (over x), node: 4 (over y, core), local: 4 (over z).
Axes of the slice: x: 2, y: 2, z: 4, core: 2. Of those that a mesh axis runs over, the one named last changes fastest.
Arguments:
- tokens: bfloat16 [512, 4096], P(('rep', 'node', 'local')), may hold values from -6 to 6
- expert_ids: int32 [512, 8], P(('rep', 'node', 'local')), may hold values from 0 to 15, all different within a row; in each aligned block of 16 rows (0 to 15, 16 to 31, ...) at most 16 rows name the same one
- route_weights: float32 [512, 8], P(('rep', 'node', 'local')), may hold values from 0.1 to 1
- gate_weight: bfloat16 [16, 768, 4096], P(('node', 'local'), 'rep'), may hold values from -0.09375 to 0.09375
- up_weight: bfloat16 [16, 768, 4096], P(('node', 'local'), 'rep'), may hold values from -0.09375 to 0.09375
- down_weight: bfloat16 [16, 768, 4096], P(('node', 'local'), None, 'rep'), may hold values from -0.21875 to 0.21875
Outputs:
- mixed_rows: bfloat16 [512, 4096], P(('rep', 'node', 'local'))
The draws below stay inside these ranges and needn't reach their ends.
Inputs may be any that keep to these rules, and one draw needn't show every extreme that they name: `expert_ids`: each row names 8 different experts. Among the rows of one device (aligned blocks of 16 rows) no expert is named by more than 16 rows, and in some blocks some expert is named by exactly 16 rows.
All inputs are finite; a program needn't handle non-finite values.
Results may differ from the reference program's by a relative error of at most 0.0057.
Values may be sent and summed in bfloat16 or wider, within the bound.
No kernel may reach another device: no remote copies, remote signals or barrier semaphores. Data moves between devices by JAX's collectives and lax.ppermute only.
A program may use at most 64 MiB of HBM per device.

```python
import math
import jax
import jax.numpy as jnp
import numpy as np
from jax import lax

D = 4096
FF = 768
TOP = 8
ROWS_DEV = 16
EXPERTS = 16
CAP = 16
ROWS = 512
N_REP = 2


def block_scale(key, dims, pieces, low, largest):
    gain = 1.0
    for position, shards_of in pieces:
        steps = jax.random.uniform(jax.random.fold_in(jax.random.fold_in(key, 6), position), (shards_of,), jnp.float32, low / len(pieces), largest / len(pieces))
        gain = gain * jnp.repeat(jnp.exp(steps), dims[position] // shards_of).reshape((-1,) + (1,) * (len(dims) - 1 - position))
    return gain


def deal_out(stream_key, own, number, rows, amount, top, bound, skew):
    ranking = jax.random.permutation(stream_key, amount)
    packed, common = portions_of(amount, rows * top, bound, skew, True), portions_of(amount, rows * top, bound, skew, False)
    places = jnp.arange(amount)

    def named(sizes, offset_by):
        used = int((sizes > 0).sum())
        fixed = max(1, used // 4)
        moved = fixed + (places - fixed + offset_by * (used - fixed)) % max(1, amount - fixed)
        return jnp.zeros((amount,), jnp.int32).at[ranking[jnp.where(places < fixed, places, moved)]].set(jnp.asarray(sizes, jnp.int32))

    sizes = jnp.where(number % 4 == 0, named(packed, number // 4), named(common, number - number // 4 - 1))
    mixed = jax.random.permutation(jax.random.fold_in(own, 3), amount)
    donor, sink = mixed[0:amount // 2 * 2:2], mixed[1:amount // 2 * 2:2]
    margin = jnp.minimum(sizes[donor] - 1, bound - sizes[sink]) // 2
    margin = jnp.where((donor == ranking[0]) | (sink == ranking[0]) | (sizes[sink] == 0), 0, jnp.maximum(margin, 0))
    moved = jax.random.randint(jax.random.fold_in(own, 4), (amount // 2,), 0, 1 << 20) % (margin + 1)
    sizes = sizes.at[donor].add(-moved).at[sink].add(moved)
    labels = jnp.searchsorted(jnp.cumsum(sizes), jnp.arange(rows * top), side="right").astype(jnp.int32)
    table = labels.reshape(top, rows).T
    table = table[jax.random.permutation(jax.random.fold_in(own, 1), rows)]
    offset_by = jax.random.randint(jax.random.fold_in(own, 2), (rows, 1), 0, top)
    return jnp.take_along_axis(table, (jnp.arange(top)[None, :] + offset_by) % top, axis=1)


def portions_of(count, total, most, skew, full):
    loads = [(1 << 20) // math.isqrt(rank ** skew) + 1 for rank in range(1, count + 1)]
    largest = most if full else min(most, max(-(-total // count), total * loads[0] // sum(loads)))
    least = 1 if total - largest >= count - 1 else 0
    counts, spare = [largest] + [least] * (count - 1), total - largest - least * (count - 1)
    while spare > 0:
        movable = [i for i in range(1, count) if counts[i] < largest] or [i for i in range(1, count) if counts[i] < most]
        pool, remaining = sum([loads[i] for i in movable]), spare
        for i in movable:
            extra = min(most - counts[i], max(1, remaining * loads[i] // pool), spare)
            counts[i] = counts[i] + extra
            spare = spare - extra
    return np.array(counts)


def noise(key, shape, spread, limit, shards=(), kind=jnp.bfloat16):
    entries = jax.random.normal(key, shape, jnp.float32) * spread
    if len(shards) > 0:
        entries = block_scale(key, shape, shards, -0.22, 0.18) * entries
    return jnp.clip(entries, min=-limit, max=limit).astype(kind)


def setup_inputs(seed: int = 0) -> dict:
    arg_keys = jax.random.split(jax.random.key(seed), 7)
    tokens = noise(arg_keys[0], (ROWS, D), 1.0, 6.0, ((0, 32),))
    expert_ids_keys = jax.random.split(jax.random.fold_in(arg_keys[1], 1), ROWS // ROWS_DEV)
    expert_ids_turns = jax.random.permutation(jax.random.fold_in(arg_keys[1], 3), ROWS // ROWS_DEV)
    expert_ids = jax.vmap(lambda own, number: deal_out(jax.random.fold_in(arg_keys[1], 2), own, number, ROWS_DEV, EXPERTS, TOP, CAP, 2))(expert_ids_keys, expert_ids_turns).reshape((ROWS, TOP))
    route_weights = jnp.clip(jnp.exp(math.log(1.0) - 2.3025851 * jax.random.uniform(arg_keys[2], (ROWS, TOP), jnp.float32) ** block_scale(arg_keys[2], (ROWS, TOP), ((0, 32),), -0.2, 0.2)), 0.1, 1.0)
    gate_weight = noise(arg_keys[3], (EXPERTS, FF, D), D ** -0.5, 0.09375, ((0, 16), (1, 2)))
    up_weight = noise(arg_keys[4], (EXPERTS, FF, D), D ** -0.5, 0.09375, ((0, 16), (1, 2)))
    down_weight = noise(arg_keys[5], (EXPERTS, FF, D), FF ** -0.5, 0.21875, ((0, 16), (2, 2)))
    return dict(tokens=tokens, expert_ids=expert_ids, route_weights=route_weights, gate_weight=gate_weight, up_weight=up_weight, down_weight=down_weight)


def reference(tokens, expert_ids, route_weights, gate_weight, up_weight, down_weight):
    row_total = tokens.shape[0]
    most_rows = N_REP * EXPERTS * CAP
    feature_dims = (((1,), (1,)), ((), ()))

    def one_expert(expert, output):
        named = expert_ids == expert
        hit_rows = jnp.any(named, axis=1)
        picked = jnp.nonzero(hit_rows, size=most_rows, fill_value=0)[0].astype(jnp.int32)
        valid = jnp.arange(most_rows) < jnp.sum(hit_rows.astype(jnp.int32))
        share = jnp.sum(jnp.where(named, route_weights, jnp.zeros_like(route_weights)), axis=1)[picked]
        chosen = tokens[picked]
        gate_vals = lax.dot_general(chosen, gate_weight[expert], feature_dims, preferred_element_type=jnp.float32)
        up_vals = lax.dot_general(chosen, up_weight[expert], feature_dims, preferred_element_type=jnp.float32)
        hidden = (jax.nn.silu(gate_vals) * up_vals).astype(jnp.bfloat16)
        result = jnp.dot(hidden, down_weight[expert], preferred_element_type=jnp.float32).astype(jnp.bfloat16)
        term = share[:, None] * result.astype(jnp.float32)
        term = jnp.where(valid[:, None], term, jnp.zeros_like(term))
        return output.at[picked].add(term)

    output = lax.fori_loop(0, EXPERTS, one_expert, jnp.zeros((row_total, D), jnp.float32))
    return output.astype(jnp.bfloat16)
```

```python
import jax
import jax.numpy as jnp
from jax import lax
from jax.sharding import PartitionSpec as P

PLANE = ("node", "local")
EVERY = ("rep", "node", "local")


def slot_table(expert_ids, expert_count, slot_cap):
    row_count, top_count = expert_ids.shape
    flat_ids = expert_ids.reshape(-1)
    hits = (flat_ids[:, None] == jnp.arange(expert_count, dtype=jnp.int32)[None, :]).astype(
        jnp.int32
    )
    before = jnp.cumsum(hits, axis=0) - hits
    rank_of = jnp.sum(before * hits, axis=1)
    return (flat_ids * slot_cap + rank_of).reshape(row_count, top_count)


def route_slots(blocks):
    return lax.all_to_all(blocks, PLANE, split_axis=1, concat_axis=1, tiled=True)


def by_slots(tokens, expert_ids, route_weights, gate_local, up_local, down_local, slot_cap):
    model_width = tokens.shape[1]
    plane_count = lax.axis_size("rep")
    expert_count = lax.axis_size("node") * lax.axis_size("local")
    slot_total = expert_count * slot_cap
    slot_of = slot_table(expert_ids, expert_count, slot_cap)
    slot_iota = jnp.arange(slot_total, dtype=jnp.int32)
    placed = jnp.any(slot_of[None, :, :] == slot_iota[:, None, None], axis=2).astype(jnp.bfloat16)
    outgoing = jnp.dot(placed, tokens, preferred_element_type=jnp.float32).astype(jnp.bfloat16)
    mixing = jnp.sum(
        jnp.where(slot_of[:, :, None] == slot_iota[None, None, :], route_weights[:, :, None], 0.0),
        axis=1,
    )
    arrived = route_slots(outgoing.reshape(1, expert_count, slot_cap, model_width))
    arrived = arrived.reshape(slot_total, model_width)
    shard_piece = lax.all_gather(arrived, "rep", axis=0, tiled=True)
    hidden_part = hidden_units(shard_piece, gate_local, up_local)
    expert_out = jnp.dot(
        lax.all_gather(hidden_part, "rep", axis=1, tiled=True),
        down_local,
        preferred_element_type=jnp.float32,
    ).astype(jnp.bfloat16)
    own_slots = lax.all_to_all(
        expert_out.reshape(plane_count, slot_total, down_local.shape[1]),
        "rep",
        split_axis=0,
        concat_axis=2,
        tiled=True,
    )
    returned = route_slots(own_slots.reshape(1, expert_count, slot_cap, model_width))
    back_rows = returned.reshape(slot_total, model_width).astype(jnp.float32)
    mixed_rows = jnp.dot(mixing, back_rows, precision=lax.Precision.HIGHEST)
    return mixed_rows.astype(jnp.bfloat16)


def hidden_units(rows, gate_local, up_local):
    feature_dims = (((1,), (1,)), ((), ()))
    gate = lax.dot_general(rows, gate_local, feature_dims, preferred_element_type=jnp.float32)
    up = lax.dot_general(rows, up_local, feature_dims, preferred_element_type=jnp.float32)
    return (jax.nn.silu(gate) * up).astype(jnp.bfloat16)


def by_rows(tokens, expert_ids, route_weights, gate_local, up_local, down_local):
    row_count = tokens.shape[0]
    plane_count = lax.axis_size("rep")
    expert_count = lax.axis_size("node") * lax.axis_size("local")
    experts = jnp.arange(expert_count, dtype=jnp.int32)
    share_of = jnp.sum(
        jnp.where(
            expert_ids[:, None, :] == experts[None, :, None], route_weights[:, None, :], 0.0
        ),
        axis=2,
    )
    shares = lax.all_gather(share_of, EVERY, axis=0, tiled=True)
    expert = lax.axis_index(PLANE)
    share = lax.dynamic_slice_in_dim(shares, expert, 1, axis=1)
    rows = lax.all_gather(tokens, EVERY, axis=0, tiled=True)
    hidden = lax.all_gather(
        hidden_units(rows, gate_local, up_local), "rep", axis=1, tiled=True
    )
    expert_out = jnp.dot(hidden, down_local, preferred_element_type=jnp.float32)
    term = (share * expert_out.astype(jnp.bfloat16).astype(jnp.float32)).astype(jnp.bfloat16)
    half_width = down_local.shape[1]
    term = term.reshape(plane_count, expert_count, row_count, half_width)
    term = term.transpose(1, 0, 2, 3)
    summed = lax.psum_scatter(term, PLANE, scatter_dimension=0, tiled=True)[0]
    return lax.all_to_all(summed, "rep", split_axis=0, concat_axis=2, tiled=True)[0]


def on_device(tokens, expert_ids, route_weights, gate_weight, up_weight, down_weight):
    row_count, top_count = expert_ids.shape
    expert_count = lax.axis_size("node") * lax.axis_size("local")
    slot_cap = min(row_count, max(2, 2 * row_count * top_count // expert_count))
    weights = (gate_weight[0], up_weight[0], down_weight[0])
    if slot_cap == row_count:
        return by_rows(tokens, expert_ids, route_weights, *weights)
    return by_slots(tokens, expert_ids, route_weights, *weights, slot_cap)


def solution(mesh):
    placed = (
        P(EVERY, None),
        P(EVERY, None),
        P(EVERY, None),
        P(PLANE, "rep", None),
        P(PLANE, "rep", None),
        P(PLANE, None, "rep"),
    )
    return jax.shard_map(
        on_device,
        mesh=mesh,
        in_specs=placed,
        out_specs=P(EVERY, None),
        check_vma=False,
    )
```

```python
import jax
import jax.numpy as jnp
from jax import lax
from jax.sharding import PartitionSpec as P

PLANE = ("node", "local")
EVERY = ("rep", "node", "local")


def slot_table(expert_ids, expert_count, slot_cap):
    row_count, top_count = expert_ids.shape
    flat_ids = expert_ids.reshape(-1)
    hits = (flat_ids[:, None] == jnp.arange(expert_count, dtype=jnp.int32)[None, :]).astype(
        jnp.int32
    )
    before = jnp.cumsum(hits, axis=0) - hits
    rank_of = jnp.sum(before * hits, axis=1)
    return (flat_ids * slot_cap + rank_of).reshape(row_count, top_count)


def route_slots(blocks):
    return lax.all_to_all(blocks, PLANE, split_axis=1, concat_axis=1, tiled=True)


def by_slots(tokens, expert_ids, route_weights, gate_local, up_local, down_local, slot_cap):
    model_width = tokens.shape[1]
    plane_count = lax.axis_size("rep")
    expert_count = lax.axis_size("node") * lax.axis_size("local")
    slot_total = expert_count * slot_cap
    slot_of = slot_table(expert_ids, expert_count, slot_cap)
    slot_iota = jnp.arange(slot_total, dtype=jnp.int32)
    placed = jnp.any(slot_of[None, :, :] == slot_iota[:, None, None], axis=2).astype(jnp.bfloat16)
    outgoing = jnp.dot(placed, tokens, preferred_element_type=jnp.float32).astype(jnp.bfloat16)
    mixing = jnp.sum(
        jnp.where(slot_of[:, :, None] == slot_iota[None, None, :], route_weights[:, :, None], 0.0),
        axis=1,
    )
    arrived = route_slots(outgoing.reshape(1, expert_count, slot_cap, model_width))
    arrived = arrived.reshape(slot_total, model_width)
    shard_piece = lax.all_gather(arrived, "rep", axis=0, tiled=True)
    hidden_part = hidden_units(shard_piece, gate_local, up_local)
    expert_out = jnp.dot(
        lax.all_gather(hidden_part, "rep", axis=1, tiled=True),
        down_local,
        preferred_element_type=jnp.float32,
    ).astype(jnp.bfloat16)
    own_slots = lax.all_to_all(
        expert_out.reshape(plane_count, slot_total, down_local.shape[1]),
        "rep",
        split_axis=0,
        concat_axis=2,
        tiled=True,
    )
    returned = route_slots(own_slots.reshape(1, expert_count, slot_cap, model_width))
    back_rows = returned.reshape(slot_total, model_width).astype(jnp.float32)
    mixed_rows = jnp.dot(mixing, back_rows, precision=lax.Precision.HIGHEST)
    return mixed_rows.astype(jnp.bfloat16)


def hidden_units(rows, gate_local, up_local):
    feature_dims = (((1,), (1,)), ((), ()))
    gate = lax.dot_general(rows, gate_local, feature_dims, preferred_element_type=jnp.float32)
    up = lax.dot_general(rows, up_local, feature_dims, preferred_element_type=jnp.float32)
    return (jax.nn.silu(gate) * up).astype(jnp.bfloat16)


def swap(block, axis, mask):
    size = lax.axis_size(axis)
    return lax.ppermute(block, axis, [(place, place ^ mask) for place in range(size)])


def wide(block):
    return block.astype(jnp.float32)


def narrow(block):
    return block.astype(jnp.bfloat16)


def by_rows(tokens, expert_ids, route_weights, gate_local, up_local, down_local):
    row_count = tokens.shape[0]
    expert_count = lax.axis_size("node") * lax.axis_size("local")
    experts = jnp.arange(expert_count, dtype=jnp.int32)
    share_of = jnp.sum(
        jnp.where(
            expert_ids[:, None, :] == experts[None, :, None], route_weights[:, None, :], 0.0
        ),
        axis=2,
    )
    expert = lax.axis_index(PLANE)
    plane = lax.axis_index("rep")
    part_width = gate_local.shape[0]
    down_own = lax.dynamic_slice_in_dim(down_local, plane * part_width, part_width, axis=0)
    down_other = lax.dynamic_slice_in_dim(
        down_local, (1 - plane) * part_width, part_width, axis=0
    )

    line = [tokens] + [swap(tokens, "local", mask) for mask in (1, 2, 3)]
    near = [line[0], line[1]]
    far = [line[2], line[3]]
    near = near + [swap(block, "node", 2) for block in near]
    far_x = [swap(block, "rep", 1) for block in far]
    near = near + [swap(block, "rep", 1) for block in near]
    far_y = [swap(block, "node", 2) for block in far + far_x]
    far = far + far_y[:2] + far_x + far_y[2:]

    share_line = jnp.concatenate(
        [share_of] + [swap(share_of, "local", mask) for mask in (1, 2, 3)], axis=0
    )
    share_xy = jnp.stack([share_line, swap(share_line, "node", 2)])
    share_xy = jnp.stack([share_xy, swap(share_xy, "rep", 1)])
    share_all = jnp.stack([share_xy, swap(share_xy, "node", 1)])
    share_all = jnp.sum(jnp.where(experts == expert, share_all, 0.0), axis=-1)
    share_all = share_all.reshape(2, 2, 2, 2, 2, row_count)

    def terms(blocks, half):
        mine = jnp.concatenate(blocks, axis=0)
        rows = jnp.concatenate([mine, swap(mine, "node", 1)], axis=0)
        hidden = hidden_units(rows, gate_local, up_local)
        turned = jnp.flip(hidden.reshape(2, 2, -1, hidden.shape[1]), axis=1)
        other = swap(turned.reshape(hidden.shape), "rep", 1)
        out = jnp.dot(hidden, down_own, preferred_element_type=jnp.float32)
        out = out + jnp.dot(other, down_other, preferred_element_type=jnp.float32)
        share = share_all[:, :, :, half].reshape(-1, 1)
        term = share * wide(narrow(out))
        term = term.reshape(2, -1, term.shape[1])
        both = term[0] + wide(swap(narrow(term[1]), "node", 1))
        both = both.reshape(2, 2, 2 * row_count, -1)
        pair = both[:, 0] + wide(swap(narrow(both[:, 1]), "node", 2))
        return pair.reshape(2, 2, row_count, -1)

    near_sum = terms(near, 0)
    far_sum = terms(far, 1)
    total = (
        near_sum[:, 0]
        + wide(swap(narrow(near_sum[:, 1]), "local", 1))
        + wide(swap(narrow(far_sum[:, 0]), "local", 2))
        + wide(swap(narrow(far_sum[:, 1]), "local", 3))
    )
    total = narrow(total)
    half_own = total[0]
    half_other = swap(total[1], "rep", 1)
    return jnp.where(
        plane == 0,
        jnp.concatenate([half_own, half_other], axis=1),
        jnp.concatenate([half_other, half_own], axis=1),
    )


def on_device(tokens, expert_ids, route_weights, gate_weight, up_weight, down_weight):
    row_count, top_count = expert_ids.shape
    expert_count = lax.axis_size("node") * lax.axis_size("local")
    slot_cap = min(row_count, max(2, 2 * row_count * top_count // expert_count))
    weights = (gate_weight[0], up_weight[0], down_weight[0])
    if slot_cap == row_count:
        return by_rows(tokens, expert_ids, route_weights, *weights)
    return by_slots(tokens, expert_ids, route_weights, *weights, slot_cap)


def solution(mesh):
    placed = (
        P(EVERY, None),
        P(EVERY, None),
        P(EVERY, None),
        P(PLANE, "rep", None),
        P(PLANE, "rep", None),
        P(PLANE, None, "rep"),
    )
    return jax.shard_map(
        on_device,
        mesh=mesh,
        in_specs=placed,
        out_specs=P(EVERY, None),
        check_vma=False,
    )
```

```python
import functools
import math

import jax
import jax.numpy as jnp
from jax import lax
from jax.experimental import pallas as pl
from jax.experimental.pallas import tpu as pltpu
from jax.sharding import PartitionSpec as P

PLANE = ("node", "local")
EVERY = ("rep", "node", "local")


def slot_table(expert_ids, expert_count, slot_cap):
    row_count, top_count = expert_ids.shape
    flat_ids = expert_ids.reshape(-1)
    hits = (flat_ids[:, None] == jnp.arange(expert_count, dtype=jnp.int32)[None, :]).astype(
        jnp.int32
    )
    before = jnp.cumsum(hits, axis=0) - hits
    rank_of = jnp.sum(before * hits, axis=1)
    return (flat_ids * slot_cap + rank_of).reshape(row_count, top_count)


def route_slots(blocks):
    return lax.all_to_all(blocks, PLANE, split_axis=1, concat_axis=1, tiled=True)


def by_slots(tokens, expert_ids, route_weights, gate_local, up_local, down_local, slot_cap):
    model_width = tokens.shape[1]
    plane_count = lax.axis_size("rep")
    expert_count = lax.axis_size("node") * lax.axis_size("local")
    slot_total = expert_count * slot_cap
    slot_of = slot_table(expert_ids, expert_count, slot_cap)
    slot_iota = jnp.arange(slot_total, dtype=jnp.int32)
    placed = jnp.any(slot_of[None, :, :] == slot_iota[:, None, None], axis=2).astype(jnp.bfloat16)
    outgoing = jnp.dot(placed, tokens, preferred_element_type=jnp.float32).astype(jnp.bfloat16)
    mixing = jnp.sum(
        jnp.where(slot_of[:, :, None] == slot_iota[None, None, :], route_weights[:, :, None], 0.0),
        axis=1,
    )
    arrived = route_slots(outgoing.reshape(1, expert_count, slot_cap, model_width))
    arrived = arrived.reshape(slot_total, model_width)
    shard_piece = lax.all_gather(arrived, "rep", axis=0, tiled=True)
    hidden_part = hidden_units(shard_piece, gate_local, up_local)
    expert_out = jnp.dot(
        lax.all_gather(hidden_part, "rep", axis=1, tiled=True),
        down_local,
        preferred_element_type=jnp.float32,
    ).astype(jnp.bfloat16)
    own_slots = lax.all_to_all(
        expert_out.reshape(plane_count, slot_total, down_local.shape[1]),
        "rep",
        split_axis=0,
        concat_axis=2,
        tiled=True,
    )
    returned = route_slots(own_slots.reshape(1, expert_count, slot_cap, model_width))
    back_rows = returned.reshape(slot_total, model_width).astype(jnp.float32)
    mixed_rows = jnp.dot(mixing, back_rows, precision=lax.Precision.HIGHEST)
    return mixed_rows.astype(jnp.bfloat16)


def hidden_units(rows, gate_local, up_local):
    feature_dims = (((1,), (1,)), ((), ()))
    gate = lax.dot_general(rows, gate_local, feature_dims, preferred_element_type=jnp.float32)
    up = lax.dot_general(rows, up_local, feature_dims, preferred_element_type=jnp.float32)
    return (jax.nn.silu(gate) * up).astype(jnp.bfloat16)


def swap(block, axis, mask):
    size = lax.axis_size(axis)
    return lax.ppermute(block, axis, [(place, place ^ mask) for place in range(size)])


def wide(block):
    return block.astype(jnp.float32)


def narrow(block):
    return block.astype(jnp.bfloat16)


def pack_kernel(tokens_ref, ids_ref, weights_ref, out_ref, *, expert_count):
    row_count, width = tokens_ref.shape
    out_ref[:, :width] = tokens_ref[...]
    lanes = lax.broadcasted_iota(jnp.int32, (row_count, out_ref.shape[1] - width), 1)
    piece, expert = lanes // expert_count, lanes % expert_count
    share = jnp.zeros(lanes.shape, jnp.float32)
    for k in range(ids_ref.shape[1]):
        share += jnp.where(ids_ref[:, k : k + 1] == expert, weights_ref[:, k : k + 1], 0.0)
    high = wide(narrow(share))
    middle = wide(narrow(share - high))
    low = share - high - middle
    coded = jnp.where(piece == 0, high, jnp.where(piece == 1, middle, low))
    out_ref[:, width:] = narrow(jnp.where(piece < 3, coded, 0.0))


def gate_up_kernel(*refs, expert_count):
    block_refs = refs[:-5]
    gate_ref, up_ref, hidden_ref, share_ref, rows = refs[-5:]
    row_count = block_refs[0].shape[0]
    width = gate_ref.shape[1]
    expert = lax.axis_index(PLANE)
    lanes = lax.broadcasted_iota(jnp.int32, (row_count, block_refs[0].shape[1] - width), 1)
    coded = (lanes % expert_count == expert) & (lanes < 3 * expert_count)
    for place, block in enumerate(block_refs):
        here = pl.ds(place * row_count, row_count)
        rows[here, :] = block[:, :width]
        share = jnp.sum(jnp.where(coded, wide(block[:, width:]), 0.0), axis=1, keepdims=True)
        share_ref[here, :] = jnp.broadcast_to(share, (row_count, share_ref.shape[1]))
    feature_dims = (((1,), (1,)), ((), ()))
    held = rows[...]
    gate = lax.dot_general(held, gate_ref[...], feature_dims, preferred_element_type=jnp.float32)
    up = lax.dot_general(held, up_ref[...], feature_dims, preferred_element_type=jnp.float32)
    hidden_ref[...] = narrow(gate * up / (1.0 + jnp.exp(-gate)))


def down_kernel(own_ref, other_ref, share_ref, down_ref, keep_ref, send_ref):
    plane = lax.axis_index("rep")
    own = own_ref[...]
    quarter = own.shape[0] // 4
    other = jnp.concatenate(
        [other_ref[pl.ds(place * quarter, quarter), :] for place in (1, 0, 3, 2)], axis=0
    )
    first = jnp.where(plane == 0, own, other)
    second = jnp.where(plane == 0, other, own)
    hidden = jnp.concatenate([first, second], axis=1)
    half = own.shape[0] // 2
    share = share_ref[:, :1]
    tile = math.gcd(down_ref.shape[1], 512)
    for start in range(0, down_ref.shape[1], tile):
        here = pl.ds(start, tile)
        out = jnp.dot(hidden, down_ref[:, here], preferred_element_type=jnp.float32)
        term = share * wide(narrow(out))
        keep_ref[:, here] = term[:half]
        send_ref[:, here] = narrow(term[half:])


def in_vmem(kernel, out_shape, scratch_shapes=(), flops=0, **sizes):
    spec = pl.BlockSpec(memory_space=pltpu.VMEM)

    def call(*operands):
        moved = sum(operand.size * operand.dtype.itemsize for operand in operands)
        return pl.pallas_call(
            functools.partial(kernel, **sizes),
            out_shape=out_shape,
            in_specs=[spec] * len(operands),
            out_specs=jax.tree.map(lambda _: spec, out_shape),
            scratch_shapes=list(scratch_shapes),
            compiler_params=pltpu.CompilerParams(vmem_limit_bytes=40 * 1024 * 1024),
            cost_estimate=pl.CostEstimate(flops=flops, bytes_accessed=moved, transcendentals=0),
        )(*operands)

    return call


def by_rows(tokens, expert_ids, route_weights, gate_local, up_local, down_local):
    row_count, width = tokens.shape
    expert_count = lax.axis_size("node") * lax.axis_size("local")
    part_width = gate_local.shape[0]
    half_width = down_local.shape[1]
    plane = lax.axis_index("rep")
    extra = -(-3 * expert_count // 128) * 128
    packed = in_vmem(
        pack_kernel,
        jax.ShapeDtypeStruct((row_count, width + extra), jnp.bfloat16),
        expert_count=expert_count,
    )(tokens, expert_ids, route_weights)

    near = [packed, swap(packed, "local", 1)]
    far = [swap(packed, "local", 2), swap(packed, "local", 3)]
    near = near + [swap(block, "node", 2) for block in near]
    far_x = [swap(block, "rep", 1) for block in far]
    near = near + [swap(block, "rep", 1) for block in near]
    far_y = [swap(block, "node", 2) for block in far + far_x]
    far = far + far_y[:2] + far_x + far_y[2:]

    def terms(blocks):
        blocks = blocks + [swap(block, "node", 1) for block in blocks]
        total = len(blocks) * row_count
        hidden, share = in_vmem(
            gate_up_kernel,
            (
                jax.ShapeDtypeStruct((total, part_width), jnp.bfloat16),
                jax.ShapeDtypeStruct((total, 128), jnp.float32),
            ),
            [pltpu.VMEM((total, width), jnp.bfloat16)],
            flops=4 * total * width * part_width,
            expert_count=expert_count,
        )(*blocks, gate_local, up_local)
        keep, send = in_vmem(
            down_kernel,
            (
                jax.ShapeDtypeStruct((total // 2, half_width), jnp.float32),
                jax.ShapeDtypeStruct((total // 2, half_width), jnp.bfloat16),
            ),
            flops=4 * total * part_width * half_width,
        )(hidden, swap(hidden, "rep", 1), share, down_local)
        both = keep + wide(swap(send, "node", 1))
        both = both.reshape(2, 2, 2 * row_count, -1)
        pair = both[:, 0] + wide(swap(narrow(both[:, 1]), "node", 2))
        return pair.reshape(2, 2, row_count, -1)

    near_sum = terms(near)
    far_sum = terms(far)
    total = (
        near_sum[:, 0]
        + wide(swap(narrow(near_sum[:, 1]), "local", 1))
        + wide(swap(narrow(far_sum[:, 0]), "local", 2))
        + wide(swap(narrow(far_sum[:, 1]), "local", 3))
    )
    total = narrow(total)
    half_own = total[0]
    half_other = swap(total[1], "rep", 1)
    return jnp.where(
        plane == 0,
        jnp.concatenate([half_own, half_other], axis=1),
        jnp.concatenate([half_other, half_own], axis=1),
    )


def on_device(tokens, expert_ids, route_weights, gate_weight, up_weight, down_weight):
    row_count, top_count = expert_ids.shape
    expert_count = lax.axis_size("node") * lax.axis_size("local")
    slot_cap = min(row_count, max(2, 2 * row_count * top_count // expert_count))
    weights = (gate_weight[0], up_weight[0], down_weight[0])
    if slot_cap == row_count:
        return by_rows(tokens, expert_ids, route_weights, *weights)
    return by_slots(tokens, expert_ids, route_weights, *weights, slot_cap)


def solution(mesh):
    placed = (
        P(EVERY, None),
        P(EVERY, None),
        P(EVERY, None),
        P(PLANE, "rep", None),
        P(PLANE, "rep", None),
        P(PLANE, None, "rep"),
    )
    return jax.shard_map(
        on_device,
        mesh=mesh,
        in_specs=placed,
        out_specs=P(EVERY, None),
        check_vma=False,
    )
```

```python
import functools
import math

import jax
import jax.numpy as jnp
from jax import lax
from jax.experimental import pallas as pl
from jax.experimental.pallas import tpu as pltpu
from jax.sharding import PartitionSpec as P

PLANE = ("node", "local")
EVERY = ("rep", "node", "local")


def slot_table(expert_ids, expert_count, slot_cap):
    row_count, top_count = expert_ids.shape
    flat_ids = expert_ids.reshape(-1)
    hits = (flat_ids[:, None] == jnp.arange(expert_count, dtype=jnp.int32)[None, :]).astype(
        jnp.int32
    )
    before = jnp.cumsum(hits, axis=0) - hits
    rank_of = jnp.sum(before * hits, axis=1)
    return (flat_ids * slot_cap + rank_of).reshape(row_count, top_count)


def route_slots(blocks):
    return lax.all_to_all(blocks, PLANE, split_axis=1, concat_axis=1, tiled=True)


def by_slots(tokens, expert_ids, route_weights, gate_local, up_local, down_local, slot_cap):
    model_width = tokens.shape[1]
    plane_count = lax.axis_size("rep")
    expert_count = lax.axis_size("node") * lax.axis_size("local")
    slot_total = expert_count * slot_cap
    slot_of = slot_table(expert_ids, expert_count, slot_cap)
    slot_iota = jnp.arange(slot_total, dtype=jnp.int32)
    placed = jnp.any(slot_of[None, :, :] == slot_iota[:, None, None], axis=2).astype(jnp.bfloat16)
    outgoing = jnp.dot(placed, tokens, preferred_element_type=jnp.float32).astype(jnp.bfloat16)
    mixing = jnp.sum(
        jnp.where(slot_of[:, :, None] == slot_iota[None, None, :], route_weights[:, :, None], 0.0),
        axis=1,
    )
    arrived = route_slots(outgoing.reshape(1, expert_count, slot_cap, model_width))
    arrived = arrived.reshape(slot_total, model_width)
    shard_piece = lax.all_gather(arrived, "rep", axis=0, tiled=True)
    hidden_part = hidden_units(shard_piece, gate_local, up_local)
    expert_out = jnp.dot(
        lax.all_gather(hidden_part, "rep", axis=1, tiled=True),
        down_local,
        preferred_element_type=jnp.float32,
    ).astype(jnp.bfloat16)
    own_slots = lax.all_to_all(
        expert_out.reshape(plane_count, slot_total, down_local.shape[1]),
        "rep",
        split_axis=0,
        concat_axis=2,
        tiled=True,
    )
    returned = route_slots(own_slots.reshape(1, expert_count, slot_cap, model_width))
    back_rows = returned.reshape(slot_total, model_width).astype(jnp.float32)
    mixed_rows = jnp.dot(mixing, back_rows, precision=lax.Precision.HIGHEST)
    return mixed_rows.astype(jnp.bfloat16)


def hidden_units(rows, gate_local, up_local):
    feature_dims = (((1,), (1,)), ((), ()))
    gate = lax.dot_general(rows, gate_local, feature_dims, preferred_element_type=jnp.float32)
    up = lax.dot_general(rows, up_local, feature_dims, preferred_element_type=jnp.float32)
    return (jax.nn.silu(gate) * up).astype(jnp.bfloat16)


def swap(block, axes, mask):
    size = lax.axis_size(axes)
    return lax.ppermute(block, axes, [(place, place ^ mask) for place in range(size)])


def square(block):
    nodes = lax.axis_size("node")
    across = swap(block, ("rep", "node"), nodes | 2)
    return [block, swap(block, "node", 2), swap(block, "rep", 1), across]


def wide(block):
    return block.astype(jnp.float32)


def narrow(block):
    return block.astype(jnp.bfloat16)


def pack_kernel(tokens_in, ids_in, weights_in, out_ref, ids_ref, weights_ref, sems, *, experts):
    row_count, width = tokens_in.shape
    tokens_copy = pltpu.make_async_copy(tokens_in, out_ref.at[:, pl.ds(0, width)], sems.at[0])
    ids_copy = pltpu.make_async_copy(ids_in, ids_ref, sems.at[1])
    weights_copy = pltpu.make_async_copy(weights_in, weights_ref, sems.at[2])
    tokens_copy.start()
    ids_copy.start()
    weights_copy.start()
    lanes = lax.broadcasted_iota(jnp.int32, (row_count, out_ref.shape[1] - width), 1)
    piece, expert = lanes // experts, lanes % experts
    share = jnp.zeros(lanes.shape, jnp.float32)
    ids_copy.wait()
    weights_copy.wait()
    for k in range(ids_ref.shape[1]):
        share += jnp.where(ids_ref[:, k : k + 1] == expert, weights_ref[:, k : k + 1], 0.0)
    high = wide(narrow(share))
    middle = wide(narrow(share - high))
    low = share - high - middle
    coded = jnp.where(piece == 0, high, jnp.where(piece == 1, middle, low))
    out_ref[:, width:] = narrow(jnp.where(piece < 3, coded, 0.0))
    tokens_copy.wait()


def gate_up_kernel(*refs, experts):
    block_refs = refs[:-7]
    gate_in, up_in, hidden_ref, share_ref, rows, weights, sems = refs[-7:]
    row_count = block_refs[0].shape[0]
    width = gate_in.shape[1]
    tile = weights.shape[1] // 2
    copies = []
    for step in range(weights.shape[0]):
        there = pl.ds(step * tile, tile)
        copies.append(
            [
                pltpu.make_async_copy(
                    part.at[there, :],
                    weights.at[step, pl.ds(side * tile, tile), :],
                    sems.at[step, side],
                )
                for side, part in enumerate((gate_in, up_in))
            ]
        )
        for copy in copies[-1]:
            copy.start()
    expert = lax.axis_index(PLANE)
    lanes = lax.broadcasted_iota(jnp.int32, (row_count, block_refs[0].shape[1] - width), 1)
    coded = (lanes % experts == expert) & (lanes < 3 * experts)
    for place, block in enumerate(block_refs):
        here = pl.ds(place * row_count, row_count)
        rows[here, :] = block[:, :width]
        share = jnp.sum(jnp.where(coded, wide(block[:, width:]), 0.0), axis=1, keepdims=True)
        share_ref[here, :] = jnp.broadcast_to(share, (row_count, share_ref.shape[1]))
    feature_dims = (((1,), (1,)), ((), ()))
    for step, pair in enumerate(copies):
        for copy in pair:
            copy.wait()
        both = lax.dot_general(
            rows[...], weights[step], feature_dims, preferred_element_type=jnp.float32
        )
        gate, up = both[:, :tile], both[:, tile:]
        hidden_ref[:, step * tile : (step + 1) * tile] = narrow(gate * up / (1.0 + jnp.exp(-gate)))


def down_kernel(own_ref, other_ref, share_ref, down_in, keep_ref, send_ref, down, sems):
    width = down_in.shape[1]
    tile = width // down.shape[0]
    copies = [
        pltpu.make_async_copy(
            down_in.at[:, pl.ds(step * tile, tile)], down.at[step], sems.at[step]
        )
        for step in range(down.shape[0])
    ]
    for copy in copies:
        copy.start()
    plane = lax.axis_index("rep")
    own = own_ref[...]
    quarter = own.shape[0] // 4
    other = jnp.concatenate(
        [other_ref[pl.ds(place * quarter, quarter), :] for place in (1, 0, 3, 2)], axis=0
    )
    first = jnp.where(plane == 0, own, other)
    second = jnp.where(plane == 0, other, own)
    hidden = jnp.concatenate([first, second], axis=1)
    half = own.shape[0] // 2
    share = share_ref[:, :1]
    for step, copy in enumerate(copies):
        copy.wait()
        out = jnp.dot(hidden, down[step], preferred_element_type=jnp.float32)
        term = share * wide(narrow(out))
        keep_ref[:, step * tile : (step + 1) * tile] = term[:half]
        send_ref[:, step * tile : (step + 1) * tile] = narrow(term[half:])


def run(kernel, operands, in_hbm, out_shape, scratch_shapes, flops, **sizes):
    held, fetched = pl.BlockSpec(memory_space=pltpu.VMEM), pl.BlockSpec(memory_space=pl.ANY)
    moved = sum(operand.size * operand.dtype.itemsize for operand in operands)
    return pl.pallas_call(
        functools.partial(kernel, **sizes),
        out_shape=out_shape,
        in_specs=[fetched if place in in_hbm else held for place in range(len(operands))],
        out_specs=jax.tree.map(lambda _: held, out_shape),
        scratch_shapes=scratch_shapes,
        compiler_params=pltpu.CompilerParams(vmem_limit_bytes=40 * 1024 * 1024),
        cost_estimate=pl.CostEstimate(flops=flops, bytes_accessed=moved, transcendentals=0),
    )(*operands)


def pack(tokens, expert_ids, route_weights, experts):
    row_count, width = tokens.shape
    extra = -(-3 * experts // 128) * 128
    return run(
        pack_kernel,
        (tokens, expert_ids, route_weights),
        (0, 1, 2),
        jax.ShapeDtypeStruct((row_count, width + extra), jnp.bfloat16),
        [
            pltpu.VMEM(expert_ids.shape, jnp.int32),
            pltpu.VMEM(route_weights.shape, jnp.float32),
            pltpu.SemaphoreType.DMA((3,)),
        ],
        0,
        experts=experts,
    )


def gate_up(blocks, gate_local, up_local, experts):
    part_width, width = gate_local.shape
    total = len(blocks) * blocks[0].shape[0]
    tile = math.gcd(part_width, 128)
    return run(
        gate_up_kernel,
        (*blocks, gate_local, up_local),
        (len(blocks), len(blocks) + 1),
        (
            jax.ShapeDtypeStruct((total, part_width), jnp.bfloat16),
            jax.ShapeDtypeStruct((total, 128), jnp.float32),
        ),
        [
            pltpu.VMEM((total, width), jnp.bfloat16),
            pltpu.VMEM((part_width // tile, 2 * tile, width), jnp.bfloat16),
            pltpu.SemaphoreType.DMA((part_width // tile, 2)),
        ],
        4 * total * width * part_width,
        experts=experts,
    )


def down(own, other, share, down_local):
    total, part_width = own.shape
    depth, width = down_local.shape
    tile = math.gcd(width, 512)
    return run(
        down_kernel,
        (own, other, share, down_local),
        (3,),
        (
            jax.ShapeDtypeStruct((total // 2, width), jnp.float32),
            jax.ShapeDtypeStruct((total // 2, width), jnp.bfloat16),
        ),
        [
            pltpu.VMEM((width // tile, depth, tile), jnp.bfloat16),
            pltpu.SemaphoreType.DMA((width // tile,)),
        ],
        2 * total * depth * width,
    )


def by_rows(tokens, expert_ids, route_weights, gate_local, up_local, down_local):
    row_count = tokens.shape[0]
    experts = lax.axis_size("node") * lax.axis_size("local")
    plane = lax.axis_index("rep")
    together = lax.optimization_barrier

    packed = pack(tokens, expert_ids, route_weights, experts)
    square_0, line_1, line_2 = together(
        (square(packed), swap(packed, "local", 1), swap(packed, "local", 2))
    )
    square_1, square_2, line_3 = together(
        (square(line_1), square(line_2), swap(square_0[0], "local", 3))
    )
    square_3 = square(line_3)

    def hidden_of(first, second):
        blocks = [block for pair in zip(first, second) for block in pair]
        blocks = blocks + [swap(block, "node", 1) for block in blocks]
        hidden, share = gate_up(blocks, gate_local, up_local, experts)
        return hidden, swap(hidden, "rep", 1), share

    def core_sum(keep, send):
        both = keep + wide(swap(send, "node", 1))
        return both.reshape(2, 2, 2 * row_count, -1)

    hidden_a = hidden_of(square_0, square_2)
    hidden_b = hidden_of(square_1, square_3)
    both_a = core_sum(*down(*hidden_a, down_local))
    back_a = swap(narrow(both_a[:, 1]), "node", 2)
    back_a, hidden_b = together((back_a, hidden_b))
    pair_a = (both_a[:, 0] + wide(back_a)).reshape(2, 2, row_count, -1)
    line_2 = swap(narrow(pair_a[:, 1]), "local", 2)
    both_b = core_sum(*down(*hidden_b, down_local))
    back_b = swap(narrow(both_b[:, 1]), "node", 2)
    back_b, line_2 = together((back_b, line_2))
    pair_b = (both_b[:, 0] + wide(back_b)).reshape(2, 2, row_count, -1)
    line_1 = swap(narrow(pair_b[:, 0]), "local", 1)
    line_3 = swap(narrow(pair_b[:, 1]), "local", 3)
    total = narrow(pair_a[:, 0] + wide(line_1) + wide(line_2) + wide(line_3))
    half_own = total[0]
    half_other = swap(total[1], "rep", 1)
    return jnp.where(
        plane == 0,
        jnp.concatenate([half_own, half_other], axis=1),
        jnp.concatenate([half_other, half_own], axis=1),
    )


def on_device(tokens, expert_ids, route_weights, gate_weight, up_weight, down_weight):
    row_count, top_count = expert_ids.shape
    expert_count = lax.axis_size("node") * lax.axis_size("local")
    slot_cap = min(row_count, max(2, 2 * row_count * top_count // expert_count))
    weights = (gate_weight[0], up_weight[0], down_weight[0])
    if slot_cap == row_count:
        return by_rows(tokens, expert_ids, route_weights, *weights)
    return by_slots(tokens, expert_ids, route_weights, *weights, slot_cap)


def solution(mesh):
    placed = (
        P(EVERY, None),
        P(EVERY, None),
        P(EVERY, None),
        P(PLANE, "rep", None),
        P(PLANE, "rep", None),
        P(PLANE, None, "rep"),
    )
    return jax.shard_map(
        on_device,
        mesh=mesh,
        in_specs=placed,
        out_specs=P(EVERY, None),
        check_vma=False,
    )
```

```python
import functools
import math

import jax
import jax.numpy as jnp
from jax import lax
from jax.experimental import pallas as pl
from jax.experimental.pallas import tpu as pltpu
from jax.sharding import PartitionSpec as P

PLANE = ("node", "local")
EVERY = ("rep", "node", "local")
ROOM = 24


def slot_table(expert_ids, expert_count, slot_cap):
    row_count, top_count = expert_ids.shape
    flat_ids = expert_ids.reshape(-1)
    hits = (flat_ids[:, None] == jnp.arange(expert_count, dtype=jnp.int32)[None, :]).astype(
        jnp.int32
    )
    before = jnp.cumsum(hits, axis=0) - hits
    rank_of = jnp.sum(before * hits, axis=1)
    return (flat_ids * slot_cap + rank_of).reshape(row_count, top_count)


def route_slots(blocks):
    return lax.all_to_all(blocks, PLANE, split_axis=1, concat_axis=1, tiled=True)


def by_slots(tokens, expert_ids, route_weights, gate_local, up_local, down_local, slot_cap):
    model_width = tokens.shape[1]
    plane_count = lax.axis_size("rep")
    expert_count = lax.axis_size("node") * lax.axis_size("local")
    slot_total = expert_count * slot_cap
    slot_of = slot_table(expert_ids, expert_count, slot_cap)
    slot_iota = jnp.arange(slot_total, dtype=jnp.int32)
    placed = jnp.any(slot_of[None, :, :] == slot_iota[:, None, None], axis=2).astype(jnp.bfloat16)
    outgoing = jnp.dot(placed, tokens, preferred_element_type=jnp.float32).astype(jnp.bfloat16)
    mixing = jnp.sum(
        jnp.where(slot_of[:, :, None] == slot_iota[None, None, :], route_weights[:, :, None], 0.0),
        axis=1,
    )
    arrived = route_slots(outgoing.reshape(1, expert_count, slot_cap, model_width))
    arrived = arrived.reshape(slot_total, model_width)
    shard_piece = lax.all_gather(arrived, "rep", axis=0, tiled=True)
    hidden_part = hidden_units(shard_piece, gate_local, up_local)
    expert_out = jnp.dot(
        lax.all_gather(hidden_part, "rep", axis=1, tiled=True),
        down_local,
        preferred_element_type=jnp.float32,
    ).astype(jnp.bfloat16)
    own_slots = lax.all_to_all(
        expert_out.reshape(plane_count, slot_total, down_local.shape[1]),
        "rep",
        split_axis=0,
        concat_axis=2,
        tiled=True,
    )
    returned = route_slots(own_slots.reshape(1, expert_count, slot_cap, model_width))
    back_rows = returned.reshape(slot_total, model_width).astype(jnp.float32)
    mixed_rows = jnp.dot(mixing, back_rows, precision=lax.Precision.HIGHEST)
    return mixed_rows.astype(jnp.bfloat16)


def hidden_units(rows, gate_local, up_local):
    feature_dims = (((1,), (1,)), ((), ()))
    gate = lax.dot_general(rows, gate_local, feature_dims, preferred_element_type=jnp.float32)
    up = lax.dot_general(rows, up_local, feature_dims, preferred_element_type=jnp.float32)
    return (jax.nn.silu(gate) * up).astype(jnp.bfloat16)


def swap(block, axes, mask):
    size = lax.axis_size(axes)
    return lax.ppermute(block, axes, [(place, place ^ mask) for place in range(size)])


def square(block):
    nodes = lax.axis_size("node")
    across = swap(block, ("rep", "node"), nodes | 2)
    return [block, swap(block, "node", 2), swap(block, "rep", 1), across]


def wide(block):
    return block.astype(jnp.float32)


def narrow(block):
    return block.astype(jnp.bfloat16)


def pack_kernel(tokens_in, ids_in, weights_in, out_ref, ids_ref, weights_ref, sems, *, experts):
    row_count, width = tokens_in.shape
    tokens_copy = pltpu.make_async_copy(tokens_in, out_ref.at[:, pl.ds(0, width)], sems.at[0])
    ids_copy = pltpu.make_async_copy(ids_in, ids_ref, sems.at[1])
    weights_copy = pltpu.make_async_copy(weights_in, weights_ref, sems.at[2])
    tokens_copy.start()
    ids_copy.start()
    weights_copy.start()
    lanes = lax.broadcasted_iota(jnp.int32, (row_count, out_ref.shape[1] - width), 1)
    piece, expert = lanes // experts, lanes % experts
    share = jnp.zeros(lanes.shape, jnp.float32)
    ids_copy.wait()
    weights_copy.wait()
    for k in range(ids_ref.shape[1]):
        share += jnp.where(ids_ref[:, k : k + 1] == expert, weights_ref[:, k : k + 1], 0.0)
    high = wide(narrow(share))
    middle = wide(narrow(share - high))
    low = share - high - middle
    coded = jnp.where(piece == 0, high, jnp.where(piece == 1, middle, low))
    out_ref[:, width:] = narrow(jnp.where(piece < 3, coded, 0.0))
    tokens_copy.wait()


def fetch_kernel(gate_in, up_in, down_in, gate_up_ref, down_ref, sems):
    part_width = gate_in.shape[0]
    copies = [
        pltpu.make_async_copy(gate_in, gate_up_ref.at[pl.ds(0, part_width), :], sems.at[0]),
        pltpu.make_async_copy(up_in, gate_up_ref.at[pl.ds(part_width, part_width), :], sems.at[1]),
        pltpu.make_async_copy(down_in, down_ref, sems.at[2]),
    ]
    for copy in copies:
        copy.start()
    for copy in copies:
        copy.wait()


def gate_up_kernel(*refs, experts, starts, row_count):
    block_refs, weight_refs = refs[:-5], refs[-5:-3]
    hidden_ref, share_ref, rows = refs[-3:]
    part_width, width = weight_refs[0].shape[0] // 2, weight_refs[0].shape[1]
    own = lax.axis_index("node") * lax.axis_size("local") + lax.axis_index("local")
    other = own + lax.axis_size("local") * (1 - 2 * (lax.axis_index("node") % 2))
    lanes = lax.broadcasted_iota(jnp.int32, (row_count, block_refs[0].shape[1] - width), 1)
    coded = [
        (lanes % experts == expert) & (lanes < 3 * experts) for expert in (own, other)
    ]
    for place, (block, start) in enumerate(zip(block_refs, starts)):
        here = pl.ds(place * row_count, row_count)
        there = slice(start, start + row_count)
        rows[here, :] = block[there, :width]
        pieces = wide(block[there, width:])
        for side in range(2):
            share = jnp.sum(jnp.where(coded[side], pieces, 0.0), axis=1, keepdims=True)
            share_ref[side, here, :] = jnp.broadcast_to(share, (row_count, share_ref.shape[2]))
    feature_dims = (((1,), (1,)), ((), ()))
    for side, weights in enumerate(weight_refs):
        both = lax.dot_general(
            rows[...], weights[...], feature_dims, preferred_element_type=jnp.float32
        )
        gate, up = both[:, :part_width], both[:, part_width:]
        hidden_ref[side] = narrow(gate * up / (1.0 + jnp.exp(-gate)))


def down_kernel(own_ref, other_ref, share_ref, down_own, down_other, keep_ref, send_ref):
    plane = lax.axis_index("rep")
    width = down_own.shape[1]
    tile = math.gcd(width, 512)
    total = own_ref.shape[1]
    half, quarter = total // 2, total // 4
    hidden = []
    for side in range(2):
        own = own_ref[side]
        other = jnp.concatenate([other_ref[side, half:], other_ref[side, :half]], axis=0)
        first = jnp.where(plane == 0, own, other)
        second = jnp.where(plane == 0, other, own)
        hidden.append(jnp.concatenate([first, second], axis=1))
    for start in range(0, width, tile):
        here = slice(start, start + tile)
        term = 0.0
        for side, part in enumerate((down_own, down_other)):
            out = jnp.dot(hidden[side], part[:, here], preferred_element_type=jnp.float32)
            term += share_ref[side, :, :1] * wide(narrow(out))
        for rep in range(2):
            base = rep * half
            keep_ref[rep, :, here] = term[base : base + quarter]
            send_ref[rep, :, here] = narrow(term[base + quarter : base + half])


def run(kernel, operands, in_hbm, out_shape, scratch_shapes, flops, room=24, **sizes):
    held, fetched = pl.BlockSpec(memory_space=pltpu.VMEM), pl.BlockSpec(memory_space=pltpu.HBM)
    moved = sum(operand.size * operand.dtype.itemsize for operand in operands)
    return pl.pallas_call(
        functools.partial(kernel, **sizes),
        out_shape=out_shape,
        in_specs=[fetched if place in in_hbm else held for place in range(len(operands))],
        out_specs=jax.tree.map(lambda _: held, out_shape),
        scratch_shapes=scratch_shapes,
        compiler_params=pltpu.CompilerParams(vmem_limit_bytes=room * 1024 * 1024),
        cost_estimate=pl.CostEstimate(flops=flops, bytes_accessed=moved, transcendentals=0),
    )(*operands)


def pack(tokens, expert_ids, route_weights, experts):
    row_count, width = tokens.shape
    extra = -(-3 * experts // 128) * 128
    return run(
        pack_kernel,
        (tokens, expert_ids, route_weights),
        (0, 1, 2),
        jax.ShapeDtypeStruct((row_count, width + extra), jnp.bfloat16),
        [
            pltpu.VMEM(expert_ids.shape, jnp.int32),
            pltpu.VMEM(route_weights.shape, jnp.float32),
            pltpu.SemaphoreType.DMA((3,)),
        ],
        0,
        experts=experts,
    )


def fetch(gate_local, up_local, down_local):
    part_width, width = gate_local.shape
    return run(
        fetch_kernel,
        (gate_local, up_local, down_local),
        (0, 1, 2),
        (
            jax.ShapeDtypeStruct((2 * part_width, width), gate_local.dtype),
            jax.ShapeDtypeStruct(down_local.shape, down_local.dtype),
        ),
        [pltpu.SemaphoreType.DMA((3,))],
        0,
        room=ROOM,
    )


def gate_up(blocks, starts, row_count, weights, experts):
    part_width, width = weights[0].shape[0] // 2, weights[0].shape[1]
    total = len(blocks) * row_count
    return run(
        gate_up_kernel,
        (*blocks, *weights),
        (),
        (
            jax.ShapeDtypeStruct((2, total, part_width), jnp.bfloat16),
            jax.ShapeDtypeStruct((2, total, 128), jnp.float32),
        ),
        [pltpu.VMEM((total, width), jnp.bfloat16)],
        8 * total * width * part_width,
        experts=experts,
        starts=starts,
        row_count=row_count,
    )


def down(own, other, share, down_own, down_other):
    total = own.shape[1]
    depth, width = down_own.shape
    half = (2, total // 4, width)
    return run(
        down_kernel,
        (own, other, share, down_own, down_other),
        (),
        (jax.ShapeDtypeStruct(half, jnp.float32), jax.ShapeDtypeStruct(half, jnp.bfloat16)),
        [],
        4 * total * depth * width,
    )


def by_rows(tokens, expert_ids, route_weights, gate_local, up_local, down_local):
    row_count = tokens.shape[0]
    experts = lax.axis_size("node") * lax.axis_size("local")
    places = lax.axis_size("local")
    plane = lax.axis_index("rep")
    together = lax.optimization_barrier

    packed = pack(tokens, expert_ids, route_weights, experts)
    square_0, line_1, line_2, gates, downs = together(
        (
            square(packed),
            swap(packed, "local", 1),
            swap(packed, "local", 2),
            *fetch(gate_local, up_local, down_local),
        )
    )
    other_gates, other_downs = swap(gates, "node", 1), swap(downs, "node", 1)
    square_12, line_3 = together(
        (square(jnp.concatenate([line_1, line_2], axis=0)), swap(square_0[0], "local", 3))
    )

    def hidden_of(first, first_start, second, second_start):
        blocks = [block for pair in zip(first, second) for block in pair]
        starts = [first_start, second_start] * len(first)
        return gate_up(blocks, starts, row_count, (gates, other_gates), experts)

    def exchanged(hidden, share):
        return hidden, swap(hidden, "rep", 1), share

    def line_parts(pair, place, mask):
        here = narrow(pair[0, place])
        there = narrow(pair[1, place])
        return (
            swap(here, "local", mask) if mask else pair[0, place],
            swap(there, ("rep", "local"), places | mask),
        )

    def pair_of(keep, back):
        return (keep + wide(back)).reshape(2, 2, row_count, -1)

    hidden_a = hidden_of(square_0, 0, square_12, row_count)
    hidden_a, square_3, other_downs = together((hidden_a, square(line_3), other_downs))
    hidden_b = hidden_of(square_12, 0, square_3, 0)
    hidden_a, hidden_b = exchanged(*hidden_a), exchanged(*hidden_b)
    keep_a, send_a = down(*hidden_a, downs, other_downs)
    back_a = swap(send_a, "node", 2)
    pair_a = pair_of(keep_a, back_a)
    keep_b, send_b = down(*hidden_b, downs, other_downs)
    part_0, part_2, back_b = together(
        (line_parts(pair_a, 0, 0), line_parts(pair_a, 1, 2), swap(send_b, "node", 2))
    )
    pair_b = pair_of(keep_b, back_b)
    parts = [part_0, line_parts(pair_b, 0, 1), part_2, line_parts(pair_b, 1, 3)]
    half_own, half_other = (narrow(sum(wide(part[side]) for part in parts)) for side in (0, 1))
    return jnp.where(
        plane == 0,
        jnp.concatenate([half_own, half_other], axis=1),
        jnp.concatenate([half_other, half_own], axis=1),
    )


def on_device(tokens, expert_ids, route_weights, gate_weight, up_weight, down_weight):
    row_count, top_count = expert_ids.shape
    expert_count = lax.axis_size("node") * lax.axis_size("local")
    slot_cap = min(row_count, max(2, 2 * row_count * top_count // expert_count))
    weights = (gate_weight[0], up_weight[0], down_weight[0])
    if slot_cap == row_count:
        return by_rows(tokens, expert_ids, route_weights, *weights)
    return by_slots(tokens, expert_ids, route_weights, *weights, slot_cap)


def solution(mesh):
    placed = (
        P(EVERY, None),
        P(EVERY, None),
        P(EVERY, None),
        P(PLANE, "rep", None),
        P(PLANE, "rep", None),
        P(PLANE, None, "rep"),
    )
    return jax.shard_map(
        on_device,
        mesh=mesh,
        in_specs=placed,
        out_specs=P(EVERY, None),
        check_vma=False,
    )
```

```python
import functools
import math

import jax
import jax.numpy as jnp
from jax import lax
from jax.experimental import pallas as pl
from jax.experimental.pallas import tpu as pltpu
from jax.sharding import PartitionSpec as P

PLANE = ("node", "local")
EVERY = ("rep", "node", "local")


def slot_table(expert_ids, expert_count, slot_cap):
    row_count, top_count = expert_ids.shape
    flat_ids = expert_ids.reshape(-1)
    hits = (flat_ids[:, None] == jnp.arange(expert_count, dtype=jnp.int32)[None, :]).astype(
        jnp.int32
    )
    before = jnp.cumsum(hits, axis=0) - hits
    rank_of = jnp.sum(before * hits, axis=1)
    return (flat_ids * slot_cap + rank_of).reshape(row_count, top_count)


def route_slots(blocks):
    return lax.all_to_all(blocks, PLANE, split_axis=1, concat_axis=1, tiled=True)


def by_slots(tokens, expert_ids, route_weights, gate_local, up_local, down_local, slot_cap):
    model_width = tokens.shape[1]
    plane_count = lax.axis_size("rep")
    expert_count = lax.axis_size("node") * lax.axis_size("local")
    slot_total = expert_count * slot_cap
    slot_of = slot_table(expert_ids, expert_count, slot_cap)
    slot_iota = jnp.arange(slot_total, dtype=jnp.int32)
    placed = jnp.any(slot_of[None, :, :] == slot_iota[:, None, None], axis=2).astype(jnp.bfloat16)
    outgoing = jnp.dot(placed, tokens, preferred_element_type=jnp.float32).astype(jnp.bfloat16)
    mixing = jnp.sum(
        jnp.where(slot_of[:, :, None] == slot_iota[None, None, :], route_weights[:, :, None], 0.0),
        axis=1,
    )
    arrived = route_slots(outgoing.reshape(1, expert_count, slot_cap, model_width))
    arrived = arrived.reshape(slot_total, model_width)
    shard_piece = lax.all_gather(arrived, "rep", axis=0, tiled=True)
    hidden_part = hidden_units(shard_piece, gate_local, up_local)
    expert_out = jnp.dot(
        lax.all_gather(hidden_part, "rep", axis=1, tiled=True),
        down_local,
        preferred_element_type=jnp.float32,
    ).astype(jnp.bfloat16)
    own_slots = lax.all_to_all(
        expert_out.reshape(plane_count, slot_total, down_local.shape[1]),
        "rep",
        split_axis=0,
        concat_axis=2,
        tiled=True,
    )
    returned = route_slots(own_slots.reshape(1, expert_count, slot_cap, model_width))
    back_rows = returned.reshape(slot_total, model_width).astype(jnp.float32)
    mixed_rows = jnp.dot(mixing, back_rows, precision=lax.Precision.HIGHEST)
    return mixed_rows.astype(jnp.bfloat16)


def hidden_units(rows, gate_local, up_local):
    feature_dims = (((1,), (1,)), ((), ()))
    gate = lax.dot_general(rows, gate_local, feature_dims, preferred_element_type=jnp.float32)
    up = lax.dot_general(rows, up_local, feature_dims, preferred_element_type=jnp.float32)
    return (jax.nn.silu(gate) * up).astype(jnp.bfloat16)


def swap(block, axes, mask):
    size = lax.axis_size(axes)
    return lax.ppermute(block, axes, [(place, place ^ mask) for place in range(size)])


def square(block):
    nodes = lax.axis_size("node")
    across = swap(block, ("rep", "node"), nodes | 2)
    return [block, swap(block, "node", 2), swap(block, "rep", 1), across]


def wide(block):
    return block.astype(jnp.float32)


def narrow(block):
    return block.astype(jnp.bfloat16)


def pack_kernel(tokens_in, ids_in, weights_in, out_ref, ids_ref, weights_ref, sems, *, experts):
    row_count, width = tokens_in.shape
    tokens_copy = pltpu.make_async_copy(tokens_in, out_ref.at[:, pl.ds(0, width)], sems.at[0])
    ids_copy = pltpu.make_async_copy(ids_in, ids_ref, sems.at[1])
    weights_copy = pltpu.make_async_copy(weights_in, weights_ref, sems.at[2])
    tokens_copy.start()
    ids_copy.start()
    weights_copy.start()
    extra = out_ref.shape[1] - width
    expert = lax.broadcasted_iota(jnp.int32, (extra, row_count), 0) % experts
    share = jnp.zeros(expert.shape, jnp.float32)
    ids_copy.wait()
    weights_copy.wait()
    for k in range(ids_ref.shape[0]):
        share += jnp.where(ids_ref[k : k + 1, :] == expert, weights_ref[k : k + 1, :], 0.0)
    share = jnp.concatenate([share, jnp.zeros((extra, extra - row_count), jnp.float32)], axis=1)
    share = share.T[:row_count]
    piece = lax.broadcasted_iota(jnp.int32, share.shape, 1) // experts
    high = wide(narrow(share))
    middle = wide(narrow(share - high))
    low = share - high - middle
    coded = jnp.where(piece == 0, high, jnp.where(piece == 1, middle, low))
    out_ref[:, width:] = narrow(jnp.where(piece < 3, coded, 0.0))
    tokens_copy.wait()


def fetch_kernel(*refs):
    *parts, out_ref, sems = refs
    row, copies = 0, []
    for place, part in enumerate(parts):
        rows = part.shape[0]
        there = out_ref.at[pl.ds(row, rows), :]
        copies.append(pltpu.make_async_copy(part, there, sems.at[place]))
        copies[-1].start()
        row += rows
    for copy in copies:
        copy.wait()


def gate_up_kernel(*refs, experts, starts, row_count):
    block_refs, weight_refs = refs[:-5], refs[-5:-3]
    hidden_ref, share_ref, rows = refs[-3:]
    part_width, width = weight_refs[0].shape[0] // 2, weight_refs[0].shape[1]
    own = lax.axis_index("node") * lax.axis_size("local") + lax.axis_index("local")
    other = own + lax.axis_size("local") * (1 - 2 * (lax.axis_index("node") % 2))
    lanes = lax.broadcasted_iota(jnp.int32, (row_count, block_refs[0].shape[1] - width), 1)
    coded = [
        (lanes % experts == expert) & (lanes < 3 * experts) for expert in (own, other)
    ]
    for place, (block, start) in enumerate(zip(block_refs, starts)):
        here = pl.ds(place * row_count, row_count)
        there = slice(start, start + row_count)
        rows[here, :] = block[there, :width]
        pieces = wide(block[there, width:])
        for side in range(2):
            share = jnp.sum(jnp.where(coded[side], pieces, 0.0), axis=1, keepdims=True)
            share_ref[side, here, :] = jnp.broadcast_to(share, (row_count, share_ref.shape[2]))
    feature_dims = (((1,), (1,)), ((), ()))
    for side, weights in enumerate(weight_refs):
        both = lax.dot_general(
            rows[...], weights[...], feature_dims, preferred_element_type=jnp.float32
        )
        gate, up = both[:, :part_width], both[:, part_width:]
        hidden_ref[side] = narrow(gate * up / (1.0 + jnp.exp(-gate)))


def down_kernel(own_ref, other_ref, share_ref, down_own, down_other, *out_refs):
    plane = lax.axis_index("rep")
    width = down_own.shape[1]
    tile = math.gcd(width, 512)
    total = own_ref.shape[1]
    half, quarter = total // 2, total // 4
    hidden = []
    for side in range(2):
        own = own_ref[side]
        other = jnp.concatenate([other_ref[side, half:], other_ref[side, :half]], axis=0)
        first = jnp.where(plane == 0, own, other)
        second = jnp.where(plane == 0, other, own)
        hidden.append(jnp.concatenate([first, second], axis=1))
    for start in range(0, width, tile):
        here = slice(start, start + tile)
        term = 0.0
        for side, part in enumerate((down_own, down_other)):
            out = jnp.dot(hidden[side], part[:, here], preferred_element_type=jnp.float32)
            term += share_ref[side, :, :1] * wide(narrow(out))
        for place, out_ref in enumerate(out_refs):
            rows = term[place * quarter : (place + 1) * quarter]
            out_ref[:, here] = rows.astype(out_ref.dtype)


def run(kernel, operands, in_hbm, out_shape, scratch_shapes, flops, room=24, **sizes):
    held, fetched = pl.BlockSpec(memory_space=pltpu.VMEM), pl.BlockSpec(memory_space=pltpu.HBM)
    moved = sum(operand.size * operand.dtype.itemsize for operand in operands)
    return pl.pallas_call(
        functools.partial(kernel, **sizes),
        out_shape=out_shape,
        in_specs=[fetched if place in in_hbm else held for place in range(len(operands))],
        out_specs=jax.tree.map(lambda _: held, out_shape),
        scratch_shapes=scratch_shapes,
        compiler_params=pltpu.CompilerParams(vmem_limit_bytes=room * 1024 * 1024),
        cost_estimate=pl.CostEstimate(flops=flops, bytes_accessed=moved, transcendentals=0),
    )(*operands)


def pack(tokens, expert_ids, route_weights, experts):
    row_count, width = tokens.shape
    extra = -(-3 * experts // 128) * 128
    return run(
        pack_kernel,
        (tokens, expert_ids.T, route_weights.T),
        (0, 1, 2),
        jax.ShapeDtypeStruct((row_count, width + extra), jnp.bfloat16),
        [
            pltpu.VMEM(expert_ids.shape[::-1], jnp.int32),
            pltpu.VMEM(route_weights.shape[::-1], jnp.float32),
            pltpu.SemaphoreType.DMA((3,)),
        ],
        0,
        room=60,
        experts=experts,
    )


def fetch(arrays):
    rows = sum(array.shape[0] for array in arrays)
    return run(
        fetch_kernel,
        arrays,
        range(len(arrays)),
        jax.ShapeDtypeStruct((rows, arrays[0].shape[1]), arrays[0].dtype),
        [pltpu.SemaphoreType.DMA((len(arrays),))],
        0,
    )


def gate_up(blocks, starts, row_count, weights, experts):
    part_width, width = weights[0].shape[0] // 2, weights[0].shape[1]
    total = len(blocks) * row_count
    return run(
        gate_up_kernel,
        (*blocks, *weights),
        (),
        (
            jax.ShapeDtypeStruct((2, total, part_width), jnp.bfloat16),
            jax.ShapeDtypeStruct((2, total, 128), jnp.float32),
        ),
        [pltpu.VMEM((total, width), jnp.bfloat16)],
        8 * total * width * part_width,
        experts=experts,
        starts=starts,
        row_count=row_count,
    )


def down(own, other, share, down_own, down_other):
    total = own.shape[1]
    depth, width = down_own.shape
    quarter = (total // 4, width)
    return run(
        down_kernel,
        (own, other, share, down_own, down_other),
        (),
        [jax.ShapeDtypeStruct(quarter, jnp.float32)]
        + [jax.ShapeDtypeStruct(quarter, jnp.bfloat16)] * 3,
        [],
        4 * total * depth * width,
    )


def by_rows(tokens, expert_ids, route_weights, gate_local, up_local, down_local):
    row_count = tokens.shape[0]
    experts = lax.axis_size("node") * lax.axis_size("local")
    places = lax.axis_size("local")
    plane = lax.axis_index("rep")
    together = lax.optimization_barrier

    packed = pack(tokens, expert_ids, route_weights, experts)
    square_0, line_1, line_3, gates = together(
        (
            square(packed),
            swap(packed, "local", 1),
            swap(packed, "local", 3),
            fetch((gate_local, up_local)),
        )
    )
    other_gates = swap(gates, "node", 1)
    square_13, line_2, downs = together(
        (
            square(jnp.concatenate([line_1, line_3], axis=0)),
            swap(square_0[0], "local", 2),
            fetch((down_local,)),
        )
    )

    def hidden_of(*parts):
        blocks = [block for pair in zip(*(part[0] for part in parts)) for block in pair]
        starts = [part[1] for part in parts] * len(parts[0][0])
        return gate_up(blocks, starts, row_count, (gates, other_gates), experts)

    def exchanged(hidden, share):
        return hidden, swap(hidden, "rep", 1), share

    def square_back(keep, send_y, send_x, send_across):
        nodes = lax.axis_size("node")
        across = swap(send_across, ("rep", "node"), nodes | 2)
        return keep, swap(send_y, "node", 2), swap(send_x, "rep", 1), across

    def square_sum(keep, back_y, back_x, back_across):
        own, other = keep + wide(back_y), wide(back_x) + wide(back_across)
        return jnp.stack([own, other]).reshape(2, 2, row_count, -1)

    hidden_b = hidden_of((square_13, 0), (square_13, row_count))
    hidden_b, square_2, other_downs = together(
        (hidden_b, square(line_2), swap(downs, "node", 1))
    )
    hidden_a = hidden_of((square_0, 0), (square_2, 0))
    hidden_b, hidden_a = exchanged(*hidden_b), exchanged(*hidden_a)
    back_b = square_back(*down(*hidden_b, downs, other_downs))
    hidden_a, back_y = together((hidden_a, back_b[1]))
    sum_b = square_sum(back_b[0], back_y, *back_b[2:])
    sum_a = square_sum(*square_back(*down(*hidden_a, downs, other_downs)))
    sum_a = sum_a + wide(swap(narrow(sum_b), "local", 1))
    own, other = narrow(sum_a[:, 0] + wide(swap(narrow(sum_a[:, 1]), "local", 2)))
    return jnp.where(
        plane == 0,
        jnp.concatenate([own, other], axis=1),
        jnp.concatenate([other, own], axis=1),
    )


def on_device(tokens, expert_ids, route_weights, gate_weight, up_weight, down_weight):
    row_count, top_count = expert_ids.shape
    expert_count = lax.axis_size("node") * lax.axis_size("local")
    slot_cap = min(row_count, max(2, 2 * row_count * top_count // expert_count))
    weights = (gate_weight[0], up_weight[0], down_weight[0])
    if slot_cap == row_count:
        return by_rows(tokens, expert_ids, route_weights, *weights)
    return by_slots(tokens, expert_ids, route_weights, *weights, slot_cap)


def solution(mesh):
    placed = (
        P(EVERY, None),
        P(EVERY, None),
        P(EVERY, None),
        P(PLANE, "rep", None),
        P(PLANE, "rep", None),
        P(PLANE, None, "rep"),
    )
    return jax.shard_map(
        on_device,
        mesh=mesh,
        in_specs=placed,
        out_specs=P(EVERY, None),
        check_vma=False,
    )
```

```python
import functools
import math

import jax
import jax.numpy as jnp
from jax import lax
from jax.experimental import pallas as pl
from jax.experimental.pallas import tpu as pltpu
from jax.sharding import PartitionSpec as P

PLANE = ("node", "local")
EVERY = ("rep", "node", "local")


def slot_table(expert_ids, expert_count, slot_cap):
    row_count, top_count = expert_ids.shape
    flat_ids = expert_ids.reshape(-1)
    hits = (flat_ids[:, None] == jnp.arange(expert_count, dtype=jnp.int32)[None, :]).astype(
        jnp.int32
    )
    before = jnp.cumsum(hits, axis=0) - hits
    rank_of = jnp.sum(before * hits, axis=1)
    return (flat_ids * slot_cap + rank_of).reshape(row_count, top_count)


def route_slots(blocks):
    return lax.all_to_all(blocks, PLANE, split_axis=1, concat_axis=1, tiled=True)


def by_slots(tokens, expert_ids, route_weights, gate_local, up_local, down_local, slot_cap):
    model_width = tokens.shape[1]
    plane_count = lax.axis_size("rep")
    expert_count = lax.axis_size("node") * lax.axis_size("local")
    slot_total = expert_count * slot_cap
    slot_of = slot_table(expert_ids, expert_count, slot_cap)
    slot_iota = jnp.arange(slot_total, dtype=jnp.int32)
    placed = jnp.any(slot_of[None, :, :] == slot_iota[:, None, None], axis=2).astype(jnp.bfloat16)
    outgoing = jnp.dot(placed, tokens, preferred_element_type=jnp.float32).astype(jnp.bfloat16)
    mixing = jnp.sum(
        jnp.where(slot_of[:, :, None] == slot_iota[None, None, :], route_weights[:, :, None], 0.0),
        axis=1,
    )
    arrived = route_slots(outgoing.reshape(1, expert_count, slot_cap, model_width))
    arrived = arrived.reshape(slot_total, model_width)
    shard_piece = lax.all_gather(arrived, "rep", axis=0, tiled=True)
    hidden_part = hidden_units(shard_piece, gate_local, up_local)
    expert_out = jnp.dot(
        lax.all_gather(hidden_part, "rep", axis=1, tiled=True),
        down_local,
        preferred_element_type=jnp.float32,
    ).astype(jnp.bfloat16)
    own_slots = lax.all_to_all(
        expert_out.reshape(plane_count, slot_total, down_local.shape[1]),
        "rep",
        split_axis=0,
        concat_axis=2,
        tiled=True,
    )
    returned = route_slots(own_slots.reshape(1, expert_count, slot_cap, model_width))
    back_rows = returned.reshape(slot_total, model_width).astype(jnp.float32)
    mixed_rows = jnp.dot(mixing, back_rows, precision=lax.Precision.HIGHEST)
    return mixed_rows.astype(jnp.bfloat16)


def hidden_units(rows, gate_local, up_local):
    feature_dims = (((1,), (1,)), ((), ()))
    gate = lax.dot_general(rows, gate_local, feature_dims, preferred_element_type=jnp.float32)
    up = lax.dot_general(rows, up_local, feature_dims, preferred_element_type=jnp.float32)
    return (jax.nn.silu(gate) * up).astype(jnp.bfloat16)


def swap(block, axes, mask):
    size = lax.axis_size(axes)
    return lax.ppermute(block, axes, [(place, place ^ mask) for place in range(size)])


def square(block):
    nodes = lax.axis_size("node")
    across = swap(block, ("rep", "node"), nodes | 2)
    return [block, swap(block, "node", 2), swap(block, "rep", 1), across]


def wide(block):
    return block.astype(jnp.float32)


def narrow(block):
    return block.astype(jnp.bfloat16)


def pack_kernel(tokens_in, ids_in, weights_in, out_ref, ids_ref, weights_ref, sems, *, experts):
    row_count, width = tokens_in.shape
    tokens_copy = pltpu.make_async_copy(tokens_in, out_ref.at[:, pl.ds(0, width)], sems.at[0])
    ids_copy = pltpu.make_async_copy(ids_in, ids_ref, sems.at[1])
    weights_copy = pltpu.make_async_copy(weights_in, weights_ref, sems.at[2])
    tokens_copy.start()
    ids_copy.start()
    weights_copy.start()
    extra = out_ref.shape[1] - width
    expert = lax.broadcasted_iota(jnp.int32, (extra, row_count), 0) % experts
    share = jnp.zeros(expert.shape, jnp.float32)
    ids_copy.wait()
    weights_copy.wait()
    for k in range(ids_ref.shape[0]):
        share += jnp.where(ids_ref[k : k + 1, :] == expert, weights_ref[k : k + 1, :], 0.0)
    share = jnp.concatenate([share, jnp.zeros((extra, extra - row_count), jnp.float32)], axis=1)
    share = share.T[:row_count]
    piece = lax.broadcasted_iota(jnp.int32, share.shape, 1) // experts
    high = wide(narrow(share))
    middle = wide(narrow(share - high))
    low = share - high - middle
    coded = jnp.where(piece == 0, high, jnp.where(piece == 1, middle, low))
    out_ref[:, width:] = narrow(jnp.where(piece < 3, coded, 0.0))
    tokens_copy.wait()


def fetch_kernel(*refs):
    *parts, out_ref, sems = refs
    row, copies = 0, []
    for place, part in enumerate(parts):
        rows = part.shape[0]
        there = out_ref.at[pl.ds(row, rows), :]
        copies.append(pltpu.make_async_copy(part, there, sems.at[place]))
        copies[-1].start()
        row += rows
    for copy in copies:
        copy.wait()


def gate_up_kernel(*refs, experts, starts, row_count):
    block_refs, weight_refs = refs[:-5], refs[-5:-3]
    hidden_ref, share_ref, rows = refs[-3:]
    part_width, width = weight_refs[0].shape[0] // 2, weight_refs[0].shape[1]
    own = lax.axis_index("node") * lax.axis_size("local") + lax.axis_index("local")
    other = own + lax.axis_size("local") * (1 - 2 * (lax.axis_index("node") % 2))
    lanes = lax.broadcasted_iota(jnp.int32, (row_count, block_refs[0].shape[1] - width), 1)
    coded = [
        (lanes % experts == expert) & (lanes < 3 * experts) for expert in (own, other)
    ]
    for place, (block, start) in enumerate(zip(block_refs, starts)):
        here = pl.ds(place * row_count, row_count)
        there = slice(start, start + row_count)
        rows[here, :] = block[there, :width]
        pieces = wide(block[there, width:])
        for side in range(2):
            share = jnp.sum(jnp.where(coded[side], pieces, 0.0), axis=1, keepdims=True)
            share_ref[side, here, :] = jnp.broadcast_to(share, (row_count, share_ref.shape[2]))
    feature_dims = (((1,), (1,)), ((), ()))
    for side, weights in enumerate(weight_refs):
        both = lax.dot_general(
            weights[...], rows[...], feature_dims, preferred_element_type=jnp.float32
        )
        gate, up = both[:part_width], both[part_width:]
        hidden_ref[side] = narrow((gate * up / (1.0 + jnp.exp(-gate))).T)


def down_kernel(own_ref, other_ref, share_ref, down_own, down_other, *out_refs, quarters):
    plane = lax.axis_index("rep")
    width = down_own.shape[1]
    tile = math.gcd(width, 512)
    total = own_ref.shape[1]
    half, quarter = total // 2, total // 4
    hidden = []
    for side in range(2):
        own = own_ref[side]
        other = jnp.concatenate([other_ref[side, half:], other_ref[side, :half]], axis=0)
        first = jnp.where(plane == 0, own, other)
        second = jnp.where(plane == 0, other, own)
        hidden.append(jnp.concatenate([first, second], axis=1))
    for start in range(0, width, tile):
        here = slice(start, start + tile)
        term = 0.0
        for side, part in enumerate((down_own, down_other)):
            out = jnp.dot(hidden[side], part[:, here], preferred_element_type=jnp.float32)
            term += share_ref[side, :, :1] * wide(narrow(out))
        for out_ref, places in zip(out_refs, quarters):
            rows = [term[place * quarter : (place + 1) * quarter] for place in places]
            out_ref[:, here] = jnp.concatenate(rows, axis=0).astype(out_ref.dtype)


def run(kernel, operands, in_hbm, out_shape, scratch_shapes, flops, room=24, **sizes):
    held, fetched = pl.BlockSpec(memory_space=pltpu.VMEM), pl.BlockSpec(memory_space=pltpu.HBM)
    moved = sum(operand.size * operand.dtype.itemsize for operand in operands)
    return pl.pallas_call(
        functools.partial(kernel, **sizes),
        out_shape=out_shape,
        in_specs=[fetched if place in in_hbm else held for place in range(len(operands))],
        out_specs=jax.tree.map(lambda _: held, out_shape),
        scratch_shapes=scratch_shapes,
        compiler_params=pltpu.CompilerParams(vmem_limit_bytes=room * 1024 * 1024),
        cost_estimate=pl.CostEstimate(flops=flops, bytes_accessed=moved, transcendentals=0),
    )(*operands)


def pack(tokens, expert_ids, route_weights, experts):
    row_count, width = tokens.shape
    extra = -(-3 * experts // 128) * 128
    return run(
        pack_kernel,
        (tokens, expert_ids.T, route_weights.T),
        (0, 1, 2),
        jax.ShapeDtypeStruct((row_count, width + extra), jnp.bfloat16),
        [
            pltpu.VMEM(expert_ids.shape[::-1], jnp.int32),
            pltpu.VMEM(route_weights.shape[::-1], jnp.float32),
            pltpu.SemaphoreType.DMA((3,)),
        ],
        0,
        room=60,
        experts=experts,
    )


def fetch(arrays):
    rows = sum(array.shape[0] for array in arrays)
    return run(
        fetch_kernel,
        arrays,
        range(len(arrays)),
        jax.ShapeDtypeStruct((rows, arrays[0].shape[1]), arrays[0].dtype),
        [pltpu.SemaphoreType.DMA((len(arrays),))],
        0,
    )


def gate_up(blocks, starts, row_count, weights, experts):
    part_width, width = weights[0].shape[0] // 2, weights[0].shape[1]
    total = len(blocks) * row_count
    return run(
        gate_up_kernel,
        (*blocks, *weights),
        (),
        (
            jax.ShapeDtypeStruct((2, total, part_width), jnp.bfloat16),
            jax.ShapeDtypeStruct((2, total, 128), jnp.float32),
        ),
        [pltpu.VMEM((total, width), jnp.bfloat16)],
        8 * total * width * part_width,
        experts=experts,
        starts=starts,
        row_count=row_count,
    )


def down(own, other, share, weights, quarters):
    total = own.shape[1]
    depth, width = weights[0].shape
    sizes = [(len(places) * total // 4, width) for places in quarters]
    return run(
        down_kernel,
        (own, other, share, *weights),
        (),
        [jax.ShapeDtypeStruct(sizes[0], jnp.float32)]
        + [jax.ShapeDtypeStruct(size, jnp.bfloat16) for size in sizes[1:]],
        [],
        4 * total * depth * width,
        quarters=quarters,
    )


def by_rows(tokens, expert_ids, route_weights, gate_local, up_local, down_local):
    row_count = tokens.shape[0]
    experts = lax.axis_size("node") * lax.axis_size("local")
    places = lax.axis_size("local")
    plane = lax.axis_index("rep")
    together = lax.optimization_barrier

    packed = pack(tokens, expert_ids, route_weights, experts)
    square_0, line_1, line_3, gates = together(
        (
            square(packed),
            swap(packed, "local", 1),
            swap(packed, "local", 3),
            fetch((gate_local, up_local)),
        )
    )
    other_gates = swap(gates, "node", 1)
    square_13, line_2, downs = together(
        (
            square(jnp.concatenate([line_1, line_3], axis=0)),
            swap(square_0[0], "local", 2),
            fetch((down_local,)),
        )
    )

    def hidden_of(*parts):
        blocks = [block for pair in zip(*(part[0] for part in parts)) for block in pair]
        starts = [part[1] for part in parts] * len(parts[0][0])
        return gate_up(blocks, starts, row_count, (gates, other_gates), experts)

    def exchanged(hidden, share):
        return hidden, swap(hidden, "rep", 1), share

    hidden_b = hidden_of((square_13, 0), (square_13, row_count))
    hidden_b, square_2, other_downs = together(
        (hidden_b, square(line_2), swap(downs, "node", 1))
    )
    hidden_a = hidden_of((square_0, 0), (square_2, 0))
    hidden_b, hidden_a = exchanged(*hidden_b), exchanged(*hidden_a)
    weights = (downs, other_downs)
    keep, send_y = down(*hidden_b, weights, ((0, 2), (1, 3)))
    back_y = swap(send_y, "node", 2)
    hidden_a, back_y = together((hidden_a, back_y))
    here, there = narrow(keep + wide(back_y)).reshape(2, 2 * row_count, -1)
    keep, send_y, send_x, send_across = down(*hidden_a, weights, ((0,), (1,), (2,), (3,)))
    across = swap(send_across, ("rep", "node"), lax.axis_size("node") | 2)
    along_x, along_y = swap(send_x, "rep", 1), swap(send_y, "node", 2)
    there = swap(there, ("rep", "local"), places | 1)
    here = swap(here, "local", 1)
    own = keep + wide(along_y) + wide(here)
    other = wide(along_x) + wide(across) + wide(there)
    total = jnp.stack([own, other]).reshape(2, 2, row_count, -1)
    own, other = narrow(total[:, 0] + wide(swap(narrow(total[:, 1]), "local", 2)))
    return jnp.where(
        plane == 0,
        jnp.concatenate([own, other], axis=1),
        jnp.concatenate([other, own], axis=1),
    )


def on_device(tokens, expert_ids, route_weights, gate_weight, up_weight, down_weight):
    row_count, top_count = expert_ids.shape
    expert_count = lax.axis_size("node") * lax.axis_size("local")
    slot_cap = min(row_count, max(2, 2 * row_count * top_count // expert_count))
    weights = (gate_weight[0], up_weight[0], down_weight[0])
    if slot_cap == row_count:
        return by_rows(tokens, expert_ids, route_weights, *weights)
    return by_slots(tokens, expert_ids, route_weights, *weights, slot_cap)


def solution(mesh):
    placed = (
        P(EVERY, None),
        P(EVERY, None),
        P(EVERY, None),
        P(PLANE, "rep", None),
        P(PLANE, "rep", None),
        P(PLANE, None, "rep"),
    )
    return jax.shard_map(
        on_device,
        mesh=mesh,
        in_specs=placed,
        out_specs=P(EVERY, None),
        check_vma=False,
    )
```

```python
import functools
import math

import jax
import jax.numpy as jnp
from jax import lax
from jax.experimental import pallas as pl
from jax.experimental.pallas import tpu as pltpu
from jax.sharding import PartitionSpec as P

PLANE = ("node", "local")
EVERY = ("rep", "node", "local")


def slot_table(expert_ids, expert_count, slot_cap):
    row_count, top_count = expert_ids.shape
    flat_ids = expert_ids.reshape(-1)
    hits = (flat_ids[:, None] == jnp.arange(expert_count, dtype=jnp.int32)[None, :]).astype(
        jnp.int32
    )
    before = jnp.cumsum(hits, axis=0) - hits
    rank_of = jnp.sum(before * hits, axis=1)
    return (flat_ids * slot_cap + rank_of).reshape(row_count, top_count)


def route_slots(blocks):
    return lax.all_to_all(blocks, PLANE, split_axis=1, concat_axis=1, tiled=True)


def by_slots(tokens, expert_ids, route_weights, gate_local, up_local, down_local, slot_cap):
    model_width = tokens.shape[1]
    plane_count = lax.axis_size("rep")
    expert_count = lax.axis_size("node") * lax.axis_size("local")
    slot_total = expert_count * slot_cap
    slot_of = slot_table(expert_ids, expert_count, slot_cap)
    slot_iota = jnp.arange(slot_total, dtype=jnp.int32)
    placed = jnp.any(slot_of[None, :, :] == slot_iota[:, None, None], axis=2).astype(jnp.bfloat16)
    outgoing = jnp.dot(placed, tokens, preferred_element_type=jnp.float32).astype(jnp.bfloat16)
    mixing = jnp.sum(
        jnp.where(slot_of[:, :, None] == slot_iota[None, None, :], route_weights[:, :, None], 0.0),
        axis=1,
    )
    arrived = route_slots(outgoing.reshape(1, expert_count, slot_cap, model_width))
    arrived = arrived.reshape(slot_total, model_width)
    shard_piece = lax.all_gather(arrived, "rep", axis=0, tiled=True)
    hidden_part = hidden_units(shard_piece, gate_local, up_local)
    expert_out = jnp.dot(
        lax.all_gather(hidden_part, "rep", axis=1, tiled=True),
        down_local,
        preferred_element_type=jnp.float32,
    ).astype(jnp.bfloat16)
    own_slots = lax.all_to_all(
        expert_out.reshape(plane_count, slot_total, down_local.shape[1]),
        "rep",
        split_axis=0,
        concat_axis=2,
        tiled=True,
    )
    returned = route_slots(own_slots.reshape(1, expert_count, slot_cap, model_width))
    back_rows = returned.reshape(slot_total, model_width).astype(jnp.float32)
    mixed_rows = jnp.dot(mixing, back_rows, precision=lax.Precision.HIGHEST)
    return mixed_rows.astype(jnp.bfloat16)


def hidden_units(rows, gate_local, up_local):
    feature_dims = (((1,), (1,)), ((), ()))
    gate = lax.dot_general(rows, gate_local, feature_dims, preferred_element_type=jnp.float32)
    up = lax.dot_general(rows, up_local, feature_dims, preferred_element_type=jnp.float32)
    return (jax.nn.silu(gate) * up).astype(jnp.bfloat16)


def swap(block, axes, mask):
    size = lax.axis_size(axes)
    return lax.ppermute(block, axes, [(place, place ^ mask) for place in range(size)])


def square(block):
    across = swap(block, ("rep", "node"), lax.axis_size("node") | 2)
    along_x = swap(block, "rep", 1)
    return [across, along_x, swap(block, "node", 2), block]


def wide(block):
    return block.astype(jnp.float32)


def narrow(block):
    return block.astype(jnp.bfloat16)


def pack_kernel(tokens_in, ids_in, weights_in, out_ref, ids_ref, weights_ref, sems, *, experts):
    row_count, width = tokens_in.shape
    tokens_copy = pltpu.make_async_copy(tokens_in, out_ref.at[:, pl.ds(0, width)], sems.at[0])
    ids_copy = pltpu.make_async_copy(ids_in, ids_ref, sems.at[1])
    weights_copy = pltpu.make_async_copy(weights_in, weights_ref, sems.at[2])
    tokens_copy.start()
    ids_copy.start()
    weights_copy.start()
    extra = out_ref.shape[1] - width
    expert = lax.broadcasted_iota(jnp.int32, (extra, row_count), 0) % experts
    share = jnp.zeros(expert.shape, jnp.float32)
    ids_copy.wait()
    weights_copy.wait()
    for k in range(ids_ref.shape[0]):
        share += jnp.where(ids_ref[k : k + 1, :] == expert, weights_ref[k : k + 1, :], 0.0)
    share = jnp.concatenate([share, jnp.zeros((extra, extra - row_count), jnp.float32)], axis=1)
    share = share.T[:row_count]
    piece = lax.broadcasted_iota(jnp.int32, share.shape, 1) // experts
    high = wide(narrow(share))
    middle = wide(narrow(share - high))
    low = share - high - middle
    coded = jnp.where(piece == 0, high, jnp.where(piece == 1, middle, low))
    out_ref[:, width:] = narrow(jnp.where(piece < 3, coded, 0.0))
    tokens_copy.wait()


def fetch_kernel(*refs):
    *parts, out_ref, sems = refs
    row, copies = 0, []
    for place, part in enumerate(parts):
        rows = part.shape[0]
        there = out_ref.at[pl.ds(row, rows), :]
        copies.append(pltpu.make_async_copy(part, there, sems.at[place]))
        copies[-1].start()
        row += rows
    for copy in copies:
        copy.wait()


def gate_up_kernel(*refs, experts, starts, row_count, chunks):
    rows, out_refs = refs[-1], refs[-1 - 2 * chunks : -1]
    block_refs, weight_refs = refs[: len(starts)], refs[len(starts) : len(starts) + 2]
    part_width, width = weight_refs[0].shape[0] // 2, weight_refs[0].shape[1]
    own = lax.axis_index("node") * lax.axis_size("local") + lax.axis_index("local")
    other = own + lax.axis_size("local") * (1 - 2 * (lax.axis_index("node") % 2))
    lanes = lax.broadcasted_iota(jnp.int32, (row_count, block_refs[0].shape[1] - width), 1)
    coded = [
        (lanes % experts == expert) & (lanes < 3 * experts) for expert in (own, other)
    ]
    each = len(starts) // chunks
    for place, (block, start) in enumerate(zip(block_refs, starts)):
        there = slice(start, start + row_count)
        rows[place * row_count : (place + 1) * row_count, :] = block[there, :width]
        pieces = wide(block[there, width:])
        share_ref, place = out_refs[chunks + place // each], place % each
        for side in range(2):
            share = jnp.sum(jnp.where(coded[side], pieces, 0.0), axis=1, keepdims=True)
            share = jnp.broadcast_to(share, (row_count, share_ref.shape[2]))
            share_ref[side, place * row_count : (place + 1) * row_count, :] = share
    feature_dims = (((1,), (1,)), ((), ()))
    for side, weights in enumerate(weight_refs):
        both = lax.dot_general(
            weights[...], rows[...], feature_dims, preferred_element_type=jnp.float32
        )
        gate, up = both[:part_width], both[part_width:]
        hidden = narrow((gate * up / (1.0 + jnp.exp(-gate))).T)
        for chunk, hidden_ref in enumerate(out_refs[:chunks]):
            total = hidden_ref.shape[1]
            hidden_ref[side] = hidden[chunk * total : (chunk + 1) * total]


def down_kernel(own_ref, other_ref, share_ref, down_own, down_other, *out_refs, quarters):
    plane = lax.axis_index("rep")
    width = down_own.shape[1]
    tile = math.gcd(width, 512)
    total = own_ref.shape[1]
    half, quarter = total // 2, total // 4
    hidden = []
    for side in range(2):
        own = own_ref[side]
        other = jnp.concatenate([other_ref[side, half:], other_ref[side, :half]], axis=0)
        first = jnp.where(plane == 0, own, other)
        second = jnp.where(plane == 0, other, own)
        hidden.append(jnp.concatenate([first, second], axis=1))
    for start in range(0, width, tile):
        here = slice(start, start + tile)
        term = 0.0
        for side, part in enumerate((down_own, down_other)):
            out = jnp.dot(hidden[side], part[:, here], preferred_element_type=jnp.float32)
            term += share_ref[side, :, :1] * wide(narrow(out))
        for out_ref, places in zip(out_refs, quarters):
            rows = [term[place * quarter : (place + 1) * quarter] for place in places]
            out_ref[:, here] = jnp.concatenate(rows, axis=0).astype(out_ref.dtype)


def run(kernel, operands, in_hbm, out_shape, scratch_shapes, flops, room=24, **sizes):
    held, fetched = pl.BlockSpec(memory_space=pltpu.VMEM), pl.BlockSpec(memory_space=pltpu.HBM)
    moved = sum(operand.size * operand.dtype.itemsize for operand in operands)
    return pl.pallas_call(
        functools.partial(kernel, **sizes),
        out_shape=out_shape,
        in_specs=[fetched if place in in_hbm else held for place in range(len(operands))],
        out_specs=jax.tree.map(lambda _: held, out_shape),
        scratch_shapes=scratch_shapes,
        compiler_params=pltpu.CompilerParams(vmem_limit_bytes=room * 1024 * 1024),
        cost_estimate=pl.CostEstimate(flops=flops, bytes_accessed=moved, transcendentals=0),
    )(*operands)


def pack(tokens, expert_ids, route_weights, experts):
    row_count, width = tokens.shape
    extra = -(-3 * experts // 128) * 128
    return run(
        pack_kernel,
        (tokens, expert_ids.T, route_weights.T),
        (0, 1, 2),
        jax.ShapeDtypeStruct((row_count, width + extra), jnp.bfloat16),
        [
            pltpu.VMEM(expert_ids.shape[::-1], jnp.int32),
            pltpu.VMEM(route_weights.shape[::-1], jnp.float32),
            pltpu.SemaphoreType.DMA((3,)),
        ],
        0,
        room=60,
        experts=experts,
    )


def fetch(arrays):
    rows = sum(array.shape[0] for array in arrays)
    return run(
        fetch_kernel,
        arrays,
        range(len(arrays)),
        jax.ShapeDtypeStruct((rows, arrays[0].shape[1]), arrays[0].dtype),
        [pltpu.SemaphoreType.DMA((len(arrays),))],
        0,
    )


def gate_up(parts, row_count, weights, experts):
    part_width, width = weights[0].shape[0] // 2, weights[0].shape[1]
    blocks, starts = zip(*(block for part in parts for block in part))
    total, chunks = len(blocks) * row_count, len(parts)
    outs = run(
        gate_up_kernel,
        (*blocks, *weights),
        (),
        [jax.ShapeDtypeStruct((2, total // chunks, part_width), jnp.bfloat16)] * chunks
        + [jax.ShapeDtypeStruct((2, total // chunks, 128), jnp.float32)] * chunks,
        [pltpu.VMEM((total, width), jnp.bfloat16)],
        8 * total * width * part_width,
        experts=experts,
        starts=starts,
        row_count=row_count,
        chunks=chunks,
    )
    return list(zip(outs[:chunks], outs[chunks:]))


def down(own, other, share, weights, quarters):
    total = own.shape[1]
    depth, width = weights[0].shape
    sizes = [(len(places) * total // 4, width) for places in quarters]
    return run(
        down_kernel,
        (own, other, share, *weights),
        (),
        [jax.ShapeDtypeStruct(sizes[0], jnp.float32)]
        + [jax.ShapeDtypeStruct(size, jnp.bfloat16) for size in sizes[1:]],
        [],
        4 * total * depth * width,
        quarters=quarters,
    )


def by_rows(tokens, expert_ids, route_weights, gate_local, up_local, down_local):
    row_count = tokens.shape[0]
    experts = lax.axis_size("node") * lax.axis_size("local")
    places = lax.axis_size("local")
    plane = lax.axis_index("rep")
    together = lax.optimization_barrier

    packed = pack(tokens, expert_ids, route_weights, experts)
    line_3, line_2, line_1 = (swap(packed, "local", mask) for mask in (3, 2, 1))
    line_3, line_2, line_1, square_0, gates = together(
        (line_3, line_2, line_1, square(packed), fetch((gate_local, up_local)))
    )
    square_0 = square_0[::-1]
    other_gates = swap(gates, "node", 1)
    downs = fetch((down_local,))
    square_132, other_downs = together(
        (square(jnp.concatenate([line_1, line_3, line_2], axis=0)), swap(downs, "node", 1))
    )
    square_132 = square_132[::-1]
    chunk_b = [(block, place * row_count) for block in square_132 for place in (0, 1)]
    chunk_a = [
        pair
        for own, block in zip(square_0, square_132)
        for pair in ((own, 0), (block, 2 * row_count))
    ]
    hidden_b, hidden_a = (
        (hidden, swap(hidden, "rep", 1), share)
        for hidden, share in gate_up(
            (chunk_b, chunk_a), row_count, (gates, other_gates), experts
        )
    )
    weights = (downs, other_downs)
    keep, send_y = down(*hidden_b, weights, ((0, 2), (1, 3)))
    back_y = swap(send_y, "node", 2)
    here, there = narrow(keep + wide(back_y)).reshape(2, 2 * row_count, -1)
    keep, send_y, send_x, send_across = down(*hidden_a, weights, ((0,), (1,), (2,), (3,)))
    across = swap(send_across, ("rep", "node"), lax.axis_size("node") | 2)
    along_x, along_y = swap(send_x, "rep", 1), swap(send_y, "node", 2)
    there = swap(there, ("rep", "local"), places | 1)
    here = swap(here, "local", 1)
    own = keep + wide(along_y) + wide(here)
    other = wide(along_x) + wide(across) + wide(there)
    total = jnp.stack([own, other]).reshape(2, 2, row_count, -1)
    own, other = narrow(total[:, 0] + wide(swap(narrow(total[:, 1]), "local", 2)))
    return jnp.where(
        plane == 0,
        jnp.concatenate([own, other], axis=1),
        jnp.concatenate([other, own], axis=1),
    )


def on_device(tokens, expert_ids, route_weights, gate_weight, up_weight, down_weight):
    row_count, top_count = expert_ids.shape
    expert_count = lax.axis_size("node") * lax.axis_size("local")
    slot_cap = min(row_count, max(2, 2 * row_count * top_count // expert_count))
    weights = (gate_weight[0], up_weight[0], down_weight[0])
    if slot_cap == row_count:
        return by_rows(tokens, expert_ids, route_weights, *weights)
    return by_slots(tokens, expert_ids, route_weights, *weights, slot_cap)


def solution(mesh):
    placed = (
        P(EVERY, None),
        P(EVERY, None),
        P(EVERY, None),
        P(PLANE, "rep", None),
        P(PLANE, "rep", None),
        P(PLANE, None, "rep"),
    )
    return jax.shard_map(
        on_device,
        mesh=mesh,
        in_specs=placed,
        out_specs=P(EVERY, None),
        check_vma=False,
    )
```

```python
import functools
import math

import jax
import jax.numpy as jnp
from jax import lax
from jax.experimental import pallas as pl
from jax.experimental.pallas import tpu as pltpu
from jax.sharding import PartitionSpec as P

PLANE = ("node", "local")
EVERY = ("rep", "node", "local")


def slot_table(expert_ids, expert_count, slot_cap):
    row_count, top_count = expert_ids.shape
    flat_ids = expert_ids.reshape(-1)
    hits = (flat_ids[:, None] == jnp.arange(expert_count, dtype=jnp.int32)[None, :]).astype(
        jnp.int32
    )
    before = jnp.cumsum(hits, axis=0) - hits
    rank_of = jnp.sum(before * hits, axis=1)
    return (flat_ids * slot_cap + rank_of).reshape(row_count, top_count)


def route_slots(blocks):
    return lax.all_to_all(blocks, PLANE, split_axis=1, concat_axis=1, tiled=True)


def by_slots(tokens, expert_ids, route_weights, gate_local, up_local, down_local, slot_cap):
    model_width = tokens.shape[1]
    plane_count = lax.axis_size("rep")
    expert_count = lax.axis_size("node") * lax.axis_size("local")
    slot_total = expert_count * slot_cap
    slot_of = slot_table(expert_ids, expert_count, slot_cap)
    slot_iota = jnp.arange(slot_total, dtype=jnp.int32)
    placed = jnp.any(slot_of[None, :, :] == slot_iota[:, None, None], axis=2).astype(jnp.bfloat16)
    outgoing = jnp.dot(placed, tokens, preferred_element_type=jnp.float32).astype(jnp.bfloat16)
    mixing = jnp.sum(
        jnp.where(slot_of[:, :, None] == slot_iota[None, None, :], route_weights[:, :, None], 0.0),
        axis=1,
    )
    arrived = route_slots(outgoing.reshape(1, expert_count, slot_cap, model_width))
    arrived = arrived.reshape(slot_total, model_width)
    shard_piece = lax.all_gather(arrived, "rep", axis=0, tiled=True)
    hidden_part = hidden_units(shard_piece, gate_local, up_local)
    expert_out = jnp.dot(
        lax.all_gather(hidden_part, "rep", axis=1, tiled=True),
        down_local,
        preferred_element_type=jnp.float32,
    ).astype(jnp.bfloat16)
    own_slots = lax.all_to_all(
        expert_out.reshape(plane_count, slot_total, down_local.shape[1]),
        "rep",
        split_axis=0,
        concat_axis=2,
        tiled=True,
    )
    returned = route_slots(own_slots.reshape(1, expert_count, slot_cap, model_width))
    back_rows = returned.reshape(slot_total, model_width).astype(jnp.float32)
    mixed_rows = jnp.dot(mixing, back_rows, precision=lax.Precision.HIGHEST)
    return mixed_rows.astype(jnp.bfloat16)


def hidden_units(rows, gate_local, up_local):
    feature_dims = (((1,), (1,)), ((), ()))
    gate = lax.dot_general(rows, gate_local, feature_dims, preferred_element_type=jnp.float32)
    up = lax.dot_general(rows, up_local, feature_dims, preferred_element_type=jnp.float32)
    return (jax.nn.silu(gate) * up).astype(jnp.bfloat16)


def swap(block, axes, mask):
    size = lax.axis_size(axes)
    return lax.ppermute(block, axes, [(place, place ^ mask) for place in range(size)])


def turn(block, first):
    nodes, size = lax.axis_size("node"), lax.axis_size(("rep", "node"))
    mask_of = [2 if (place % 2 == 0) == first else nodes for place in range(size)]
    pairs = [(place, place ^ mask) for place, mask in enumerate(mask_of)]
    return lax.ppermute(block, ("rep", "node"), pairs)


def square(block):
    side = turn(block, True)
    other_side = turn(block, False)
    return [side, turn(side, False), other_side, block]


def wide(block):
    return block.astype(jnp.float32)


def narrow(block):
    return block.astype(jnp.bfloat16)


def pack_kernel(tokens_in, ids_in, weights_in, out_ref, ids_ref, weights_ref, sems, *, experts):
    row_count, width = tokens_in.shape
    tokens_copy = pltpu.make_async_copy(tokens_in, out_ref.at[:, pl.ds(0, width)], sems.at[0])
    ids_copy = pltpu.make_async_copy(ids_in, ids_ref, sems.at[1])
    weights_copy = pltpu.make_async_copy(weights_in, weights_ref, sems.at[2])
    tokens_copy.start()
    ids_copy.start()
    weights_copy.start()
    extra = out_ref.shape[1] - width
    expert = lax.broadcasted_iota(jnp.int32, (extra, row_count), 0) % experts
    share = jnp.zeros(expert.shape, jnp.float32)
    ids_copy.wait()
    weights_copy.wait()
    for k in range(ids_ref.shape[0]):
        share += jnp.where(ids_ref[k : k + 1, :] == expert, weights_ref[k : k + 1, :], 0.0)
    share = jnp.concatenate([share, jnp.zeros((extra, extra - row_count), jnp.float32)], axis=1)
    share = share.T[:row_count]
    piece = lax.broadcasted_iota(jnp.int32, share.shape, 1) // experts
    high = wide(narrow(share))
    middle = wide(narrow(share - high))
    low = share - high - middle
    coded = jnp.where(piece == 0, high, jnp.where(piece == 1, middle, low))
    out_ref[:, width:] = narrow(jnp.where(piece < 3, coded, 0.0))
    tokens_copy.wait()


def fetch_kernel(*refs):
    *parts, out_ref, sems = refs
    row, copies = 0, []
    for place, part in enumerate(parts):
        rows = part.shape[0]
        there = out_ref.at[pl.ds(row, rows), :]
        copies.append(pltpu.make_async_copy(part, there, sems.at[place]))
        copies[-1].start()
        row += rows
    for copy in copies:
        copy.wait()


def gate_up_kernel(*refs, experts, starts, row_count, chunks):
    rows, out_refs = refs[-1], refs[-1 - 2 * chunks : -1]
    block_refs, weight_refs = refs[: len(starts)], refs[len(starts) : len(starts) + 2]
    part_width, width = weight_refs[0].shape[0] // 2, weight_refs[0].shape[1]
    own = lax.axis_index("node") * lax.axis_size("local") + lax.axis_index("local")
    other = own + lax.axis_size("local") * (1 - 2 * (lax.axis_index("node") % 2))
    lanes = lax.broadcasted_iota(jnp.int32, (row_count, block_refs[0].shape[1] - width), 1)
    coded = [
        (lanes % experts == expert) & (lanes < 3 * experts) for expert in (own, other)
    ]
    each = len(starts) // chunks
    core = lax.axis_index("node") % 2
    for place, (block, start) in enumerate(zip(block_refs, starts)):
        there = slice(start, start + row_count)
        chunk, (side, inner) = place // each, divmod(place % each, each // 4)
        if side in (1, 2):
            side = jnp.where(core == 0, side, 3 - side)
        first = pl.multiple_of((side * (each // 4) + inner) * row_count, row_count)
        rows[pl.ds(first + chunk * each * row_count, row_count), :] = block[there, :width]
        pieces = wide(block[there, width:])
        share_ref = out_refs[chunks + chunk]
        for expert in range(2):
            share = jnp.sum(jnp.where(coded[expert], pieces, 0.0), axis=1, keepdims=True)
            share = jnp.broadcast_to(share, (row_count, share_ref.shape[2]))
            share_ref[expert, pl.ds(first, row_count), :] = share
    feature_dims = (((1,), (1,)), ((), ()))
    for side, weights in enumerate(weight_refs):
        both = lax.dot_general(
            weights[...], rows[...], feature_dims, preferred_element_type=jnp.float32
        )
        gate, up = both[:part_width], both[part_width:]
        hidden = narrow((gate * up / (1.0 + jnp.exp(-gate))).T)
        for chunk, hidden_ref in enumerate(out_refs[:chunks]):
            total = hidden_ref.shape[1]
            hidden_ref[side] = hidden[chunk * total : (chunk + 1) * total]


def down_kernel(own_ref, other_ref, share_ref, down_own, down_other, *out_refs, quarters):
    plane = lax.axis_index("rep")
    width = down_own.shape[1]
    tile = math.gcd(width, 512)
    total = own_ref.shape[1]
    half, quarter = total // 2, total // 4
    hidden = []
    for side in range(2):
        own = own_ref[side]
        other = jnp.concatenate([other_ref[side, half:], other_ref[side, :half]], axis=0)
        first = jnp.where(plane == 0, own, other)
        second = jnp.where(plane == 0, other, own)
        hidden.append(jnp.concatenate([first, second], axis=1))
    for start in range(0, width, tile):
        here = slice(start, start + tile)
        term = 0.0
        for side, part in enumerate((down_own, down_other)):
            out = jnp.dot(hidden[side], part[:, here], preferred_element_type=jnp.float32)
            term += share_ref[side, :, :1] * wide(narrow(out))
        for out_ref, places in zip(out_refs, quarters):
            rows = [term[place * quarter : (place + 1) * quarter] for place in places]
            out_ref[:, here] = jnp.concatenate(rows, axis=0).astype(out_ref.dtype)


def run(kernel, operands, in_hbm, out_shape, scratch_shapes, flops, room=24, **sizes):
    held, fetched = pl.BlockSpec(memory_space=pltpu.VMEM), pl.BlockSpec(memory_space=pltpu.HBM)
    moved = sum(operand.size * operand.dtype.itemsize for operand in operands)
    return pl.pallas_call(
        functools.partial(kernel, **sizes),
        out_shape=out_shape,
        in_specs=[fetched if place in in_hbm else held for place in range(len(operands))],
        out_specs=jax.tree.map(lambda _: held, out_shape),
        scratch_shapes=scratch_shapes,
        compiler_params=pltpu.CompilerParams(vmem_limit_bytes=room * 1024 * 1024),
        cost_estimate=pl.CostEstimate(flops=flops, bytes_accessed=moved, transcendentals=0),
    )(*operands)


def pack(tokens, expert_ids, route_weights, experts):
    row_count, width = tokens.shape
    extra = -(-3 * experts // 128) * 128
    return run(
        pack_kernel,
        (tokens, expert_ids.T, route_weights.T),
        (0, 1, 2),
        jax.ShapeDtypeStruct((row_count, width + extra), jnp.bfloat16),
        [
            pltpu.VMEM(expert_ids.shape[::-1], jnp.int32),
            pltpu.VMEM(route_weights.shape[::-1], jnp.float32),
            pltpu.SemaphoreType.DMA((3,)),
        ],
        0,
        room=60,
        experts=experts,
    )


def fetch(arrays):
    rows = sum(array.shape[0] for array in arrays)
    return run(
        fetch_kernel,
        arrays,
        range(len(arrays)),
        jax.ShapeDtypeStruct((rows, arrays[0].shape[1]), arrays[0].dtype),
        [pltpu.SemaphoreType.DMA((len(arrays),))],
        0,
    )


def gate_up(parts, row_count, weights, experts):
    part_width, width = weights[0].shape[0] // 2, weights[0].shape[1]
    blocks, starts = zip(*(block for part in parts for block in part))
    total, chunks = len(blocks) * row_count, len(parts)
    outs = run(
        gate_up_kernel,
        (*blocks, *weights),
        (),
        [jax.ShapeDtypeStruct((2, total // chunks, part_width), jnp.bfloat16)] * chunks
        + [jax.ShapeDtypeStruct((2, total // chunks, 128), jnp.float32)] * chunks,
        [pltpu.VMEM((total, width), jnp.bfloat16)],
        8 * total * width * part_width,
        experts=experts,
        starts=starts,
        row_count=row_count,
        chunks=chunks,
    )
    return list(zip(outs[:chunks], outs[chunks:]))


def down(own, other, share, weights, quarters):
    total = own.shape[1]
    depth, width = weights[0].shape
    sizes = [(len(places) * total // 4, width) for places in quarters]
    return run(
        down_kernel,
        (own, other, share, *weights),
        (),
        [jax.ShapeDtypeStruct(sizes[0], jnp.float32)]
        + [jax.ShapeDtypeStruct(size, jnp.bfloat16) for size in sizes[1:]],
        [],
        4 * total * depth * width,
        quarters=quarters,
    )


def by_rows(tokens, expert_ids, route_weights, gate_local, up_local, down_local):
    row_count = tokens.shape[0]
    experts = lax.axis_size("node") * lax.axis_size("local")
    places = lax.axis_size("local")
    plane = lax.axis_index("rep")
    together = lax.optimization_barrier

    packed = pack(tokens, expert_ids, route_weights, experts)
    square_0, line_3, line_2, line_1, gates = together(
        (
            square(packed),
            *(swap(packed, "local", mask) for mask in (3, 2, 1)),
            fetch((gate_local, up_local)),
        )
    )
    other_gates = swap(gates, "node", 1)
    downs = fetch((down_local,))
    square_132, other_downs = together(
        (square(jnp.concatenate([line_1, line_3, line_2], axis=0)), swap(downs, "node", 1))
    )
    square_0, square_132 = (
        [own, side, other_side, both] for side, both, other_side, own in (square_0, square_132)
    )
    chunk_b = [(block, place * row_count) for block in square_132 for place in (0, 1)]
    chunk_a = [
        pair
        for own, block in zip(square_0, square_132)
        for pair in ((own, 0), (block, 2 * row_count))
    ]
    hidden_b, hidden_a = (
        (hidden, swap(hidden, "rep", 1), share)
        for hidden, share in gate_up(
            (chunk_b, chunk_a), row_count, (gates, other_gates), experts
        )
    )
    weights = (downs, other_downs)

    def square_back(keep, send_y, send_x, send_across):
        along_y = swap(send_y, "node", 2)
        across = swap(send_across, ("rep", "node"), lax.axis_size("node") | 2)
        own, other = keep + wide(along_y), wide(swap(send_x, "rep", 1)) + wide(across)
        return jnp.stack([own, other]).reshape(2, 2, row_count, -1)

    quarters = ((0,), (1,), (2,), (3,))
    sum_b = square_back(*down(*hidden_b, weights, quarters))
    sum_a = square_back(*down(*hidden_a, weights, quarters))
    sum_a = sum_a + wide(swap(narrow(sum_b), "local", 1))
    own, other = narrow(sum_a[:, 0] + wide(swap(narrow(sum_a[:, 1]), "local", 2)))
    return jnp.where(
        plane == 0,
        jnp.concatenate([own, other], axis=1),
        jnp.concatenate([other, own], axis=1),
    )


def on_device(tokens, expert_ids, route_weights, gate_weight, up_weight, down_weight):
    row_count, top_count = expert_ids.shape
    expert_count = lax.axis_size("node") * lax.axis_size("local")
    slot_cap = min(row_count, max(2, 2 * row_count * top_count // expert_count))
    weights = (gate_weight[0], up_weight[0], down_weight[0])
    if slot_cap == row_count:
        return by_rows(tokens, expert_ids, route_weights, *weights)
    return by_slots(tokens, expert_ids, route_weights, *weights, slot_cap)


def solution(mesh):
    placed = (
        P(EVERY, None),
        P(EVERY, None),
        P(EVERY, None),
        P(PLANE, "rep", None),
        P(PLANE, "rep", None),
        P(PLANE, None, "rep"),
    )
    return jax.shard_map(
        on_device,
        mesh=mesh,
        in_specs=placed,
        out_specs=P(EVERY, None),
        check_vma=False,
    )
```

```python
import functools
import math

import jax
import jax.numpy as jnp
from jax import lax
from jax.experimental import pallas as pl
from jax.experimental.pallas import tpu as pltpu
from jax.sharding import PartitionSpec as P

PLANE = ("node", "local")
EVERY = ("rep", "node", "local")


def slot_table(expert_ids, expert_count, slot_cap):
    row_count, top_count = expert_ids.shape
    flat_ids = expert_ids.reshape(-1)
    hits = (flat_ids[:, None] == jnp.arange(expert_count, dtype=jnp.int32)[None, :]).astype(
        jnp.int32
    )
    before = jnp.cumsum(hits, axis=0) - hits
    rank_of = jnp.sum(before * hits, axis=1)
    return (flat_ids * slot_cap + rank_of).reshape(row_count, top_count)


def route_slots(blocks):
    return lax.all_to_all(blocks, PLANE, split_axis=1, concat_axis=1, tiled=True)


def by_slots(tokens, expert_ids, route_weights, gate_local, up_local, down_local, slot_cap):
    model_width = tokens.shape[1]
    plane_count = lax.axis_size("rep")
    expert_count = lax.axis_size("node") * lax.axis_size("local")
    slot_total = expert_count * slot_cap
    slot_of = slot_table(expert_ids, expert_count, slot_cap)
    slot_iota = jnp.arange(slot_total, dtype=jnp.int32)
    placed = jnp.any(slot_of[None, :, :] == slot_iota[:, None, None], axis=2).astype(jnp.bfloat16)
    outgoing = jnp.dot(placed, tokens, preferred_element_type=jnp.float32).astype(jnp.bfloat16)
    mixing = jnp.sum(
        jnp.where(slot_of[:, :, None] == slot_iota[None, None, :], route_weights[:, :, None], 0.0),
        axis=1,
    )
    arrived = route_slots(outgoing.reshape(1, expert_count, slot_cap, model_width))
    arrived = arrived.reshape(slot_total, model_width)
    shard_piece = lax.all_gather(arrived, "rep", axis=0, tiled=True)
    hidden_part = hidden_units(shard_piece, gate_local, up_local)
    expert_out = jnp.dot(
        lax.all_gather(hidden_part, "rep", axis=1, tiled=True),
        down_local,
        preferred_element_type=jnp.float32,
    ).astype(jnp.bfloat16)
    own_slots = lax.all_to_all(
        expert_out.reshape(plane_count, slot_total, down_local.shape[1]),
        "rep",
        split_axis=0,
        concat_axis=2,
        tiled=True,
    )
    returned = route_slots(own_slots.reshape(1, expert_count, slot_cap, model_width))
    back_rows = returned.reshape(slot_total, model_width).astype(jnp.float32)
    mixed_rows = jnp.dot(mixing, back_rows, precision=lax.Precision.HIGHEST)
    return mixed_rows.astype(jnp.bfloat16)


def hidden_units(rows, gate_local, up_local):
    feature_dims = (((1,), (1,)), ((), ()))
    gate = lax.dot_general(rows, gate_local, feature_dims, preferred_element_type=jnp.float32)
    up = lax.dot_general(rows, up_local, feature_dims, preferred_element_type=jnp.float32)
    return (jax.nn.silu(gate) * up).astype(jnp.bfloat16)


def swap(block, axes, mask):
    size = lax.axis_size(axes)
    return lax.ppermute(block, axes, [(place, place ^ mask) for place in range(size)])


def turn(block, first):
    nodes, size = lax.axis_size("node"), lax.axis_size(("rep", "node"))
    mask_of = [2 if (place % 2 == 0) == first else nodes for place in range(size)]
    pairs = [(place, place ^ mask) for place, mask in enumerate(mask_of)]
    return lax.ppermute(block, ("rep", "node"), pairs)


def square(block):
    side = turn(block, True)
    other_side = turn(block, False)
    return [side, turn(side, False), other_side, block]


def wide(block):
    return block.astype(jnp.float32)


def narrow(block):
    return block.astype(jnp.bfloat16)


def pack_kernel(tokens_in, ids_in, weights_in, out_ref, ids_ref, weights_ref, sems, *, experts):
    row_count, width = tokens_in.shape
    tokens_copy = pltpu.make_async_copy(tokens_in, out_ref.at[:, pl.ds(0, width)], sems.at[0])
    ids_copy = pltpu.make_async_copy(ids_in, ids_ref, sems.at[1])
    weights_copy = pltpu.make_async_copy(weights_in, weights_ref, sems.at[2])
    tokens_copy.start()
    ids_copy.start()
    weights_copy.start()
    extra = out_ref.shape[1] - width
    expert = lax.broadcasted_iota(jnp.int32, (extra, row_count), 0) % experts
    share = jnp.zeros(expert.shape, jnp.float32)
    ids_copy.wait()
    weights_copy.wait()
    for k in range(ids_ref.shape[0]):
        share += jnp.where(ids_ref[k : k + 1, :] == expert, weights_ref[k : k + 1, :], 0.0)
    share = jnp.concatenate([share, jnp.zeros((extra, extra - row_count), jnp.float32)], axis=1)
    share = share.T[:row_count]
    piece = lax.broadcasted_iota(jnp.int32, share.shape, 1) // experts
    high = wide(narrow(share))
    middle = wide(narrow(share - high))
    low = share - high - middle
    coded = jnp.where(piece == 0, high, jnp.where(piece == 1, middle, low))
    out_ref[:, width:] = narrow(jnp.where(piece < 3, coded, 0.0))
    tokens_copy.wait()


def fetch_kernel(*refs):
    *parts, out_ref, sems = refs
    row, copies = 0, []
    for place, part in enumerate(parts):
        rows = part.shape[0]
        there = out_ref.at[pl.ds(row, rows), :]
        copies.append(pltpu.make_async_copy(part, there, sems.at[place]))
        copies[-1].start()
        row += rows
    for copy in copies:
        copy.wait()


def gate_up_kernel(*refs, experts, starts, row_count, chunks):
    rows, out_refs = refs[-1], refs[-1 - 2 * chunks : -1]
    block_refs, weight_refs = refs[: len(starts)], refs[len(starts) : len(starts) + 2]
    part_width, width = weight_refs[0].shape[0] // 2, weight_refs[0].shape[1]
    own = lax.axis_index("node") * lax.axis_size("local") + lax.axis_index("local")
    other = own + lax.axis_size("local") * (1 - 2 * (lax.axis_index("node") % 2))
    lanes = lax.broadcasted_iota(jnp.int32, (row_count, block_refs[0].shape[1] - width), 1)
    coded = [
        (lanes % experts == expert) & (lanes < 3 * experts) for expert in (own, other)
    ]
    each = len(starts) // chunks
    core = lax.axis_index("node") % 2
    for place, (block, start) in enumerate(zip(block_refs, starts)):
        there = slice(start, start + row_count)
        chunk, (side, inner) = place // each, divmod(place % each, each // 4)
        if side in (1, 2):
            side = jnp.where(core == 0, side, 3 - side)
        first = pl.multiple_of((side * (each // 4) + inner) * row_count, row_count)
        rows[pl.ds(first + chunk * each * row_count, row_count), :] = block[there, :width]
        pieces = wide(block[there, width:])
        share_ref = out_refs[chunks + chunk]
        for expert in range(2):
            share = jnp.sum(jnp.where(coded[expert], pieces, 0.0), axis=1, keepdims=True)
            share = jnp.broadcast_to(share, (row_count, share_ref.shape[2]))
            share_ref[expert, pl.ds(first, row_count), :] = share
    feature_dims = (((1,), (1,)), ((), ()))
    for side, weights in enumerate(weight_refs):
        both = lax.dot_general(
            weights[...], rows[...], feature_dims, preferred_element_type=jnp.float32
        )
        gate, up = both[:part_width], both[part_width:]
        hidden = narrow((gate * up / (1.0 + jnp.exp(-gate))).T)
        for chunk, hidden_ref in enumerate(out_refs[:chunks]):
            total = hidden_ref.shape[1]
            hidden_ref[side] = hidden[chunk * total : (chunk + 1) * total]


def down_kernel(own_ref, other_ref, share_ref, down_own, down_other, *out_refs, quarters):
    plane = lax.axis_index("rep")
    width = down_own.shape[1]
    tile = math.gcd(width, 512)
    total = own_ref.shape[1]
    half, quarter = total // 2, total // 4
    hidden = []
    for side in range(2):
        own = own_ref[side]
        other = jnp.concatenate([other_ref[side, half:], other_ref[side, :half]], axis=0)
        first = jnp.where(plane == 0, own, other)
        second = jnp.where(plane == 0, other, own)
        hidden.append(jnp.concatenate([first, second], axis=1))
    for start in range(0, width, tile):
        here = slice(start, start + tile)
        term = 0.0
        for side, part in enumerate((down_own, down_other)):
            out = jnp.dot(hidden[side], part[:, here], preferred_element_type=jnp.float32)
            term += share_ref[side, :, :1] * wide(narrow(out))
        for out_ref, places in zip(out_refs, quarters):
            rows = [term[place * quarter : (place + 1) * quarter] for place in places]
            out_ref[:, here] = jnp.concatenate(rows, axis=0).astype(out_ref.dtype)


def run(kernel, operands, in_hbm, out_shape, scratch_shapes, flops, room=24, **sizes):
    held, fetched = pl.BlockSpec(memory_space=pltpu.VMEM), pl.BlockSpec(memory_space=pltpu.HBM)
    moved = sum(operand.size * operand.dtype.itemsize for operand in operands)
    return pl.pallas_call(
        functools.partial(kernel, **sizes),
        out_shape=out_shape,
        in_specs=[fetched if place in in_hbm else held for place in range(len(operands))],
        out_specs=jax.tree.map(lambda _: held, out_shape),
        scratch_shapes=scratch_shapes,
        compiler_params=pltpu.CompilerParams(vmem_limit_bytes=room * 1024 * 1024),
        cost_estimate=pl.CostEstimate(flops=flops, bytes_accessed=moved, transcendentals=0),
    )(*operands)


def pack(tokens, expert_ids, route_weights, experts):
    row_count, width = tokens.shape
    extra = -(-3 * experts // 128) * 128
    return run(
        pack_kernel,
        (tokens, expert_ids.T, route_weights.T),
        (0, 1, 2),
        jax.ShapeDtypeStruct((row_count, width + extra), jnp.bfloat16),
        [
            pltpu.VMEM(expert_ids.shape[::-1], jnp.int32),
            pltpu.VMEM(route_weights.shape[::-1], jnp.float32),
            pltpu.SemaphoreType.DMA((3,)),
        ],
        0,
        room=60,
        experts=experts,
    )


def fetch(arrays):
    rows = sum(array.shape[0] for array in arrays)
    return run(
        fetch_kernel,
        arrays,
        range(len(arrays)),
        jax.ShapeDtypeStruct((rows, arrays[0].shape[1]), arrays[0].dtype),
        [pltpu.SemaphoreType.DMA((len(arrays),))],
        0,
    )


def gate_up(parts, row_count, weights, experts):
    part_width, width = weights[0].shape[0] // 2, weights[0].shape[1]
    blocks, starts = zip(*(block for part in parts for block in part))
    total, chunks = len(blocks) * row_count, len(parts)
    outs = run(
        gate_up_kernel,
        (*blocks, *weights),
        (),
        [jax.ShapeDtypeStruct((2, total // chunks, part_width), jnp.bfloat16)] * chunks
        + [jax.ShapeDtypeStruct((2, total // chunks, 128), jnp.float32)] * chunks,
        [pltpu.VMEM((total, width), jnp.bfloat16)],
        8 * total * width * part_width,
        experts=experts,
        starts=starts,
        row_count=row_count,
        chunks=chunks,
    )
    return list(zip(outs[:chunks], outs[chunks:]))


def down(own, other, share, weights, quarters):
    total = own.shape[1]
    depth, width = weights[0].shape
    sizes = [(len(places) * total // 4, width) for places in quarters]
    return run(
        down_kernel,
        (own, other, share, *weights),
        (),
        [jax.ShapeDtypeStruct(sizes[0], jnp.float32)]
        + [jax.ShapeDtypeStruct(size, jnp.bfloat16) for size in sizes[1:]],
        [],
        4 * total * depth * width,
        quarters=quarters,
    )


def by_rows(tokens, expert_ids, route_weights, gate_local, up_local, down_local):
    row_count = tokens.shape[0]
    experts = lax.axis_size("node") * lax.axis_size("local")
    places = lax.axis_size("local")
    plane = lax.axis_index("rep")
    together = lax.optimization_barrier

    packed = pack(tokens, expert_ids, route_weights, experts)
    square_0, line_3, line_1, gates = together(
        (
            square(packed),
            swap(packed, "local", 3),
            swap(packed, "local", 1),
            fetch((gate_local, up_local)),
        )
    )
    other_gates = swap(gates, "node", 1)
    block_13 = jnp.concatenate([line_1, line_3], axis=0)
    side_13, other_13, line_2 = turn(block_13, True), turn(block_13, False), swap(line_3, "local", 1)
    line_2, side_13, other_13, downs = together((line_2, side_13, other_13, fetch((down_local,))))
    square_13 = [side_13, turn(side_13, False), other_13, block_13]

    def hidden_of(*parts):
        order = (3, 0, 2, 1)
        blocks = [(square[side], row) for side in order for square, row in parts]
        return gate_up((blocks,), row_count, (gates, other_gates), experts)[0]

    def exchanged(hidden, share):
        return hidden, swap(hidden, "rep", 1), share

    def square_back(keep, send_y, send_x, send_across):
        across = swap(send_across, ("rep", "node"), lax.axis_size("node") | 2)
        along_x = swap(send_x, "rep", 1)
        return keep, swap(send_y, "node", 2), along_x, across

    def square_sum(keep, back_y, back_x, back_across):
        own, other = keep + wide(back_y), wide(back_x) + wide(back_across)
        return jnp.stack([own, other]).reshape(2, 2, row_count, -1)

    hidden_b = hidden_of((square_13, 0), (square_13, row_count))
    hidden_b, square_2, other_downs = together(
        (hidden_b, square(line_2), swap(downs, "node", 1))
    )
    weights = (downs, other_downs)
    hidden_a = hidden_of((square_0, 0), (square_2, 0))
    hidden_b, hidden_a = exchanged(*hidden_b), exchanged(*hidden_a)
    quarters = ((0,), (1,), (2,), (3,))
    back_b = square_back(*down(*hidden_b, weights, quarters))
    hidden_a, back_y = together((hidden_a, back_b[1]))
    sum_b = square_sum(back_b[0], back_y, *back_b[2:])
    sum_a = square_sum(*square_back(*down(*hidden_a, weights, quarters)))
    sum_a = sum_a + wide(swap(narrow(sum_b), "local", 1))
    own, other = narrow(sum_a[:, 0] + wide(swap(narrow(sum_a[:, 1]), "local", 2)))
    return jnp.where(
        plane == 0,
        jnp.concatenate([own, other], axis=1),
        jnp.concatenate([other, own], axis=1),
    )


def on_device(tokens, expert_ids, route_weights, gate_weight, up_weight, down_weight):
    row_count, top_count = expert_ids.shape
    expert_count = lax.axis_size("node") * lax.axis_size("local")
    slot_cap = min(row_count, max(2, 2 * row_count * top_count // expert_count))
    weights = (gate_weight[0], up_weight[0], down_weight[0])
    if slot_cap == row_count:
        return by_rows(tokens, expert_ids, route_weights, *weights)
    return by_slots(tokens, expert_ids, route_weights, *weights, slot_cap)


def solution(mesh):
    placed = (
        P(EVERY, None),
        P(EVERY, None),
        P(EVERY, None),
        P(PLANE, "rep", None),
        P(PLANE, "rep", None),
        P(PLANE, None, "rep"),
    )
    return jax.shard_map(
        on_device,
        mesh=mesh,
        in_specs=placed,
        out_specs=P(EVERY, None),
        check_vma=False,
    )
```

```python
import functools
import math

import jax
import jax.numpy as jnp
from jax import lax
from jax.experimental import pallas as pl
from jax.experimental.pallas import tpu as pltpu
from jax.sharding import PartitionSpec as P

PLANE = ("node", "local")
EVERY = ("rep", "node", "local")


def slot_table(expert_ids, expert_count, slot_cap):
    row_count, top_count = expert_ids.shape
    flat_ids = expert_ids.reshape(-1)
    hits = (flat_ids[:, None] == jnp.arange(expert_count, dtype=jnp.int32)[None, :]).astype(
        jnp.int32
    )
    before = jnp.cumsum(hits, axis=0) - hits
    rank_of = jnp.sum(before * hits, axis=1)
    return (flat_ids * slot_cap + rank_of).reshape(row_count, top_count)


def route_slots(blocks):
    return lax.all_to_all(blocks, PLANE, split_axis=1, concat_axis=1, tiled=True)


def by_slots(tokens, expert_ids, route_weights, gate_local, up_local, down_local, slot_cap):
    model_width = tokens.shape[1]
    plane_count = lax.axis_size("rep")
    expert_count = lax.axis_size("node") * lax.axis_size("local")
    slot_total = expert_count * slot_cap
    slot_of = slot_table(expert_ids, expert_count, slot_cap)
    slot_iota = jnp.arange(slot_total, dtype=jnp.int32)
    placed = jnp.any(slot_of[None, :, :] == slot_iota[:, None, None], axis=2).astype(jnp.bfloat16)
    outgoing = jnp.dot(placed, tokens, preferred_element_type=jnp.float32).astype(jnp.bfloat16)
    mixing = jnp.sum(
        jnp.where(slot_of[:, :, None] == slot_iota[None, None, :], route_weights[:, :, None], 0.0),
        axis=1,
    )
    arrived = route_slots(outgoing.reshape(1, expert_count, slot_cap, model_width))
    arrived = arrived.reshape(slot_total, model_width)
    shard_piece = lax.all_gather(arrived, "rep", axis=0, tiled=True)
    hidden_part = hidden_units(shard_piece, gate_local, up_local)
    expert_out = jnp.dot(
        lax.all_gather(hidden_part, "rep", axis=1, tiled=True),
        down_local,
        preferred_element_type=jnp.float32,
    ).astype(jnp.bfloat16)
    own_slots = lax.all_to_all(
        expert_out.reshape(plane_count, slot_total, down_local.shape[1]),
        "rep",
        split_axis=0,
        concat_axis=2,
        tiled=True,
    )
    returned = route_slots(own_slots.reshape(1, expert_count, slot_cap, model_width))
    back_rows = returned.reshape(slot_total, model_width).astype(jnp.float32)
    mixed_rows = jnp.dot(mixing, back_rows, precision=lax.Precision.HIGHEST)
    return mixed_rows.astype(jnp.bfloat16)


def hidden_units(rows, gate_local, up_local):
    feature_dims = (((1,), (1,)), ((), ()))
    gate = lax.dot_general(rows, gate_local, feature_dims, preferred_element_type=jnp.float32)
    up = lax.dot_general(rows, up_local, feature_dims, preferred_element_type=jnp.float32)
    return (jax.nn.silu(gate) * up).astype(jnp.bfloat16)


def swap(block, axes, mask):
    size = lax.axis_size(axes)
    return lax.ppermute(block, axes, [(place, place ^ mask) for place in range(size)])


def turn(block, first):
    nodes, size = lax.axis_size("node"), lax.axis_size(("rep", "node"))
    mask_of = [2 if (place % 2 == 0) == first else nodes for place in range(size)]
    pairs = [(place, place ^ mask) for place, mask in enumerate(mask_of)]
    return lax.ppermute(block, ("rep", "node"), pairs)


def square(block):
    side = turn(block, True)
    other_side = turn(block, False)
    return [side, turn(side, False), other_side, block]


def wide(block):
    return block.astype(jnp.float32)


def narrow(block):
    return block.astype(jnp.bfloat16)


def pack_kernel(tokens_in, ids_in, weights_in, out_ref, ids_ref, weights_ref, sems, *, experts):
    row_count, width = tokens_in.shape
    tokens_copy = pltpu.make_async_copy(tokens_in, out_ref.at[:, pl.ds(0, width)], sems.at[0])
    ids_copy = pltpu.make_async_copy(ids_in, ids_ref, sems.at[1])
    weights_copy = pltpu.make_async_copy(weights_in, weights_ref, sems.at[2])
    tokens_copy.start()
    ids_copy.start()
    weights_copy.start()
    extra = out_ref.shape[1] - width
    expert = lax.broadcasted_iota(jnp.int32, (extra, row_count), 0) % experts
    share = jnp.zeros(expert.shape, jnp.float32)
    ids_copy.wait()
    weights_copy.wait()
    for k in range(ids_ref.shape[0]):
        share += jnp.where(ids_ref[k : k + 1, :] == expert, weights_ref[k : k + 1, :], 0.0)
    share = jnp.concatenate([share, jnp.zeros((extra, extra - row_count), jnp.float32)], axis=1)
    share = share.T[:row_count]
    piece = lax.broadcasted_iota(jnp.int32, share.shape, 1) // experts
    high = wide(narrow(share))
    middle = wide(narrow(share - high))
    low = share - high - middle
    coded = jnp.where(piece == 0, high, jnp.where(piece == 1, middle, low))
    out_ref[:, width:] = narrow(jnp.where(piece < 3, coded, 0.0))
    tokens_copy.wait()


def fetch_kernel(*refs):
    count = len(refs) // 2
    copies = [
        pltpu.make_async_copy(refs[place], refs[count + place], refs[-1].at[place])
        for place in range(count)
    ]
    for copy in copies:
        copy.start()
    for copy in copies:
        copy.wait()


def gate_up_kernel(*refs, experts, starts, row_count, chunks):
    rows, out_refs = refs[-1], refs[-1 - 2 * chunks : -1]
    block_refs, weight_refs = refs[: len(starts)], refs[len(starts) : len(starts) + 4]
    width = weight_refs[0].shape[1]
    own = lax.axis_index("node") * lax.axis_size("local") + lax.axis_index("local")
    other = own + lax.axis_size("local") * (1 - 2 * (lax.axis_index("node") % 2))
    lanes = lax.broadcasted_iota(jnp.int32, (row_count, block_refs[0].shape[1] - width), 1)
    coded = [
        (lanes % experts == expert) & (lanes < 3 * experts) for expert in (own, other)
    ]
    each = len(starts) // chunks
    core = lax.axis_index("node") % 2
    for place, (block, start) in enumerate(zip(block_refs, starts)):
        there = slice(start, start + row_count)
        chunk, (side, inner) = place // each, divmod(place % each, each // 4)
        if side in (1, 2):
            side = jnp.where(core == 0, side, 3 - side)
        first = pl.multiple_of((side * (each // 4) + inner) * row_count, row_count)
        rows[pl.ds(first + chunk * each * row_count, row_count), :] = block[there, :width]
        pieces = wide(block[there, width:])
        share_ref = out_refs[chunks + chunk]
        for expert in range(2):
            share = jnp.sum(jnp.where(coded[expert], pieces, 0.0), axis=1, keepdims=True)
            share = jnp.broadcast_to(share, (row_count, share_ref.shape[2]))
            share_ref[expert, pl.ds(first, row_count), :] = share
    feature_dims = (((1,), (1,)), ((), ()))
    for side in range(2):
        gate, up = (
            lax.dot_general(
                weights[...], rows[...], feature_dims, preferred_element_type=jnp.float32
            )
            for weights in weight_refs[2 * side : 2 * side + 2]
        )
        hidden = narrow((gate * up / (1.0 + jnp.exp(-gate))).T)
        for chunk, hidden_ref in enumerate(out_refs[:chunks]):
            total = hidden_ref.shape[1]
            hidden_ref[side] = hidden[chunk * total : (chunk + 1) * total]


def down_kernel(own_ref, other_ref, share_ref, down_own, down_other, *out_refs, quarters):
    plane = lax.axis_index("rep")
    width = down_own.shape[1]
    tile = math.gcd(width, 512)
    total = own_ref.shape[1]
    half, quarter = total // 2, total // 4
    hidden = []
    for side in range(2):
        own = own_ref[side]
        other = jnp.concatenate([other_ref[side, half:], other_ref[side, :half]], axis=0)
        first = jnp.where(plane == 0, own, other)
        second = jnp.where(plane == 0, other, own)
        hidden.append(jnp.concatenate([first, second], axis=1))
    for start in range(0, width, tile):
        here = slice(start, start + tile)
        term = 0.0
        for side, part in enumerate((down_own, down_other)):
            out = jnp.dot(hidden[side], part[:, here], preferred_element_type=jnp.float32)
            term += share_ref[side, :, :1] * wide(narrow(out))
        for out_ref, places in zip(out_refs, quarters):
            rows = [term[place * quarter : (place + 1) * quarter] for place in places]
            out_ref[:, here] = jnp.concatenate(rows, axis=0).astype(out_ref.dtype)


def run(kernel, operands, in_hbm, out_shape, scratch_shapes, flops, room=24, **sizes):
    held, fetched = pl.BlockSpec(memory_space=pltpu.VMEM), pl.BlockSpec(memory_space=pltpu.HBM)
    moved = sum(operand.size * operand.dtype.itemsize for operand in operands)
    return pl.pallas_call(
        functools.partial(kernel, **sizes),
        out_shape=out_shape,
        in_specs=[fetched if place in in_hbm else held for place in range(len(operands))],
        out_specs=jax.tree.map(lambda _: held, out_shape),
        scratch_shapes=scratch_shapes,
        compiler_params=pltpu.CompilerParams(vmem_limit_bytes=room * 1024 * 1024),
        cost_estimate=pl.CostEstimate(flops=flops, bytes_accessed=moved, transcendentals=0),
    )(*operands)


def pack(tokens, expert_ids, route_weights, experts):
    row_count, width = tokens.shape
    extra = -(-3 * experts // 128) * 128
    return run(
        pack_kernel,
        (tokens, expert_ids.T, route_weights.T),
        (0, 1, 2),
        jax.ShapeDtypeStruct((row_count, width + extra), jnp.bfloat16),
        [
            pltpu.VMEM(expert_ids.shape[::-1], jnp.int32),
            pltpu.VMEM(route_weights.shape[::-1], jnp.float32),
            pltpu.SemaphoreType.DMA((3,)),
        ],
        0,
        room=60,
        experts=experts,
    )


def fetch(arrays):
    return run(
        fetch_kernel,
        arrays,
        range(len(arrays)),
        [jax.ShapeDtypeStruct(array.shape, array.dtype) for array in arrays],
        [pltpu.SemaphoreType.DMA((len(arrays),))],
        0,
    )


def gate_up(parts, row_count, weights, experts):
    part_width, width = weights[0].shape
    blocks, starts = zip(*(block for part in parts for block in part))
    total, chunks = len(blocks) * row_count, len(parts)
    outs = run(
        gate_up_kernel,
        (*blocks, *weights),
        (),
        [jax.ShapeDtypeStruct((2, total // chunks, part_width), jnp.bfloat16)] * chunks
        + [jax.ShapeDtypeStruct((2, total // chunks, 128), jnp.float32)] * chunks,
        [pltpu.VMEM((total, width), jnp.bfloat16)],
        8 * total * width * part_width,
        experts=experts,
        starts=starts,
        row_count=row_count,
        chunks=chunks,
    )
    return list(zip(outs[:chunks], outs[chunks:]))


def down(own, other, share, weights, quarters):
    total = own.shape[1]
    depth, width = weights[0].shape
    sizes = [(len(places) * total // 4, width) for places in quarters]
    return run(
        down_kernel,
        (own, other, share, *weights),
        (),
        [jax.ShapeDtypeStruct(sizes[0], jnp.float32)]
        + [jax.ShapeDtypeStruct(size, jnp.bfloat16) for size in sizes[1:]],
        [],
        4 * total * depth * width,
        quarters=quarters,
    )


def by_rows(tokens, expert_ids, route_weights, gate_local, up_local, down_local):
    row_count = tokens.shape[0]
    experts = lax.axis_size("node") * lax.axis_size("local")
    places = lax.axis_size("local")
    plane = lax.axis_index("rep")
    together = lax.optimization_barrier

    packed = pack(tokens, expert_ids, route_weights, experts)
    line_3, line_1, square_0, other_downs, gate_local, up_local = together(
        (
            swap(packed, "local", 3),
            swap(packed, "local", 1),
            square(packed),
            swap(down_local, "node", 1),
            gate_local,
            up_local,
        )
    )
    other_gates = [swap(weight, "node", 1) for weight in (gate_local, up_local)]
    block_13 = jnp.concatenate([line_1, line_3], axis=0)
    side_13, other_13, line_2 = turn(block_13, True), turn(block_13, False), swap(line_3, "local", 1)
    line_2, side_13, other_13, (gate_own, up_own, downs) = together(
        (line_2, side_13, other_13, fetch((gate_local, up_local, down_local)))
    )
    square_13 = [side_13, turn(side_13, False), other_13, block_13]
    gates = (gate_own, up_own, *other_gates)

    def hidden_of(*parts):
        order = (3, 0, 2, 1)
        blocks = [(square[side], row) for side in order for square, row in parts]
        return gate_up((blocks,), row_count, gates, experts)[0]

    def exchanged(hidden, share):
        return hidden, swap(hidden, "rep", 1), share

    def square_back(keep, send_y, send_x, send_across):
        across = swap(send_across, ("rep", "node"), lax.axis_size("node") | 2)
        along_x = swap(send_x, "rep", 1)
        return keep, swap(send_y, "node", 2), along_x, across

    def square_sum(keep, back_y, back_x, back_across):
        own, other = keep + wide(back_y), wide(back_x) + wide(back_across)
        return jnp.stack([own, other]).reshape(2, 2, row_count, -1)

    hidden_b = hidden_of((square_13, 0), (square_13, row_count))
    hidden_b, square_2 = together((hidden_b, square(line_2)))
    weights = (downs, other_downs)
    hidden_a = hidden_of((square_0, 0), (square_2, 0))
    hidden_b, hidden_a = exchanged(*hidden_b), exchanged(*hidden_a)
    quarters = ((0,), (1,), (2,), (3,))
    back_b = square_back(*down(*hidden_b, weights, quarters))
    hidden_a, back_y = together((hidden_a, back_b[1]))
    sum_b = square_sum(back_b[0], back_y, *back_b[2:])
    sum_a = square_sum(*square_back(*down(*hidden_a, weights, quarters)))
    sum_a = sum_a + wide(swap(narrow(sum_b), "local", 1))
    own, other = narrow(sum_a[:, 0] + wide(swap(narrow(sum_a[:, 1]), "local", 2)))
    return jnp.where(
        plane == 0,
        jnp.concatenate([own, other], axis=1),
        jnp.concatenate([other, own], axis=1),
    )


def on_device(tokens, expert_ids, route_weights, gate_weight, up_weight, down_weight):
    row_count, top_count = expert_ids.shape
    expert_count = lax.axis_size("node") * lax.axis_size("local")
    slot_cap = min(row_count, max(2, 2 * row_count * top_count // expert_count))
    weights = (gate_weight[0], up_weight[0], down_weight[0])
    if slot_cap == row_count:
        return by_rows(tokens, expert_ids, route_weights, *weights)
    return by_slots(tokens, expert_ids, route_weights, *weights, slot_cap)


def solution(mesh):
    placed = (
        P(EVERY, None),
        P(EVERY, None),
        P(EVERY, None),
        P(PLANE, "rep", None),
        P(PLANE, "rep", None),
        P(PLANE, None, "rep"),
    )
    return jax.shard_map(
        on_device,
        mesh=mesh,
        in_specs=placed,
        out_specs=P(EVERY, None),
        check_vma=False,
    )
```

```python
import functools
import math

import jax
import jax.numpy as jnp
from jax import lax
from jax.experimental import pallas as pl
from jax.experimental.pallas import tpu as pltpu
from jax.sharding import PartitionSpec as P

PLANE = ("node", "local")
EVERY = ("rep", "node", "local")


def slot_table(expert_ids, expert_count, slot_cap):
    row_count, top_count = expert_ids.shape
    flat_ids = expert_ids.reshape(-1)
    hits = (flat_ids[:, None] == jnp.arange(expert_count, dtype=jnp.int32)[None, :]).astype(
        jnp.int32
    )
    before = jnp.cumsum(hits, axis=0) - hits
    rank_of = jnp.sum(before * hits, axis=1)
    return (flat_ids * slot_cap + rank_of).reshape(row_count, top_count)


def route_slots(blocks):
    return lax.all_to_all(blocks, PLANE, split_axis=1, concat_axis=1, tiled=True)


def by_slots(tokens, expert_ids, route_weights, gate_local, up_local, down_local, slot_cap):
    model_width = tokens.shape[1]
    plane_count = lax.axis_size("rep")
    expert_count = lax.axis_size("node") * lax.axis_size("local")
    slot_total = expert_count * slot_cap
    slot_of = slot_table(expert_ids, expert_count, slot_cap)
    slot_iota = jnp.arange(slot_total, dtype=jnp.int32)
    placed = jnp.any(slot_of[None, :, :] == slot_iota[:, None, None], axis=2).astype(jnp.bfloat16)
    outgoing = jnp.dot(placed, tokens, preferred_element_type=jnp.float32).astype(jnp.bfloat16)
    mixing = jnp.sum(
        jnp.where(slot_of[:, :, None] == slot_iota[None, None, :], route_weights[:, :, None], 0.0),
        axis=1,
    )
    arrived = route_slots(outgoing.reshape(1, expert_count, slot_cap, model_width))
    arrived = arrived.reshape(slot_total, model_width)
    shard_piece = lax.all_gather(arrived, "rep", axis=0, tiled=True)
    hidden_part = hidden_units(shard_piece, gate_local, up_local)
    expert_out = jnp.dot(
        lax.all_gather(hidden_part, "rep", axis=1, tiled=True),
        down_local,
        preferred_element_type=jnp.float32,
    ).astype(jnp.bfloat16)
    own_slots = lax.all_to_all(
        expert_out.reshape(plane_count, slot_total, down_local.shape[1]),
        "rep",
        split_axis=0,
        concat_axis=2,
        tiled=True,
    )
    returned = route_slots(own_slots.reshape(1, expert_count, slot_cap, model_width))
    back_rows = returned.reshape(slot_total, model_width).astype(jnp.float32)
    mixed_rows = jnp.dot(mixing, back_rows, precision=lax.Precision.HIGHEST)
    return mixed_rows.astype(jnp.bfloat16)


def hidden_units(rows, gate_local, up_local):
    feature_dims = (((1,), (1,)), ((), ()))
    gate = lax.dot_general(rows, gate_local, feature_dims, preferred_element_type=jnp.float32)
    up = lax.dot_general(rows, up_local, feature_dims, preferred_element_type=jnp.float32)
    return (jax.nn.silu(gate) * up).astype(jnp.bfloat16)


def swap(block, axes, mask):
    size = lax.axis_size(axes)
    return lax.ppermute(block, axes, [(place, place ^ mask) for place in range(size)])


def turn(block, first):
    nodes, size = lax.axis_size("node"), lax.axis_size(("rep", "node"))
    mask_of = [2 if (place % 2 == 0) == first else nodes for place in range(size)]
    pairs = [(place, place ^ mask) for place, mask in enumerate(mask_of)]
    return lax.ppermute(block, ("rep", "node"), pairs)


def square(block):
    side = turn(block, True)
    other_side = turn(block, False)
    return [side, turn(side, False), other_side, block]


def wide(block):
    return block.astype(jnp.float32)


def narrow(block):
    return block.astype(jnp.bfloat16)


def pack_kernel(tokens_in, ids_in, weights_in, out_ref, ids_ref, weights_ref, sems, *, experts):
    row_count, width = tokens_in.shape
    tokens_copy = pltpu.make_async_copy(tokens_in, out_ref.at[:, pl.ds(0, width)], sems.at[0])
    ids_copy = pltpu.make_async_copy(ids_in, ids_ref, sems.at[1])
    weights_copy = pltpu.make_async_copy(weights_in, weights_ref, sems.at[2])
    tokens_copy.start()
    ids_copy.start()
    weights_copy.start()
    extra = out_ref.shape[1] - width
    expert = lax.broadcasted_iota(jnp.int32, (extra, row_count), 0) % experts
    share = jnp.zeros(expert.shape, jnp.float32)
    ids_copy.wait()
    weights_copy.wait()
    for k in range(ids_ref.shape[0]):
        share += jnp.where(ids_ref[k : k + 1, :] == expert, weights_ref[k : k + 1, :], 0.0)
    share = jnp.concatenate([share, jnp.zeros((extra, extra - row_count), jnp.float32)], axis=1)
    share = share.T[:row_count]
    piece = lax.broadcasted_iota(jnp.int32, share.shape, 1) // experts
    high = wide(narrow(share))
    middle = wide(narrow(share - high))
    low = share - high - middle
    coded = jnp.where(piece == 0, high, jnp.where(piece == 1, middle, low))
    out_ref[:, width:] = narrow(jnp.where(piece < 3, coded, 0.0))
    tokens_copy.wait()


def fetch_kernel(*refs):
    *parts, out_ref, sems = refs
    row, copies = 0, []
    for place, part in enumerate(parts):
        rows = part.shape[0]
        there = out_ref.at[pl.ds(row, rows), :]
        copies.append(pltpu.make_async_copy(part, there, sems.at[place]))
        copies[-1].start()
        row += rows
    for copy in copies:
        copy.wait()


def gate_up_kernel(*refs, experts, starts, row_count, chunks):
    rows, out_refs = refs[-1], refs[-1 - 2 * chunks : -1]
    block_refs, weight_refs = refs[: len(starts)], refs[len(starts) : len(starts) + 2]
    part_width, width = weight_refs[0].shape[0] // 2, weight_refs[0].shape[1]
    own = lax.axis_index("node") * lax.axis_size("local") + lax.axis_index("local")
    other = own + lax.axis_size("local") * (1 - 2 * (lax.axis_index("node") % 2))
    lanes = lax.broadcasted_iota(jnp.int32, (row_count, block_refs[0].shape[1] - width), 1)
    coded = [
        (lanes % experts == expert) & (lanes < 3 * experts) for expert in (own, other)
    ]
    each = len(starts) // chunks
    core = lax.axis_index("node") % 2
    for place, (block, start) in enumerate(zip(block_refs, starts)):
        there = slice(start, start + row_count)
        chunk, (side, inner) = place // each, divmod(place % each, each // 4)
        if side in (1, 2):
            side = jnp.where(core == 0, side, 3 - side)
        first = pl.multiple_of((side * (each // 4) + inner) * row_count, row_count)
        rows[pl.ds(first + chunk * each * row_count, row_count), :] = block[there, :width]
        pieces = wide(block[there, width:])
        share_ref = out_refs[chunks + chunk]
        for expert in range(2):
            share = jnp.sum(jnp.where(coded[expert], pieces, 0.0), axis=1, keepdims=True)
            share = jnp.broadcast_to(share, (row_count, share_ref.shape[2]))
            share_ref[expert, pl.ds(first, row_count), :] = share
    feature_dims = (((1,), (1,)), ((), ()))
    for side, weights in enumerate(weight_refs):
        both = lax.dot_general(
            weights[...], rows[...], feature_dims, preferred_element_type=jnp.float32
        )
        gate, up = both[:part_width], both[part_width:]
        hidden = narrow((gate * up / (1.0 + jnp.exp(-gate))).T)
        for chunk, hidden_ref in enumerate(out_refs[:chunks]):
            total = hidden_ref.shape[1]
            hidden_ref[side] = hidden[chunk * total : (chunk + 1) * total]


def down_kernel(own_ref, other_ref, share_ref, down_own, down_other, *refs, quarters):
    out_refs = refs[-len(quarters) :]
    plane = lax.axis_index("rep")
    width = down_own.shape[1]
    tile = math.gcd(width, 512)
    total = own_ref.shape[1]
    half, quarter = total // 2, total // 4
    hidden = []
    for side in range(2):
        own = own_ref[side]
        other = jnp.concatenate([other_ref[side, half:], other_ref[side, :half]], axis=0)
        first = jnp.where(plane == 0, own, other)
        second = jnp.where(plane == 0, other, own)
        hidden.append(jnp.concatenate([first, second], axis=1))
    for start in range(0, width, tile):
        here = slice(start, start + tile)
        term = 0.0
        for side, part in enumerate((down_own, down_other)):
            out = jnp.dot(hidden[side], part[:, here], preferred_element_type=jnp.float32)
            term += share_ref[side, :, :1] * wide(narrow(out))
        for out_ref, places in zip(out_refs, quarters):
            rows = [term[place * quarter : (place + 1) * quarter] for place in places]
            out_ref[:, here] = jnp.concatenate(rows, axis=0).astype(out_ref.dtype)


def run(kernel, operands, in_hbm, out_shape, scratch_shapes, flops, room=24, **sizes):
    held, fetched = pl.BlockSpec(memory_space=pltpu.VMEM), pl.BlockSpec(memory_space=pltpu.HBM)
    moved = sum(operand.size * operand.dtype.itemsize for operand in operands)
    return pl.pallas_call(
        functools.partial(kernel, **sizes),
        out_shape=out_shape,
        in_specs=[fetched if place in in_hbm else held for place in range(len(operands))],
        out_specs=jax.tree.map(lambda _: held, out_shape),
        scratch_shapes=scratch_shapes,
        compiler_params=pltpu.CompilerParams(vmem_limit_bytes=room * 1024 * 1024),
        cost_estimate=pl.CostEstimate(flops=flops, bytes_accessed=moved, transcendentals=0),
    )(*operands)


def pack(tokens, expert_ids, route_weights, experts):
    row_count, width = tokens.shape
    extra = -(-3 * experts // 128) * 128
    return run(
        pack_kernel,
        (tokens, expert_ids.T, route_weights.T),
        (0, 1, 2),
        jax.ShapeDtypeStruct((row_count, width + extra), jnp.bfloat16),
        [
            pltpu.VMEM(expert_ids.shape[::-1], jnp.int32),
            pltpu.VMEM(route_weights.shape[::-1], jnp.float32),
            pltpu.SemaphoreType.DMA((3,)),
        ],
        0,
        room=60,
        experts=experts,
    )


def fetch(arrays):
    rows = sum(array.shape[0] for array in arrays)
    return run(
        fetch_kernel,
        arrays,
        range(len(arrays)),
        jax.ShapeDtypeStruct((rows, arrays[0].shape[1]), arrays[0].dtype),
        [pltpu.SemaphoreType.DMA((len(arrays),))],
        0,
    )


def gate_up(parts, row_count, weights, experts):
    part_width, width = weights[0].shape[0] // 2, weights[0].shape[1]
    blocks, starts = zip(*(block for part in parts for block in part))
    total, chunks = len(blocks) * row_count, len(parts)
    outs = run(
        gate_up_kernel,
        (*blocks, *weights),
        (),
        [jax.ShapeDtypeStruct((2, total // chunks, part_width), jnp.bfloat16)] * chunks
        + [jax.ShapeDtypeStruct((2, total // chunks, 128), jnp.float32)] * chunks,
        [pltpu.VMEM((total, width), jnp.bfloat16)],
        8 * total * width * part_width,
        experts=experts,
        starts=starts,
        row_count=row_count,
        chunks=chunks,
    )
    return list(zip(outs[:chunks], outs[chunks:]))


def down(own, other, share, weights, quarters, after=()):
    total = own.shape[1]
    depth, width = weights[0].shape
    sizes = [(len(places) * total // 4, width) for places in quarters]
    return run(
        down_kernel,
        (own, other, share, *weights, *after),
        (),
        [jax.ShapeDtypeStruct(sizes[0], jnp.float32)]
        + [jax.ShapeDtypeStruct(size, jnp.bfloat16) for size in sizes[1:]],
        [],
        4 * total * depth * width,
        quarters=quarters,
    )


def by_rows(tokens, expert_ids, route_weights, gate_local, up_local, down_local):
    row_count = tokens.shape[0]
    experts = lax.axis_size("node") * lax.axis_size("local")
    places = lax.axis_size("local")
    plane = lax.axis_index("rep")
    together = lax.optimization_barrier

    packed = pack(tokens, expert_ids, route_weights, experts)
    line_3, line_1, square_0, gates = together(
        (
            swap(packed, "local", 3),
            swap(packed, "local", 1),
            square(packed),
            fetch((gate_local, up_local)),
        )
    )
    other_gates = swap(gates, "node", 1)
    block_13 = jnp.concatenate([line_1, line_3], axis=0)
    side_13, other_13, line_2 = turn(block_13, True), turn(block_13, False), swap(line_3, "local", 1)
    line_2, side_13, other_13, downs = together((line_2, side_13, other_13, fetch((down_local,))))
    square_13 = [side_13, turn(side_13, False), other_13, block_13]

    def hidden_of(*parts):
        order = (3, 0, 2, 1)
        blocks = [(square[side], row) for side in order for square, row in parts]
        return gate_up((blocks,), row_count, (gates, other_gates), experts)[0]

    def exchanged(hidden, share):
        return hidden, swap(hidden, "rep", 1), share

    def square_back(keep, send_y, send_x, send_across):
        across = swap(send_across, ("rep", "node"), lax.axis_size("node") | 2)
        along_x = swap(send_x, "rep", 1)
        return keep, swap(send_y, "node", 2), along_x, across

    def square_sum(keep, back_y, back_x, back_across):
        own, other = keep + wide(back_y), wide(back_x) + wide(back_across)
        return jnp.stack([own, other]).reshape(2, 2, row_count, -1)

    hidden_b = hidden_of((square_13, 0), (square_13, row_count))
    hidden_b, square_2, other_downs = together(
        (hidden_b, square(line_2), swap(downs, "node", 1))
    )
    weights = (downs, other_downs)
    hidden_a = hidden_of((square_0, 0), (square_2, 0))
    hidden_b, hidden_a = exchanged(*hidden_b), exchanged(*hidden_a)
    quarters = ((0,), (1,), (2,), (3,))
    meeting = swap(hidden_a[2][0, :8], "node", 1)
    back_b = square_back(*down(*hidden_b, weights, quarters, (meeting,)))
    hidden_a, back_y = together((hidden_a, back_b[1]))
    sum_b = square_sum(back_b[0], back_y, *back_b[2:])
    sum_a = square_sum(*square_back(*down(*hidden_a, weights, quarters)))
    sum_a = sum_a + wide(swap(narrow(sum_b), "local", 1))
    own, other = narrow(sum_a[:, 0] + wide(swap(narrow(sum_a[:, 1]), "local", 2)))
    return jnp.where(
        plane == 0,
        jnp.concatenate([own, other], axis=1),
        jnp.concatenate([other, own], axis=1),
    )


def on_device(tokens, expert_ids, route_weights, gate_weight, up_weight, down_weight):
    row_count, top_count = expert_ids.shape
    expert_count = lax.axis_size("node") * lax.axis_size("local")
    slot_cap = min(row_count, max(2, 2 * row_count * top_count // expert_count))
    weights = (gate_weight[0], up_weight[0], down_weight[0])
    if slot_cap == row_count:
        return by_rows(tokens, expert_ids, route_weights, *weights)
    return by_slots(tokens, expert_ids, route_weights, *weights, slot_cap)


def solution(mesh):
    placed = (
        P(EVERY, None),
        P(EVERY, None),
        P(EVERY, None),
        P(PLANE, "rep", None),
        P(PLANE, "rep", None),
        P(PLANE, None, "rep"),
    )
    return jax.shard_map(
        on_device,
        mesh=mesh,
        in_specs=placed,
        out_specs=P(EVERY, None),
        check_vma=False,
    )
```

```python
import functools
import math

import jax
import jax.numpy as jnp
from jax import lax
from jax.experimental import pallas as pl
from jax.experimental.pallas import tpu as pltpu
from jax.sharding import PartitionSpec as P

PLANE = ("node", "local")
EVERY = ("rep", "node", "local")


def slot_table(expert_ids, expert_count, slot_cap):
    row_count, top_count = expert_ids.shape
    flat_ids = expert_ids.reshape(-1)
    hits = (flat_ids[:, None] == jnp.arange(expert_count, dtype=jnp.int32)[None, :]).astype(
        jnp.int32
    )
    before = jnp.cumsum(hits, axis=0) - hits
    rank_of = jnp.sum(before * hits, axis=1)
    return (flat_ids * slot_cap + rank_of).reshape(row_count, top_count)


def route_slots(blocks):
    return lax.all_to_all(blocks, PLANE, split_axis=1, concat_axis=1, tiled=True)


def by_slots(tokens, expert_ids, route_weights, gate_local, up_local, down_local, slot_cap):
    model_width = tokens.shape[1]
    plane_count = lax.axis_size("rep")
    expert_count = lax.axis_size("node") * lax.axis_size("local")
    slot_total = expert_count * slot_cap
    slot_of = slot_table(expert_ids, expert_count, slot_cap)
    slot_iota = jnp.arange(slot_total, dtype=jnp.int32)
    placed = jnp.any(slot_of[None, :, :] == slot_iota[:, None, None], axis=2).astype(jnp.bfloat16)
    outgoing = jnp.dot(placed, tokens, preferred_element_type=jnp.float32).astype(jnp.bfloat16)
    mixing = jnp.sum(
        jnp.where(slot_of[:, :, None] == slot_iota[None, None, :], route_weights[:, :, None], 0.0),
        axis=1,
    )
    arrived = route_slots(outgoing.reshape(1, expert_count, slot_cap, model_width))
    arrived = arrived.reshape(slot_total, model_width)
    shard_piece = lax.all_gather(arrived, "rep", axis=0, tiled=True)
    hidden_part = hidden_units(shard_piece, gate_local, up_local)
    expert_out = jnp.dot(
        lax.all_gather(hidden_part, "rep", axis=1, tiled=True),
        down_local,
        preferred_element_type=jnp.float32,
    ).astype(jnp.bfloat16)
    own_slots = lax.all_to_all(
        expert_out.reshape(plane_count, slot_total, down_local.shape[1]),
        "rep",
        split_axis=0,
        concat_axis=2,
        tiled=True,
    )
    returned = route_slots(own_slots.reshape(1, expert_count, slot_cap, model_width))
    back_rows = returned.reshape(slot_total, model_width).astype(jnp.float32)
    mixed_rows = jnp.dot(mixing, back_rows, precision=lax.Precision.HIGHEST)
    return mixed_rows.astype(jnp.bfloat16)


def hidden_units(rows, gate_local, up_local):
    feature_dims = (((1,), (1,)), ((), ()))
    gate = lax.dot_general(rows, gate_local, feature_dims, preferred_element_type=jnp.float32)
    up = lax.dot_general(rows, up_local, feature_dims, preferred_element_type=jnp.float32)
    return (jax.nn.silu(gate) * up).astype(jnp.bfloat16)


def swap(block, axes, mask):
    size = lax.axis_size(axes)
    return lax.ppermute(block, axes, [(place, place ^ mask) for place in range(size)])


def turn(block, first):
    nodes, size = lax.axis_size("node"), lax.axis_size(("rep", "node"))
    mask_of = [2 if (place % 2 == 0) == first else nodes for place in range(size)]
    pairs = [(place, place ^ mask) for place, mask in enumerate(mask_of)]
    return lax.ppermute(block, ("rep", "node"), pairs)


def square(block):
    side = turn(block, True)
    other_side = turn(block, False)
    return [side, turn(side, False), other_side, block]


def wide(block):
    return block.astype(jnp.float32)


def narrow(block):
    return block.astype(jnp.bfloat16)


def pack_kernel(tokens_in, ids_in, weights_in, out_ref, ids_ref, weights_ref, sems, *, experts):
    row_count, width = tokens_in.shape
    tokens_copy = pltpu.make_async_copy(tokens_in, out_ref.at[:, pl.ds(0, width)], sems.at[0])
    ids_copy = pltpu.make_async_copy(ids_in, ids_ref, sems.at[1])
    weights_copy = pltpu.make_async_copy(weights_in, weights_ref, sems.at[2])
    tokens_copy.start()
    ids_copy.start()
    weights_copy.start()
    extra = out_ref.shape[1] - width
    expert = lax.broadcasted_iota(jnp.int32, (extra, row_count), 0) % experts
    share = jnp.zeros(expert.shape, jnp.float32)
    ids_copy.wait()
    weights_copy.wait()
    for k in range(ids_ref.shape[0]):
        share += jnp.where(ids_ref[k : k + 1, :] == expert, weights_ref[k : k + 1, :], 0.0)
    share = jnp.concatenate([share, jnp.zeros((extra, extra - row_count), jnp.float32)], axis=1)
    share = share.T[:row_count]
    piece = lax.broadcasted_iota(jnp.int32, share.shape, 1) // experts
    high = wide(narrow(share))
    middle = wide(narrow(share - high))
    low = share - high - middle
    coded = jnp.where(piece == 0, high, jnp.where(piece == 1, middle, low))
    out_ref[:, width:] = narrow(jnp.where(piece < 3, coded, 0.0))
    tokens_copy.wait()


def fetch_kernel(*refs):
    *parts, out_ref, sems = refs
    row, copies = 0, []
    for place, part in enumerate(parts):
        rows = part.shape[0]
        there = out_ref.at[pl.ds(row, rows), :]
        copies.append(pltpu.make_async_copy(part, there, sems.at[place]))
        copies[-1].start()
        row += rows
    for copy in copies:
        copy.wait()


def gate_up_kernel(*refs, experts, starts, row_count, chunks):
    rows, out_refs = refs[-1], refs[-1 - 2 * chunks : -1]
    block_refs, weight_refs = refs[: len(starts)], refs[len(starts) : len(starts) + 2]
    part_width, width = weight_refs[0].shape[0] // 2, weight_refs[0].shape[1]
    own = lax.axis_index("node") * lax.axis_size("local") + lax.axis_index("local")
    other = own + lax.axis_size("local") * (1 - 2 * (lax.axis_index("node") % 2))
    lanes = lax.broadcasted_iota(jnp.int32, (row_count, block_refs[0].shape[1] - width), 1)
    coded = [
        (lanes % experts == expert) & (lanes < 3 * experts) for expert in (own, other)
    ]
    each = len(starts) // chunks
    core = lax.axis_index("node") % 2
    for place, (block, start) in enumerate(zip(block_refs, starts)):
        there = slice(start, start + row_count)
        chunk, (side, inner) = place // each, divmod(place % each, each // 4)
        if side in (1, 2):
            side = jnp.where(core == 0, side, 3 - side)
        first = pl.multiple_of((side * (each // 4) + inner) * row_count, row_count)
        rows[pl.ds(first + chunk * each * row_count, row_count), :] = block[there, :width]
        pieces = wide(block[there, width:])
        share_ref = out_refs[chunks + chunk]
        for expert in range(2):
            share = jnp.sum(jnp.where(coded[expert], pieces, 0.0), axis=1, keepdims=True)
            share = jnp.broadcast_to(share, (row_count, share_ref.shape[2]))
            share_ref[expert, pl.ds(first, row_count), :] = share
    feature_dims = (((1,), (1,)), ((), ()))
    for side, weights in enumerate(weight_refs):
        both = lax.dot_general(
            weights[...], rows[...], feature_dims, preferred_element_type=jnp.float32
        )
        gate, up = both[:part_width], both[part_width:]
        hidden = narrow((gate * up / (1.0 + jnp.exp(-gate))).T)
        for chunk, hidden_ref in enumerate(out_refs[:chunks]):
            total = hidden_ref.shape[1]
            hidden_ref[side] = hidden[chunk * total : (chunk + 1) * total]


def down_kernel(own_ref, other_ref, share_ref, down_own, down_other, *refs, quarters):
    out_refs = refs[-len(quarters) :]
    plane = lax.axis_index("rep")
    width = down_own.shape[1]
    tile = math.gcd(width, 512)
    total = own_ref.shape[1]
    half, quarter = total // 2, total // 4
    hidden = []
    for side in range(2):
        own = own_ref[side]
        other = jnp.concatenate([other_ref[side, half:], other_ref[side, :half]], axis=0)
        first = jnp.where(plane == 0, own, other)
        second = jnp.where(plane == 0, other, own)
        hidden.append(jnp.concatenate([first, second], axis=1))
    for start in range(0, width, tile):
        here = slice(start, start + tile)
        term = 0.0
        for side, part in enumerate((down_own, down_other)):
            out = jnp.dot(hidden[side], part[:, here], preferred_element_type=jnp.float32)
            term += share_ref[side, :, :1] * wide(narrow(out))
        for out_ref, places in zip(out_refs, quarters):
            rows = [term[place * quarter : (place + 1) * quarter] for place in places]
            out_ref[:, here] = jnp.concatenate(rows, axis=0).astype(out_ref.dtype)


def run(kernel, operands, in_hbm, out_shape, scratch_shapes, flops, room=24, **sizes):
    held, fetched = pl.BlockSpec(memory_space=pltpu.VMEM), pl.BlockSpec(memory_space=pltpu.HBM)
    moved = sum(operand.size * operand.dtype.itemsize for operand in operands)
    return pl.pallas_call(
        functools.partial(kernel, **sizes),
        out_shape=out_shape,
        in_specs=[fetched if place in in_hbm else held for place in range(len(operands))],
        out_specs=jax.tree.map(lambda _: held, out_shape),
        scratch_shapes=scratch_shapes,
        compiler_params=pltpu.CompilerParams(vmem_limit_bytes=room * 1024 * 1024),
        cost_estimate=pl.CostEstimate(flops=flops, bytes_accessed=moved, transcendentals=0),
    )(*operands)


def pack(tokens, expert_ids, route_weights, experts):
    row_count, width = tokens.shape
    extra = -(-3 * experts // 128) * 128
    return run(
        pack_kernel,
        (tokens, expert_ids.T, route_weights.T),
        (0, 1, 2),
        jax.ShapeDtypeStruct((row_count, width + extra), jnp.bfloat16),
        [
            pltpu.VMEM(expert_ids.shape[::-1], jnp.int32),
            pltpu.VMEM(route_weights.shape[::-1], jnp.float32),
            pltpu.SemaphoreType.DMA((3,)),
        ],
        0,
        room=60,
        experts=experts,
    )


def fetch(arrays):
    rows = sum(array.shape[0] for array in arrays)
    return run(
        fetch_kernel,
        arrays,
        range(len(arrays)),
        jax.ShapeDtypeStruct((rows, arrays[0].shape[1]), arrays[0].dtype),
        [pltpu.SemaphoreType.DMA((len(arrays),))],
        0,
    )


def gate_up(parts, row_count, weights, experts):
    part_width, width = weights[0].shape[0] // 2, weights[0].shape[1]
    blocks, starts = zip(*(block for part in parts for block in part))
    total, chunks = len(blocks) * row_count, len(parts)
    outs = run(
        gate_up_kernel,
        (*blocks, *weights),
        (),
        [jax.ShapeDtypeStruct((2, total // chunks, part_width), jnp.bfloat16)] * chunks
        + [jax.ShapeDtypeStruct((2, total // chunks, 128), jnp.float32)] * chunks,
        [pltpu.VMEM((total, width), jnp.bfloat16)],
        8 * total * width * part_width,
        experts=experts,
        starts=starts,
        row_count=row_count,
        chunks=chunks,
    )
    return list(zip(outs[:chunks], outs[chunks:]))


def down(own, other, share, weights, quarters, after=()):
    total = own.shape[1]
    depth, width = weights[0].shape
    sizes = [(len(places) * total // 4, width) for places in quarters]
    return run(
        down_kernel,
        (own, other, share, *weights, *after),
        (),
        [jax.ShapeDtypeStruct(sizes[0], jnp.float32)]
        + [jax.ShapeDtypeStruct(size, jnp.bfloat16) for size in sizes[1:]],
        [],
        4 * total * depth * width,
        quarters=quarters,
    )


def by_rows(tokens, expert_ids, route_weights, gate_local, up_local, down_local):
    row_count = tokens.shape[0]
    experts = lax.axis_size("node") * lax.axis_size("local")
    places = lax.axis_size("local")
    plane = lax.axis_index("rep")
    together = lax.optimization_barrier

    packed = pack(tokens, expert_ids, route_weights, experts)
    line_3, line_1, square_0, gates = together(
        (
            swap(packed, "local", 3),
            swap(packed, "local", 1),
            square(packed),
            fetch((gate_local, up_local)),
        )
    )
    other_gates = swap(gates, "node", 1)
    block_13 = jnp.concatenate([line_1, line_3], axis=0)
    side_13, other_13, line_2 = turn(block_13, True), turn(block_13, False), swap(line_3, "local", 1)
    line_2, side_13, other_13, downs = together((line_2, side_13, other_13, fetch((down_local,))))
    square_13 = [side_13, turn(side_13, False), other_13, block_13]

    def hidden_of(*parts):
        order = (3, 0, 2, 1)
        blocks = [(square[side], row) for side in order for square, row in parts]
        return gate_up((blocks,), row_count, (gates, other_gates), experts)[0]

    def exchanged(hidden, share):
        return hidden, swap(hidden, "rep", 1), share

    hidden_b = hidden_of((square_13, 0), (square_13, row_count))
    hidden_b, square_2, other_downs = together(
        (hidden_b, square(line_2), swap(downs, "node", 1))
    )
    weights = (downs, other_downs)
    hidden_a = hidden_of((square_0, 0), (square_2, 0))
    hidden_b, hidden_a = exchanged(*hidden_b), exchanged(*hidden_a)
    meeting = swap(hidden_a[2][0, :8], "node", 1)
    keep, send_y = down(*hidden_b, weights, ((0, 2), (1, 3)), (meeting,))
    back_y = swap(send_y, "node", 2)
    keep_a, send_y, send_x, send_across = down(*hidden_a, weights, ((0,), (1,), (2,), (3,)))
    across = swap(send_across, ("rep", "node"), lax.axis_size("node") | 2)
    along_x, along_y = swap(send_x, "rep", 1), swap(send_y, "node", 2)
    here, there = narrow(keep + wide(back_y)).reshape(2, 2 * row_count, -1)
    there = swap(there, ("rep", "local"), places | 1)
    here = swap(here, "local", 1)
    own = keep_a + wide(along_y) + wide(here)
    other = wide(along_x) + wide(across) + wide(there)
    total = jnp.stack([own, other]).reshape(2, 2, row_count, -1)
    own, other = narrow(total[:, 0] + wide(swap(narrow(total[:, 1]), "local", 2)))
    return jnp.where(
        plane == 0,
        jnp.concatenate([own, other], axis=1),
        jnp.concatenate([other, own], axis=1),
    )


def on_device(tokens, expert_ids, route_weights, gate_weight, up_weight, down_weight):
    row_count, top_count = expert_ids.shape
    expert_count = lax.axis_size("node") * lax.axis_size("local")
    slot_cap = min(row_count, max(2, 2 * row_count * top_count // expert_count))
    weights = (gate_weight[0], up_weight[0], down_weight[0])
    if slot_cap == row_count:
        return by_rows(tokens, expert_ids, route_weights, *weights)
    return by_slots(tokens, expert_ids, route_weights, *weights, slot_cap)


def solution(mesh):
    placed = (
        P(EVERY, None),
        P(EVERY, None),
        P(EVERY, None),
        P(PLANE, "rep", None),
        P(PLANE, "rep", None),
        P(PLANE, None, "rep"),
    )
    return jax.shard_map(
        on_device,
        mesh=mesh,
        in_specs=placed,
        out_specs=P(EVERY, None),
        check_vma=False,
    )
```

```python
import functools
import math

import jax
import jax.numpy as jnp
from jax import lax
from jax.experimental import pallas as pl
from jax.experimental.pallas import tpu as pltpu
from jax.sharding import PartitionSpec as P

PLANE = ("node", "local")
EVERY = ("rep", "node", "local")


def slot_table(expert_ids, expert_count, slot_cap):
    row_count, top_count = expert_ids.shape
    flat_ids = expert_ids.reshape(-1)
    hits = (flat_ids[:, None] == jnp.arange(expert_count, dtype=jnp.int32)[None, :]).astype(
        jnp.int32
    )
    before = jnp.cumsum(hits, axis=0) - hits
    rank_of = jnp.sum(before * hits, axis=1)
    return (flat_ids * slot_cap + rank_of).reshape(row_count, top_count)


def route_slots(blocks):
    return lax.all_to_all(blocks, PLANE, split_axis=1, concat_axis=1, tiled=True)


def by_slots(tokens, expert_ids, route_weights, gate_local, up_local, down_local, slot_cap):
    model_width = tokens.shape[1]
    plane_count = lax.axis_size("rep")
    expert_count = lax.axis_size("node") * lax.axis_size("local")
    slot_total = expert_count * slot_cap
    slot_of = slot_table(expert_ids, expert_count, slot_cap)
    slot_iota = jnp.arange(slot_total, dtype=jnp.int32)
    placed = jnp.any(slot_of[None, :, :] == slot_iota[:, None, None], axis=2).astype(jnp.bfloat16)
    outgoing = jnp.dot(placed, tokens, preferred_element_type=jnp.float32).astype(jnp.bfloat16)
    mixing = jnp.sum(
        jnp.where(slot_of[:, :, None] == slot_iota[None, None, :], route_weights[:, :, None], 0.0),
        axis=1,
    )
    arrived = route_slots(outgoing.reshape(1, expert_count, slot_cap, model_width))
    arrived = arrived.reshape(slot_total, model_width)
    shard_piece = lax.all_gather(arrived, "rep", axis=0, tiled=True)
    hidden_part = hidden_units(shard_piece, gate_local, up_local)
    expert_out = jnp.dot(
        lax.all_gather(hidden_part, "rep", axis=1, tiled=True),
        down_local,
        preferred_element_type=jnp.float32,
    ).astype(jnp.bfloat16)
    own_slots = lax.all_to_all(
        expert_out.reshape(plane_count, slot_total, down_local.shape[1]),
        "rep",
        split_axis=0,
        concat_axis=2,
        tiled=True,
    )
    returned = route_slots(own_slots.reshape(1, expert_count, slot_cap, model_width))
    back_rows = returned.reshape(slot_total, model_width).astype(jnp.float32)
    mixed_rows = jnp.dot(mixing, back_rows, precision=lax.Precision.HIGHEST)
    return mixed_rows.astype(jnp.bfloat16)


def hidden_units(rows, gate_local, up_local):
    feature_dims = (((1,), (1,)), ((), ()))
    gate = lax.dot_general(rows, gate_local, feature_dims, preferred_element_type=jnp.float32)
    up = lax.dot_general(rows, up_local, feature_dims, preferred_element_type=jnp.float32)
    return (jax.nn.silu(gate) * up).astype(jnp.bfloat16)


def swap(block, axes, mask):
    size = lax.axis_size(axes)
    return lax.ppermute(block, axes, [(place, place ^ mask) for place in range(size)])


def turn(block, first):
    nodes, size = lax.axis_size("node"), lax.axis_size(("rep", "node"))
    mask_of = [2 if (place % 2 == 0) == first else nodes for place in range(size)]
    pairs = [(place, place ^ mask) for place, mask in enumerate(mask_of)]
    return lax.ppermute(block, ("rep", "node"), pairs)


def square(block):
    side = turn(block, True)
    other_side = turn(block, False)
    return [side, turn(side, False), other_side, block]


def wide(block):
    return block.astype(jnp.float32)


def narrow(block):
    return block.astype(jnp.bfloat16)


def pack_kernel(tokens_in, ids_in, weights_in, out_ref, ids_ref, weights_ref, sems, *, experts):
    row_count, width = tokens_in.shape
    tokens_copy = pltpu.make_async_copy(tokens_in, out_ref.at[:, pl.ds(0, width)], sems.at[0])
    ids_copy = pltpu.make_async_copy(ids_in, ids_ref, sems.at[1])
    weights_copy = pltpu.make_async_copy(weights_in, weights_ref, sems.at[2])
    tokens_copy.start()
    ids_copy.start()
    weights_copy.start()
    extra = out_ref.shape[1] - width
    expert = lax.broadcasted_iota(jnp.int32, (extra, row_count), 0) % experts
    share = jnp.zeros(expert.shape, jnp.float32)
    ids_copy.wait()
    weights_copy.wait()
    for k in range(ids_ref.shape[0]):
        share += jnp.where(ids_ref[k : k + 1, :] == expert, weights_ref[k : k + 1, :], 0.0)
    share = jnp.concatenate([share, jnp.zeros((extra, extra - row_count), jnp.float32)], axis=1)
    share = share.T[:row_count]
    piece = lax.broadcasted_iota(jnp.int32, share.shape, 1) // experts
    high = wide(narrow(share))
    middle = wide(narrow(share - high))
    low = share - high - middle
    coded = jnp.where(piece == 0, high, jnp.where(piece == 1, middle, low))
    out_ref[:, width:] = narrow(jnp.where(piece < 3, coded, 0.0))
    tokens_copy.wait()


def fetch_kernel(*refs):
    *parts, out_ref, sems = refs
    row, copies = 0, []
    for place, part in enumerate(parts):
        rows = part.shape[0]
        there = out_ref.at[pl.ds(row, rows), :]
        copies.append(pltpu.make_async_copy(part, there, sems.at[place]))
        copies[-1].start()
        row += rows
    for copy in copies:
        copy.wait()


def gate_up_kernel(*refs, experts, starts, row_count, chunks):
    rows, out_refs = refs[-1], refs[-1 - 2 * chunks : -1]
    block_refs, weight_refs = refs[: len(starts)], refs[len(starts) : len(starts) + 2]
    part_width, width = weight_refs[0].shape[0] // 2, weight_refs[0].shape[1]
    own = lax.axis_index("node") * lax.axis_size("local") + lax.axis_index("local")
    other = own + lax.axis_size("local") * (1 - 2 * (lax.axis_index("node") % 2))
    lanes = lax.broadcasted_iota(jnp.int32, (row_count, block_refs[0].shape[1] - width), 1)
    coded = [
        (lanes % experts == expert) & (lanes < 3 * experts) for expert in (own, other)
    ]
    each = len(starts) // chunks
    core = lax.axis_index("node") % 2
    for place, (block, start) in enumerate(zip(block_refs, starts)):
        there = slice(start, start + row_count)
        chunk, (side, inner) = place // each, divmod(place % each, each // 4)
        if side in (1, 2):
            side = jnp.where(core == 0, side, 3 - side)
        first = pl.multiple_of((side * (each // 4) + inner) * row_count, row_count)
        rows[pl.ds(first + chunk * each * row_count, row_count), :] = block[there, :width]
        pieces = wide(block[there, width:])
        share_ref = out_refs[chunks + chunk]
        for expert in range(2):
            share = jnp.sum(jnp.where(coded[expert], pieces, 0.0), axis=1, keepdims=True)
            share = jnp.broadcast_to(share, (row_count, share_ref.shape[2]))
            share_ref[expert, pl.ds(first, row_count), :] = share
    feature_dims = (((1,), (1,)), ((), ()))
    for side, weights in enumerate(weight_refs):
        both = lax.dot_general(
            weights[...], rows[...], feature_dims, preferred_element_type=jnp.float32
        )
        gate, up = both[:part_width], both[part_width:]
        hidden = narrow((gate * up / (1.0 + jnp.exp(-gate))).T)
        for chunk, hidden_ref in enumerate(out_refs[:chunks]):
            total = hidden_ref.shape[1]
            hidden_ref[side] = hidden[chunk * total : (chunk + 1) * total]


def down_kernel(own_ref, other_ref, share_ref, down_own, down_other, *refs, quarters):
    out_refs = refs[-len(quarters) :]
    plane = lax.axis_index("rep")
    width = down_own.shape[1]
    tile = math.gcd(width, 512)
    total = own_ref.shape[1]
    half, quarter = total // 2, total // 4
    hidden = []
    for side in range(2):
        own = own_ref[side]
        other = jnp.concatenate([other_ref[side, half:], other_ref[side, :half]], axis=0)
        first = jnp.where(plane == 0, own, other)
        second = jnp.where(plane == 0, other, own)
        hidden.append(jnp.concatenate([first, second], axis=1))
    for start in range(0, width, tile):
        here = slice(start, start + tile)
        term = 0.0
        for side, part in enumerate((down_own, down_other)):
            out = jnp.dot(hidden[side], part[:, here], preferred_element_type=jnp.float32)
            term += share_ref[side, :, :1] * wide(narrow(out))
        for out_ref, places in zip(out_refs, quarters):
            rows = [term[place * quarter : (place + 1) * quarter] for place in places]
            out_ref[:, here] = jnp.concatenate(rows, axis=0).astype(out_ref.dtype)


def run(kernel, operands, in_hbm, out_shape, scratch_shapes, flops, room=24, **sizes):
    held, fetched = pl.BlockSpec(memory_space=pltpu.VMEM), pl.BlockSpec(memory_space=pltpu.HBM)
    moved = sum(operand.size * operand.dtype.itemsize for operand in operands)
    return pl.pallas_call(
        functools.partial(kernel, **sizes),
        out_shape=out_shape,
        in_specs=[fetched if place in in_hbm else held for place in range(len(operands))],
        out_specs=jax.tree.map(lambda _: held, out_shape),
        scratch_shapes=scratch_shapes,
        compiler_params=pltpu.CompilerParams(vmem_limit_bytes=room * 1024 * 1024),
        cost_estimate=pl.CostEstimate(flops=flops, bytes_accessed=moved, transcendentals=0),
    )(*operands)


def pack(tokens, expert_ids, route_weights, experts):
    row_count, width = tokens.shape
    extra = -(-3 * experts // 128) * 128
    return run(
        pack_kernel,
        (tokens, expert_ids.T, route_weights.T),
        (0, 1, 2),
        jax.ShapeDtypeStruct((row_count, width + extra), jnp.bfloat16),
        [
            pltpu.VMEM(expert_ids.shape[::-1], jnp.int32),
            pltpu.VMEM(route_weights.shape[::-1], jnp.float32),
            pltpu.SemaphoreType.DMA((3,)),
        ],
        0,
        room=60,
        experts=experts,
    )


def fetch(arrays):
    rows = sum(array.shape[0] for array in arrays)
    return run(
        fetch_kernel,
        arrays,
        range(len(arrays)),
        jax.ShapeDtypeStruct((rows, arrays[0].shape[1]), arrays[0].dtype),
        [pltpu.SemaphoreType.DMA((len(arrays),))],
        0,
    )


def gate_up(parts, row_count, weights, experts):
    part_width, width = weights[0].shape[0] // 2, weights[0].shape[1]
    blocks, starts = zip(*(block for part in parts for block in part))
    total, chunks = len(blocks) * row_count, len(parts)
    outs = run(
        gate_up_kernel,
        (*blocks, *weights),
        (),
        [jax.ShapeDtypeStruct((2, total // chunks, part_width), jnp.bfloat16)] * chunks
        + [jax.ShapeDtypeStruct((2, total // chunks, 128), jnp.float32)] * chunks,
        [pltpu.VMEM((total, width), jnp.bfloat16)],
        8 * total * width * part_width,
        experts=experts,
        starts=starts,
        row_count=row_count,
        chunks=chunks,
    )
    return list(zip(outs[:chunks], outs[chunks:]))


def down(own, other, share, weights, quarters, after=()):
    total = own.shape[1]
    depth, width = weights[0].shape
    sizes = [(len(places) * total // 4, width) for places in quarters]
    return run(
        down_kernel,
        (own, other, share, *weights, *after),
        (),
        [jax.ShapeDtypeStruct(sizes[0], jnp.float32)]
        + [jax.ShapeDtypeStruct(size, jnp.bfloat16) for size in sizes[1:]],
        [],
        4 * total * depth * width,
        quarters=quarters,
    )


def by_rows(tokens, expert_ids, route_weights, gate_local, up_local, down_local):
    row_count = tokens.shape[0]
    experts = lax.axis_size("node") * lax.axis_size("local")
    places = lax.axis_size("local")
    plane = lax.axis_index("rep")
    together = lax.optimization_barrier

    packed = pack(tokens, expert_ids, route_weights, experts)
    line_3, line_1, square_0, gates = together(
        (
            swap(packed, "local", 3),
            swap(packed, "local", 1),
            square(packed),
            fetch((gate_local, up_local)),
        )
    )
    other_gates = swap(gates, "node", 1)
    block_13 = jnp.concatenate([line_1, line_3], axis=0)
    side_13, other_13, line_2 = turn(block_13, True), turn(block_13, False), swap(line_3, "local", 1)
    line_2, side_13, other_13, downs = together((line_2, side_13, other_13, fetch((down_local,))))
    square_13 = [side_13, turn(side_13, False), other_13, block_13]

    def hidden_of(*parts):
        order = (3, 0, 2, 1)
        blocks = [(square[side], row) for side in order for square, row in parts]
        return gate_up((blocks,), row_count, (gates, other_gates), experts)[0]

    def exchanged(hidden, share):
        return hidden, swap(hidden, "rep", 1), share

    hidden_b = hidden_of((square_13, 0), (square_13, row_count))
    hidden_b, square_2, other_downs = together(
        (hidden_b, square(line_2), swap(downs, "node", 1))
    )
    weights = (downs, other_downs)
    hidden_a = hidden_of((square_0, 0), (square_2, 0))
    hidden_b, hidden_a = exchanged(*hidden_b), exchanged(*hidden_a)
    meeting = swap(hidden_a[2][0, :8], "node", 1)
    keep, send_y = down(*hidden_b, weights, ((0, 2), (1, 3)), (meeting,))
    back_y = swap(send_y, "node", 2)
    keep_a, send_y, send_x, send_across = down(*hidden_a, weights, ((0,), (1,), (2,), (3,)))
    across = swap(send_across, ("rep", "node"), lax.axis_size("node") | 2)
    along_x, along_y = swap(send_x, "rep", 1), swap(send_y, "node", 2)
    here, there = narrow(keep + wide(back_y)).reshape(2, 2 * row_count, -1)
    there = swap(there, ("rep", "local"), places | 1)
    here = swap(here, "local", 1)
    along_y, across, here, there = together((along_y, across, here, there))
    own = keep_a + wide(along_y) + wide(here)
    other = wide(along_x) + wide(across) + wide(there)
    total = jnp.stack([own, other]).reshape(2, 2, row_count, -1)
    own, other = narrow(total[:, 0] + wide(swap(narrow(total[:, 1]), "local", 2)))
    return jnp.where(
        plane == 0,
        jnp.concatenate([own, other], axis=1),
        jnp.concatenate([other, own], axis=1),
    )


def on_device(tokens, expert_ids, route_weights, gate_weight, up_weight, down_weight):
    row_count, top_count = expert_ids.shape
    expert_count = lax.axis_size("node") * lax.axis_size("local")
    slot_cap = min(row_count, max(2, 2 * row_count * top_count // expert_count))
    weights = (gate_weight[0], up_weight[0], down_weight[0])
    if slot_cap == row_count:
        return by_rows(tokens, expert_ids, route_weights, *weights)
    return by_slots(tokens, expert_ids, route_weights, *weights, slot_cap)


def solution(mesh):
    placed = (
        P(EVERY, None),
        P(EVERY, None),
        P(EVERY, None),
        P(PLANE, "rep", None),
        P(PLANE, "rep", None),
        P(PLANE, None, "rep"),
    )
    return jax.shard_map(
        on_device,
        mesh=mesh,
        in_specs=placed,
        out_specs=P(EVERY, None),
        check_vma=False,
    )
```

```python
import functools
import math

import jax
import jax.numpy as jnp
from jax import lax
from jax.experimental import pallas as pl
from jax.experimental.pallas import tpu as pltpu
from jax.sharding import PartitionSpec as P

PLANE = ("node", "local")
EVERY = ("rep", "node", "local")


def slot_table(expert_ids, expert_count, slot_cap):
    row_count, top_count = expert_ids.shape
    flat_ids = expert_ids.reshape(-1)
    hits = (flat_ids[:, None] == jnp.arange(expert_count, dtype=jnp.int32)[None, :]).astype(
        jnp.int32
    )
    before = jnp.cumsum(hits, axis=0) - hits
    rank_of = jnp.sum(before * hits, axis=1)
    return (flat_ids * slot_cap + rank_of).reshape(row_count, top_count)


def route_slots(blocks):
    return lax.all_to_all(blocks, PLANE, split_axis=1, concat_axis=1, tiled=True)


def by_slots(tokens, expert_ids, route_weights, gate_local, up_local, down_local, slot_cap):
    model_width = tokens.shape[1]
    plane_count = lax.axis_size("rep")
    expert_count = lax.axis_size("node") * lax.axis_size("local")
    slot_total = expert_count * slot_cap
    slot_of = slot_table(expert_ids, expert_count, slot_cap)
    slot_iota = jnp.arange(slot_total, dtype=jnp.int32)
    placed = jnp.any(slot_of[None, :, :] == slot_iota[:, None, None], axis=2).astype(jnp.bfloat16)
    outgoing = jnp.dot(placed, tokens, preferred_element_type=jnp.float32).astype(jnp.bfloat16)
    mixing = jnp.sum(
        jnp.where(slot_of[:, :, None] == slot_iota[None, None, :], route_weights[:, :, None], 0.0),
        axis=1,
    )
    arrived = route_slots(outgoing.reshape(1, expert_count, slot_cap, model_width))
    arrived = arrived.reshape(slot_total, model_width)
    shard_piece = lax.all_gather(arrived, "rep", axis=0, tiled=True)
    hidden_part = hidden_units(shard_piece, gate_local, up_local)
    expert_out = jnp.dot(
        lax.all_gather(hidden_part, "rep", axis=1, tiled=True),
        down_local,
        preferred_element_type=jnp.float32,
    ).astype(jnp.bfloat16)
    own_slots = lax.all_to_all(
        expert_out.reshape(plane_count, slot_total, down_local.shape[1]),
        "rep",
        split_axis=0,
        concat_axis=2,
        tiled=True,
    )
    returned = route_slots(own_slots.reshape(1, expert_count, slot_cap, model_width))
    back_rows = returned.reshape(slot_total, model_width).astype(jnp.float32)
    mixed_rows = jnp.dot(mixing, back_rows, precision=lax.Precision.HIGHEST)
    return mixed_rows.astype(jnp.bfloat16)


def hidden_units(rows, gate_local, up_local):
    feature_dims = (((1,), (1,)), ((), ()))
    gate = lax.dot_general(rows, gate_local, feature_dims, preferred_element_type=jnp.float32)
    up = lax.dot_general(rows, up_local, feature_dims, preferred_element_type=jnp.float32)
    return (jax.nn.silu(gate) * up).astype(jnp.bfloat16)


def swap(block, axes, mask):
    size = lax.axis_size(axes)
    return lax.ppermute(block, axes, [(place, place ^ mask) for place in range(size)])


def turn(block, first):
    nodes, size = lax.axis_size("node"), lax.axis_size(("rep", "node"))
    mask_of = [2 if (place % 2 == 0) == first else nodes for place in range(size)]
    pairs = [(place, place ^ mask) for place, mask in enumerate(mask_of)]
    return lax.ppermute(block, ("rep", "node"), pairs)


def square(block):
    side = turn(block, True)
    other_side = turn(block, False)
    return [side, turn(side, False), other_side, block]


def wide(block):
    return block.astype(jnp.float32)


def narrow(block):
    return block.astype(jnp.bfloat16)


def pack_kernel(tokens_in, ids_in, weights_in, out_ref, ids_ref, weights_ref, sems, *, experts):
    row_count, width = tokens_in.shape
    tokens_copy = pltpu.make_async_copy(tokens_in, out_ref.at[:, pl.ds(0, width)], sems.at[0])
    ids_copy = pltpu.make_async_copy(ids_in, ids_ref, sems.at[1])
    weights_copy = pltpu.make_async_copy(weights_in, weights_ref, sems.at[2])
    tokens_copy.start()
    ids_copy.start()
    weights_copy.start()
    extra = out_ref.shape[1] - width
    expert = lax.broadcasted_iota(jnp.int32, (extra, row_count), 0) % experts
    share = jnp.zeros(expert.shape, jnp.float32)
    ids_copy.wait()
    weights_copy.wait()
    for k in range(ids_ref.shape[0]):
        share += jnp.where(ids_ref[k : k + 1, :] == expert, weights_ref[k : k + 1, :], 0.0)
    share = jnp.concatenate([share, jnp.zeros((extra, extra - row_count), jnp.float32)], axis=1)
    share = share.T[:row_count]
    piece = lax.broadcasted_iota(jnp.int32, share.shape, 1) // experts
    high = wide(narrow(share))
    middle = wide(narrow(share - high))
    low = share - high - middle
    coded = jnp.where(piece == 0, high, jnp.where(piece == 1, middle, low))
    out_ref[:, width:] = narrow(jnp.where(piece < 3, coded, 0.0))
    tokens_copy.wait()


def fetch_kernel(*refs):
    *parts, out_ref, sems = refs
    row, copies = 0, []
    for place, part in enumerate(parts):
        rows = part.shape[0]
        there = out_ref.at[pl.ds(row, rows), :]
        copies.append(pltpu.make_async_copy(part, there, sems.at[place]))
        copies[-1].start()
        row += rows
    for copy in copies:
        copy.wait()


def gate_up_kernel(*refs, experts, starts, row_count, chunks):
    rows, out_refs = refs[-1], refs[-1 - 2 * chunks : -1]
    block_refs, weight_refs = refs[: len(starts)], refs[len(starts) : len(starts) + 2]
    part_width, width = weight_refs[0].shape[0] // 2, weight_refs[0].shape[1]
    own = lax.axis_index("node") * lax.axis_size("local") + lax.axis_index("local")
    other = own + lax.axis_size("local") * (1 - 2 * (lax.axis_index("node") % 2))
    lanes = lax.broadcasted_iota(jnp.int32, (row_count, block_refs[0].shape[1] - width), 1)
    coded = [
        (lanes % experts == expert) & (lanes < 3 * experts) for expert in (own, other)
    ]
    each = len(starts) // chunks
    core = lax.axis_index("node") % 2
    for place, (block, start) in enumerate(zip(block_refs, starts)):
        there = slice(start, start + row_count)
        chunk, (side, inner) = place // each, divmod(place % each, each // 4)
        if side in (1, 2):
            side = jnp.where(core == 0, side, 3 - side)
        first = pl.multiple_of((side * (each // 4) + inner) * row_count, row_count)
        rows[pl.ds(first + chunk * each * row_count, row_count), :] = block[there, :width]
        pieces = wide(block[there, width:])
        share_ref = out_refs[chunks + chunk]
        for expert in range(2):
            share = jnp.sum(jnp.where(coded[expert], pieces, 0.0), axis=1, keepdims=True)
            share = jnp.broadcast_to(share, (row_count, share_ref.shape[2]))
            share_ref[expert, pl.ds(first, row_count), :] = share
    feature_dims = (((1,), (1,)), ((), ()))
    for side, weights in enumerate(weight_refs):
        both = lax.dot_general(
            weights[...], rows[...], feature_dims, preferred_element_type=jnp.float32
        )
        gate, up = both[:part_width], both[part_width:]
        hidden = narrow((gate * up / (1.0 + jnp.exp(-gate))).T)
        for chunk, hidden_ref in enumerate(out_refs[:chunks]):
            total = hidden_ref.shape[1]
            hidden_ref[side] = hidden[chunk * total : (chunk + 1) * total]


def down_kernel(own_ref, other_ref, share_ref, down_own, down_other, *refs, quarters):
    out_refs = refs[-len(quarters) :]
    plane = lax.axis_index("rep")
    width = down_own.shape[1]
    tile = math.gcd(width, 512)
    total = own_ref.shape[1]
    half, quarter = total // 2, total // 4
    hidden = []
    for side in range(2):
        own = own_ref[side]
        other = jnp.concatenate([other_ref[side, half:], other_ref[side, :half]], axis=0)
        first = jnp.where(plane == 0, own, other)
        second = jnp.where(plane == 0, other, own)
        hidden.append(jnp.concatenate([first, second], axis=1))
    for start in range(0, width, tile):
        here = slice(start, start + tile)
        term = 0.0
        for side, part in enumerate((down_own, down_other)):
            out = jnp.dot(hidden[side], part[:, here], preferred_element_type=jnp.float32)
            term += share_ref[side, :, :1] * wide(narrow(out))
        for out_ref, places in zip(out_refs, quarters):
            rows = [term[place * quarter : (place + 1) * quarter] for place in places]
            out_ref[:, here] = jnp.concatenate(rows, axis=0).astype(out_ref.dtype)


def run(kernel, operands, in_hbm, out_shape, scratch_shapes, flops, room=24, **sizes):
    held, fetched = pl.BlockSpec(memory_space=pltpu.VMEM), pl.BlockSpec(memory_space=pltpu.HBM)
    moved = sum(operand.size * operand.dtype.itemsize for operand in operands)
    return pl.pallas_call(
        functools.partial(kernel, **sizes),
        out_shape=out_shape,
        in_specs=[fetched if place in in_hbm else held for place in range(len(operands))],
        out_specs=jax.tree.map(lambda _: held, out_shape),
        scratch_shapes=scratch_shapes,
        compiler_params=pltpu.CompilerParams(vmem_limit_bytes=room * 1024 * 1024),
        cost_estimate=pl.CostEstimate(flops=flops, bytes_accessed=moved, transcendentals=0),
    )(*operands)


def pack(tokens, expert_ids, route_weights, experts):
    row_count, width = tokens.shape
    extra = -(-3 * experts // 128) * 128
    return run(
        pack_kernel,
        (tokens, expert_ids.T, route_weights.T),
        (0, 1, 2),
        jax.ShapeDtypeStruct((row_count, width + extra), jnp.bfloat16),
        [
            pltpu.VMEM(expert_ids.shape[::-1], jnp.int32),
            pltpu.VMEM(route_weights.shape[::-1], jnp.float32),
            pltpu.SemaphoreType.DMA((3,)),
        ],
        0,
        room=60,
        experts=experts,
    )


def fetch(arrays):
    rows = sum(array.shape[0] for array in arrays)
    return run(
        fetch_kernel,
        arrays,
        range(len(arrays)),
        jax.ShapeDtypeStruct((rows, arrays[0].shape[1]), arrays[0].dtype),
        [pltpu.SemaphoreType.DMA((len(arrays),))],
        0,
    )


def gate_up(parts, row_count, weights, experts):
    part_width, width = weights[0].shape[0] // 2, weights[0].shape[1]
    blocks, starts = zip(*(block for part in parts for block in part))
    total, chunks = len(blocks) * row_count, len(parts)
    outs = run(
        gate_up_kernel,
        (*blocks, *weights),
        (),
        [jax.ShapeDtypeStruct((2, total // chunks, part_width), jnp.bfloat16)] * chunks
        + [jax.ShapeDtypeStruct((2, total // chunks, 128), jnp.float32)] * chunks,
        [pltpu.VMEM((total, width), jnp.bfloat16)],
        8 * total * width * part_width,
        experts=experts,
        starts=starts,
        row_count=row_count,
        chunks=chunks,
    )
    return list(zip(outs[:chunks], outs[chunks:]))


def down(own, other, share, weights, quarters, after=()):
    total = own.shape[1]
    depth, width = weights[0].shape
    sizes = [(len(places) * total // 4, width) for places in quarters]
    return run(
        down_kernel,
        (own, other, share, *weights, *after),
        (),
        [jax.ShapeDtypeStruct(sizes[0], jnp.float32)]
        + [jax.ShapeDtypeStruct(size, jnp.bfloat16) for size in sizes[1:]],
        [],
        4 * total * depth * width,
        quarters=quarters,
    )


def by_rows(tokens, expert_ids, route_weights, gate_local, up_local, down_local):
    row_count = tokens.shape[0]
    experts = lax.axis_size("node") * lax.axis_size("local")
    places = lax.axis_size("local")
    plane = lax.axis_index("rep")
    together = lax.optimization_barrier

    packed = pack(tokens, expert_ids, route_weights, experts)
    line_3, line_1, square_0, gates = together(
        (
            swap(packed, "local", 3),
            swap(packed, "local", 1),
            square(packed),
            fetch((gate_local, up_local)),
        )
    )
    other_gates = swap(gates, "node", 1)
    block_13 = jnp.concatenate([line_1, line_3], axis=0)
    side_13, other_13, line_2 = turn(block_13, True), turn(block_13, False), swap(line_3, "local", 1)
    line_2, side_13, other_13, downs = together((line_2, side_13, other_13, fetch((down_local,))))
    square_13 = [side_13, turn(side_13, False), other_13, block_13]

    def hidden_of(*parts):
        order = (3, 0, 2, 1)
        blocks = [(square[side], row) for side in order for square, row in parts]
        return gate_up((blocks,), row_count, (gates, other_gates), experts)[0]

    def exchanged(hidden, share):
        return hidden, swap(hidden, "rep", 1), share

    hidden_b = hidden_of((square_13, 0), (square_13, row_count))
    side_2, other_2 = turn(line_2, True), turn(line_2, False)
    side_2, other_2, hidden_b = together((side_2, other_2, hidden_b))
    both_2, other_downs = together((turn(side_2, False), swap(downs, "node", 1)))
    square_2 = [side_2, both_2, other_2, line_2]
    weights = (downs, other_downs)
    hidden_a = hidden_of((square_0, 0), (square_2, 0))
    hidden_b, hidden_a = exchanged(*hidden_b), exchanged(*hidden_a)
    meeting = swap(hidden_a[2][0, :8], "node", 1)
    keep, send_y = down(*hidden_b, weights, ((0, 2), (1, 3)), (meeting,))
    back_y = swap(send_y, "node", 2)
    keep_a, send_y, send_x, send_across = down(*hidden_a, weights, ((0,), (1,), (2,), (3,)))
    across = swap(send_across, ("rep", "node"), lax.axis_size("node") | 2)
    along_x, along_y = swap(send_x, "rep", 1), swap(send_y, "node", 2)
    here, there = narrow(keep + wide(back_y)).reshape(2, 2 * row_count, -1)
    there = swap(there, ("rep", "local"), places | 1)
    here = swap(here, "local", 1)
    own = keep_a + wide(along_y) + wide(here)
    other = wide(along_x) + wide(across) + wide(there)
    total = jnp.stack([own, other]).reshape(2, 2, row_count, -1)
    own, other = narrow(total[:, 0] + wide(swap(narrow(total[:, 1]), "local", 2)))
    return jnp.where(
        plane == 0,
        jnp.concatenate([own, other], axis=1),
        jnp.concatenate([other, own], axis=1),
    )


def on_device(tokens, expert_ids, route_weights, gate_weight, up_weight, down_weight):
    row_count, top_count = expert_ids.shape
    expert_count = lax.axis_size("node") * lax.axis_size("local")
    slot_cap = min(row_count, max(2, 2 * row_count * top_count // expert_count))
    weights = (gate_weight[0], up_weight[0], down_weight[0])
    if slot_cap == row_count:
        return by_rows(tokens, expert_ids, route_weights, *weights)
    return by_slots(tokens, expert_ids, route_weights, *weights, slot_cap)


def solution(mesh):
    placed = (
        P(EVERY, None),
        P(EVERY, None),
        P(EVERY, None),
        P(PLANE, "rep", None),
        P(PLANE, "rep", None),
        P(PLANE, None, "rep"),
    )
    return jax.shard_map(
        on_device,
        mesh=mesh,
        in_specs=placed,
        out_specs=P(EVERY, None),
        check_vma=False,
    )
```

```python
import functools
import math

import jax
import jax.numpy as jnp
from jax import lax
from jax.experimental import pallas as pl
from jax.experimental.pallas import tpu as pltpu
from jax.sharding import PartitionSpec as P

PLANE = ("node", "local")
EVERY = ("rep", "node", "local")


def slot_table(expert_ids, expert_count, slot_cap):
    row_count, top_count = expert_ids.shape
    flat_ids = expert_ids.reshape(-1)
    hits = (flat_ids[:, None] == jnp.arange(expert_count, dtype=jnp.int32)[None, :]).astype(
        jnp.int32
    )
    before = jnp.cumsum(hits, axis=0) - hits
    rank_of = jnp.sum(before * hits, axis=1)
    return (flat_ids * slot_cap + rank_of).reshape(row_count, top_count)


def route_slots(blocks):
    return lax.all_to_all(blocks, PLANE, split_axis=1, concat_axis=1, tiled=True)


def by_slots(tokens, expert_ids, route_weights, gate_local, up_local, down_local, slot_cap):
    model_width = tokens.shape[1]
    plane_count = lax.axis_size("rep")
    expert_count = lax.axis_size("node") * lax.axis_size("local")
    slot_total = expert_count * slot_cap
    slot_of = slot_table(expert_ids, expert_count, slot_cap)
    slot_iota = jnp.arange(slot_total, dtype=jnp.int32)
    placed = jnp.any(slot_of[None, :, :] == slot_iota[:, None, None], axis=2).astype(jnp.bfloat16)
    outgoing = jnp.dot(placed, tokens, preferred_element_type=jnp.float32).astype(jnp.bfloat16)
    mixing = jnp.sum(
        jnp.where(slot_of[:, :, None] == slot_iota[None, None, :], route_weights[:, :, None], 0.0),
        axis=1,
    )
    arrived = route_slots(outgoing.reshape(1, expert_count, slot_cap, model_width))
    arrived = arrived.reshape(slot_total, model_width)
    shard_piece = lax.all_gather(arrived, "rep", axis=0, tiled=True)
    hidden_part = hidden_units(shard_piece, gate_local, up_local)
    expert_out = jnp.dot(
        lax.all_gather(hidden_part, "rep", axis=1, tiled=True),
        down_local,
        preferred_element_type=jnp.float32,
    ).astype(jnp.bfloat16)
    own_slots = lax.all_to_all(
        expert_out.reshape(plane_count, slot_total, down_local.shape[1]),
        "rep",
        split_axis=0,
        concat_axis=2,
        tiled=True,
    )
    returned = route_slots(own_slots.reshape(1, expert_count, slot_cap, model_width))
    back_rows = returned.reshape(slot_total, model_width).astype(jnp.float32)
    mixed_rows = jnp.dot(mixing, back_rows, precision=lax.Precision.HIGHEST)
    return mixed_rows.astype(jnp.bfloat16)


def hidden_units(rows, gate_local, up_local):
    feature_dims = (((1,), (1,)), ((), ()))
    gate = lax.dot_general(rows, gate_local, feature_dims, preferred_element_type=jnp.float32)
    up = lax.dot_general(rows, up_local, feature_dims, preferred_element_type=jnp.float32)
    return (jax.nn.silu(gate) * up).astype(jnp.bfloat16)


def swap(block, axes, mask):
    size = lax.axis_size(axes)
    return lax.ppermute(block, axes, [(place, place ^ mask) for place in range(size)])


def turn(block, first):
    nodes, size = lax.axis_size("node"), lax.axis_size(("rep", "node"))
    mask_of = [2 if (place % 2 == 0) == first else nodes for place in range(size)]
    pairs = [(place, place ^ mask) for place, mask in enumerate(mask_of)]
    return lax.ppermute(block, ("rep", "node"), pairs)


def square(block):
    side = turn(block, True)
    other_side = turn(block, False)
    return [side, turn(side, False), other_side, block]


def wide(block):
    return block.astype(jnp.float32)


def narrow(block):
    return block.astype(jnp.bfloat16)


def pack_kernel(tokens_in, ids_in, weights_in, out_ref, ids_ref, weights_ref, share_ref, sems, *, experts):
    row_count, width = tokens_in.shape
    ids_copy = pltpu.make_async_copy(ids_in, ids_ref, sems.at[0])
    weights_copy = pltpu.make_async_copy(weights_in, weights_ref, sems.at[1])
    tokens_copy = pltpu.make_async_copy(tokens_in, out_ref.at[:, pl.ds(0, width)], sems.at[2])
    ids_copy.start()
    weights_copy.start()
    tokens_copy.start()
    extra = share_ref.shape[1]
    expert = lax.broadcasted_iota(jnp.int32, (extra, row_count), 0) % experts
    share = jnp.zeros(expert.shape, jnp.float32)
    ids_copy.wait()
    weights_copy.wait()
    for k in range(ids_ref.shape[0]):
        share += jnp.where(ids_ref[k : k + 1, :] == expert, weights_ref[k : k + 1, :], 0.0)
    share = jnp.concatenate([share, jnp.zeros((extra, extra - row_count), jnp.float32)], axis=1)
    share = share.T[:row_count]
    piece = lax.broadcasted_iota(jnp.int32, share.shape, 1) // experts
    high = wide(narrow(share))
    middle = wide(narrow(share - high))
    low = share - high - middle
    coded = jnp.where(piece == 0, high, jnp.where(piece == 1, middle, low))
    share_ref[...] = narrow(jnp.where(piece < 3, coded, 0.0))
    share_copy = pltpu.make_async_copy(share_ref, out_ref.at[:, pl.ds(width, extra)], sems.at[3])
    share_copy.start()
    share_copy.wait()
    tokens_copy.wait()


def fetch_kernel(*refs):
    *parts, out_ref, sems = refs
    row, copies = 0, []
    for place, part in enumerate(parts):
        rows = part.shape[0]
        there = out_ref.at[pl.ds(row, rows), :]
        copies.append(pltpu.make_async_copy(part, there, sems.at[place]))
        copies[-1].start()
        row += rows
    for copy in copies:
        copy.wait()


def gate_up_kernel(*refs, experts, starts, row_count, chunks):
    rows, out_refs = refs[-1], refs[-1 - 2 * chunks : -1]
    block_refs, weight_refs = refs[: len(starts)], refs[len(starts) : len(starts) + 2]
    part_width, width = weight_refs[0].shape[0] // 2, weight_refs[0].shape[1]
    own = lax.axis_index("node") * lax.axis_size("local") + lax.axis_index("local")
    other = own + lax.axis_size("local") * (1 - 2 * (lax.axis_index("node") % 2))
    lanes = lax.broadcasted_iota(jnp.int32, (row_count, block_refs[0].shape[1] - width), 1)
    coded = [
        (lanes % experts == expert) & (lanes < 3 * experts) for expert in (own, other)
    ]
    each = len(starts) // chunks
    core = lax.axis_index("node") % 2
    for place, (block, start) in enumerate(zip(block_refs, starts)):
        there = slice(start, start + row_count)
        chunk, (side, inner) = place // each, divmod(place % each, each // 4)
        if side in (1, 2):
            side = jnp.where(core == 0, side, 3 - side)
        first = pl.multiple_of((side * (each // 4) + inner) * row_count, row_count)
        rows[pl.ds(first + chunk * each * row_count, row_count), :] = block[there, :width]
        pieces = wide(block[there, width:])
        share_ref = out_refs[chunks + chunk]
        for expert in range(2):
            share = jnp.sum(jnp.where(coded[expert], pieces, 0.0), axis=1, keepdims=True)
            share = jnp.broadcast_to(share, (row_count, share_ref.shape[2]))
            share_ref[expert, pl.ds(first, row_count), :] = share
    feature_dims = (((1,), (1,)), ((), ()))
    for side, weights in enumerate(weight_refs):
        both = lax.dot_general(
            weights[...], rows[...], feature_dims, preferred_element_type=jnp.float32
        )
        gate, up = both[:part_width], both[part_width:]
        hidden = narrow((gate * up / (1.0 + jnp.exp(-gate))).T)
        for chunk, hidden_ref in enumerate(out_refs[:chunks]):
            total = hidden_ref.shape[1]
            hidden_ref[side] = hidden[chunk * total : (chunk + 1) * total]


def down_kernel(own_ref, other_ref, share_ref, down_own, down_other, *refs, quarters):
    out_refs = refs[-len(quarters) :]
    plane = lax.axis_index("rep")
    width = down_own.shape[1]
    tile = math.gcd(width, 512)
    total = own_ref.shape[1]
    half, quarter = total // 2, total // 4
    hidden = []
    for side in range(2):
        own = own_ref[side]
        other = jnp.concatenate([other_ref[side, half:], other_ref[side, :half]], axis=0)
        first = jnp.where(plane == 0, own, other)
        second = jnp.where(plane == 0, other, own)
        hidden.append(jnp.concatenate([first, second], axis=1))
    for start in range(0, width, tile):
        here = slice(start, start + tile)
        term = 0.0
        for side, part in enumerate((down_own, down_other)):
            out = jnp.dot(hidden[side], part[:, here], preferred_element_type=jnp.float32)
            term += share_ref[side, :, :1] * wide(narrow(out))
        for out_ref, places in zip(out_refs, quarters):
            rows = [term[place * quarter : (place + 1) * quarter] for place in places]
            out_ref[:, here] = jnp.concatenate(rows, axis=0).astype(out_ref.dtype)


def run(kernel, operands, in_hbm, out_shape, scratch_shapes, flops, room=24, out=pltpu.VMEM, **sizes):
    held, fetched = pl.BlockSpec(memory_space=pltpu.VMEM), pl.BlockSpec(memory_space=pltpu.HBM)
    moved = sum(operand.size * operand.dtype.itemsize for operand in operands)
    return pl.pallas_call(
        functools.partial(kernel, **sizes),
        out_shape=out_shape,
        in_specs=[fetched if place in in_hbm else held for place in range(len(operands))],
        out_specs=jax.tree.map(lambda _: pl.BlockSpec(memory_space=out), out_shape),
        scratch_shapes=scratch_shapes,
        compiler_params=pltpu.CompilerParams(vmem_limit_bytes=room * 1024 * 1024),
        cost_estimate=pl.CostEstimate(flops=flops, bytes_accessed=moved, transcendentals=0),
    )(*operands)


def pack(tokens, expert_ids, route_weights, experts):
    row_count, width = tokens.shape
    extra = -(-3 * experts // 128) * 128
    return run(
        pack_kernel,
        (tokens, expert_ids.T, route_weights.T),
        (0, 1, 2),
        jax.ShapeDtypeStruct((row_count, width + extra), jnp.bfloat16),
        [
            pltpu.VMEM(expert_ids.shape[::-1], jnp.int32),
            pltpu.VMEM(route_weights.shape[::-1], jnp.float32),
            pltpu.VMEM((row_count, extra), jnp.bfloat16),
            pltpu.SemaphoreType.DMA((4,)),
        ],
        0,
        room=60,
        out=pltpu.HBM,
        experts=experts,
    )


def fetch(arrays):
    rows = sum(array.shape[0] for array in arrays)
    return run(
        fetch_kernel,
        arrays,
        range(len(arrays)),
        jax.ShapeDtypeStruct((rows, arrays[0].shape[1]), arrays[0].dtype),
        [pltpu.SemaphoreType.DMA((len(arrays),))],
        0,
    )


def gate_up(parts, row_count, weights, experts):
    part_width, width = weights[0].shape[0] // 2, weights[0].shape[1]
    blocks, starts = zip(*(block for part in parts for block in part))
    total, chunks = len(blocks) * row_count, len(parts)
    outs = run(
        gate_up_kernel,
        (*blocks, *weights),
        (),
        [jax.ShapeDtypeStruct((2, total // chunks, part_width), jnp.bfloat16)] * chunks
        + [jax.ShapeDtypeStruct((2, total // chunks, 128), jnp.float32)] * chunks,
        [pltpu.VMEM((total, width), jnp.bfloat16)],
        8 * total * width * part_width,
        experts=experts,
        starts=starts,
        row_count=row_count,
        chunks=chunks,
    )
    return list(zip(outs[:chunks], outs[chunks:]))


def down(own, other, share, weights, quarters, after=()):
    total = own.shape[1]
    depth, width = weights[0].shape
    sizes = [(len(places) * total // 4, width) for places in quarters]
    return run(
        down_kernel,
        (own, other, share, *weights, *after),
        (),
        [jax.ShapeDtypeStruct(sizes[0], jnp.float32)]
        + [jax.ShapeDtypeStruct(size, jnp.bfloat16) for size in sizes[1:]],
        [],
        4 * total * depth * width,
        quarters=quarters,
    )


def by_rows(tokens, expert_ids, route_weights, gate_local, up_local, down_local):
    row_count = tokens.shape[0]
    experts = lax.axis_size("node") * lax.axis_size("local")
    places = lax.axis_size("local")
    plane = lax.axis_index("rep")
    together = lax.optimization_barrier

    packed = pack(tokens, expert_ids, route_weights, experts)
    line_3, line_1, square_0, gates = together(
        (
            swap(packed, "local", 3),
            swap(packed, "local", 1),
            square(packed),
            fetch((gate_local, up_local)),
        )
    )
    other_gates = swap(gates, "node", 1)
    block_13 = jnp.concatenate([line_1, line_3], axis=0)
    side_13, other_13, line_2 = turn(block_13, True), turn(block_13, False), swap(line_3, "local", 1)
    line_2, side_13, other_13, downs = together((line_2, side_13, other_13, fetch((down_local,))))
    square_13 = [side_13, turn(side_13, False), other_13, block_13]

    def hidden_of(*parts):
        order = (3, 0, 2, 1)
        blocks = [(square[side], row) for side in order for square, row in parts]
        return gate_up((blocks,), row_count, (gates, other_gates), experts)[0]

    def exchanged(hidden, share):
        return hidden, swap(hidden, "rep", 1), share

    hidden_b = hidden_of((square_13, 0), (square_13, row_count))
    hidden_b, square_2, other_downs = together(
        (hidden_b, square(line_2), swap(downs, "node", 1))
    )
    weights = (downs, other_downs)
    hidden_a = hidden_of((square_0, 0), (square_2, 0))
    hidden_b, hidden_a = exchanged(*hidden_b), exchanged(*hidden_a)
    meeting = swap(hidden_a[2][0, :8], "node", 1)
    keep, send_y = down(*hidden_b, weights, ((0, 2), (1, 3)), (meeting,))
    back_y = swap(send_y, "node", 2)
    keep_a, send_y, send_x, send_across = down(*hidden_a, weights, ((0,), (1,), (2,), (3,)))
    across = swap(send_across, ("rep", "node"), lax.axis_size("node") | 2)
    along_x, along_y = swap(send_x, "rep", 1), swap(send_y, "node", 2)
    here, there = narrow(keep + wide(back_y)).reshape(2, 2 * row_count, -1)
    there = swap(there, ("rep", "local"), places | 1)
    here = swap(here, "local", 1)
    own = keep_a + wide(along_y) + wide(here)
    other = wide(along_x) + wide(across) + wide(there)
    total = jnp.stack([own, other]).reshape(2, 2, row_count, -1)
    own, other = narrow(total[:, 0] + wide(swap(narrow(total[:, 1]), "local", 2)))
    return jnp.where(
        plane == 0,
        jnp.concatenate([own, other], axis=1),
        jnp.concatenate([other, own], axis=1),
    )


def on_device(tokens, expert_ids, route_weights, gate_weight, up_weight, down_weight):
    row_count, top_count = expert_ids.shape
    expert_count = lax.axis_size("node") * lax.axis_size("local")
    slot_cap = min(row_count, max(2, 2 * row_count * top_count // expert_count))
    weights = (gate_weight[0], up_weight[0], down_weight[0])
    if slot_cap == row_count:
        return by_rows(tokens, expert_ids, route_weights, *weights)
    return by_slots(tokens, expert_ids, route_weights, *weights, slot_cap)


def solution(mesh):
    placed = (
        P(EVERY, None),
        P(EVERY, None),
        P(EVERY, None),
        P(PLANE, "rep", None),
        P(PLANE, "rep", None),
        P(PLANE, None, "rep"),
    )
    return jax.shard_map(
        on_device,
        mesh=mesh,
        in_specs=placed,
        out_specs=P(EVERY, None),
        check_vma=False,
    )
```

```python
import functools
import math

import jax
import jax.numpy as jnp
from jax import lax
from jax.experimental import pallas as pl
from jax.experimental.pallas import tpu as pltpu
from jax.sharding import PartitionSpec as P

PLANE = ("node", "local")
EVERY = ("rep", "node", "local")


def slot_table(expert_ids, expert_count, slot_cap):
    row_count, top_count = expert_ids.shape
    flat_ids = expert_ids.reshape(-1)
    hits = (flat_ids[:, None] == jnp.arange(expert_count, dtype=jnp.int32)[None, :]).astype(
        jnp.int32
    )
    before = jnp.cumsum(hits, axis=0) - hits
    rank_of = jnp.sum(before * hits, axis=1)
    return (flat_ids * slot_cap + rank_of).reshape(row_count, top_count)


def route_slots(blocks):
    return lax.all_to_all(blocks, PLANE, split_axis=1, concat_axis=1, tiled=True)


def by_slots(tokens, expert_ids, route_weights, gate_local, up_local, down_local, slot_cap):
    model_width = tokens.shape[1]
    plane_count = lax.axis_size("rep")
    expert_count = lax.axis_size("node") * lax.axis_size("local")
    slot_total = expert_count * slot_cap
    slot_of = slot_table(expert_ids, expert_count, slot_cap)
    slot_iota = jnp.arange(slot_total, dtype=jnp.int32)
    placed = jnp.any(slot_of[None, :, :] == slot_iota[:, None, None], axis=2).astype(jnp.bfloat16)
    outgoing = jnp.dot(placed, tokens, preferred_element_type=jnp.float32).astype(jnp.bfloat16)
    mixing = jnp.sum(
        jnp.where(slot_of[:, :, None] == slot_iota[None, None, :], route_weights[:, :, None], 0.0),
        axis=1,
    )
    arrived = route_slots(outgoing.reshape(1, expert_count, slot_cap, model_width))
    arrived = arrived.reshape(slot_total, model_width)
    shard_piece = lax.all_gather(arrived, "rep", axis=0, tiled=True)
    hidden_part = hidden_units(shard_piece, gate_local, up_local)
    expert_out = jnp.dot(
        lax.all_gather(hidden_part, "rep", axis=1, tiled=True),
        down_local,
        preferred_element_type=jnp.float32,
    ).astype(jnp.bfloat16)
    own_slots = lax.all_to_all(
        expert_out.reshape(plane_count, slot_total, down_local.shape[1]),
        "rep",
        split_axis=0,
        concat_axis=2,
        tiled=True,
    )
    returned = route_slots(own_slots.reshape(1, expert_count, slot_cap, model_width))
    back_rows = returned.reshape(slot_total, model_width).astype(jnp.float32)
    mixed_rows = jnp.dot(mixing, back_rows, precision=lax.Precision.HIGHEST)
    return mixed_rows.astype(jnp.bfloat16)


def hidden_units(rows, gate_local, up_local):
    feature_dims = (((1,), (1,)), ((), ()))
    gate = lax.dot_general(rows, gate_local, feature_dims, preferred_element_type=jnp.float32)
    up = lax.dot_general(rows, up_local, feature_dims, preferred_element_type=jnp.float32)
    return (jax.nn.silu(gate) * up).astype(jnp.bfloat16)


def swap(block, axes, mask):
    size = lax.axis_size(axes)
    return lax.ppermute(block, axes, [(place, place ^ mask) for place in range(size)])


def turn(block, first):
    nodes, size = lax.axis_size("node"), lax.axis_size(("rep", "node"))
    mask_of = [2 if (place % 2 == 0) == first else nodes for place in range(size)]
    pairs = [(place, place ^ mask) for place, mask in enumerate(mask_of)]
    return lax.ppermute(block, ("rep", "node"), pairs)


def square(block):
    side = turn(block, True)
    other_side = turn(block, False)
    return [side, turn(side, False), other_side, block]


def wide(block):
    return block.astype(jnp.float32)


def narrow(block):
    return block.astype(jnp.bfloat16)


def pack_kernel(tokens_in, ids_in, weights_in, out_ref, ids_ref, weights_ref, sems, *, experts):
    row_count, width = tokens_in.shape
    tokens_copy = pltpu.make_async_copy(tokens_in, out_ref.at[:, pl.ds(0, width)], sems.at[0])
    ids_copy = pltpu.make_async_copy(ids_in, ids_ref, sems.at[1])
    weights_copy = pltpu.make_async_copy(weights_in, weights_ref, sems.at[2])
    tokens_copy.start()
    ids_copy.start()
    weights_copy.start()
    extra = out_ref.shape[1] - width
    expert = lax.broadcasted_iota(jnp.int32, (extra, row_count), 0) % experts
    share = jnp.zeros(expert.shape, jnp.float32)
    ids_copy.wait()
    weights_copy.wait()
    for k in range(ids_ref.shape[0]):
        share += jnp.where(ids_ref[k : k + 1, :] == expert, weights_ref[k : k + 1, :], 0.0)
    share = jnp.concatenate([share, jnp.zeros((extra, extra - row_count), jnp.float32)], axis=1)
    share = share.T[:row_count]
    piece = lax.broadcasted_iota(jnp.int32, share.shape, 1) // experts
    high = wide(narrow(share))
    middle = wide(narrow(share - high))
    low = share - high - middle
    coded = jnp.where(piece == 0, high, jnp.where(piece == 1, middle, low))
    out_ref[:, width:] = narrow(jnp.where(piece < 3, coded, 0.0))
    tokens_copy.wait()


def fetch_kernel(*refs):
    *parts, out_ref, sems = refs
    row, copies = 0, []
    for place, part in enumerate(parts):
        rows = part.shape[0]
        there = out_ref.at[pl.ds(row, rows), :]
        copies.append(pltpu.make_async_copy(part, there, sems.at[place]))
        copies[-1].start()
        row += rows
    for copy in copies:
        copy.wait()


def gate_up_kernel(*refs, experts, starts, row_count, chunks):
    rows, out_refs = refs[-1], refs[-1 - 2 * chunks : -1]
    block_refs, weight_refs = refs[: len(starts)], refs[len(starts) : len(starts) + 2]
    part_width, width = weight_refs[0].shape[0] // 2, weight_refs[0].shape[1]
    own = lax.axis_index("node") * lax.axis_size("local") + lax.axis_index("local")
    other = own + lax.axis_size("local") * (1 - 2 * (lax.axis_index("node") % 2))
    lanes = lax.broadcasted_iota(jnp.int32, (row_count, block_refs[0].shape[1] - width), 1)
    coded = [
        (lanes % experts == expert) & (lanes < 3 * experts) for expert in (own, other)
    ]
    each = len(starts) // chunks
    core = lax.axis_index("node") % 2
    for place, (block, start) in enumerate(zip(block_refs, starts)):
        there = slice(start, start + row_count)
        chunk, (side, inner) = place // each, divmod(place % each, each // 4)
        if side in (1, 2):
            side = jnp.where(core == 0, side, 3 - side)
        first = pl.multiple_of((side * (each // 4) + inner) * row_count, row_count)
        rows[pl.ds(first + chunk * each * row_count, row_count), :] = block[there, :width]
        pieces = wide(block[there, width:])
        share_ref = out_refs[chunks + chunk]
        for expert in range(2):
            share = jnp.sum(jnp.where(coded[expert], pieces, 0.0), axis=1, keepdims=True)
            share = jnp.broadcast_to(share, (row_count, share_ref.shape[2]))
            share_ref[expert, pl.ds(first, row_count), :] = share
    feature_dims = (((1,), (1,)), ((), ()))
    for side, weights in enumerate(weight_refs):
        both = lax.dot_general(
            weights[...], rows[...], feature_dims, preferred_element_type=jnp.float32
        )
        gate, up = both[:part_width], both[part_width:]
        hidden = narrow((gate * up / (1.0 + jnp.exp(-gate))).T)
        for chunk, hidden_ref in enumerate(out_refs[:chunks]):
            total = hidden_ref.shape[1]
            hidden_ref[side] = hidden[chunk * total : (chunk + 1) * total]


def down_kernel(own_ref, other_ref, share_ref, down_own, down_other, *out_refs, quarters):
    plane = lax.axis_index("rep")
    width = down_own.shape[1]
    tile = math.gcd(width, 512)
    total = own_ref.shape[1]
    half, quarter = total // 2, total // 4
    hidden = []
    for side in range(2):
        own = own_ref[side]
        other = jnp.concatenate([other_ref[side, half:], other_ref[side, :half]], axis=0)
        first = jnp.where(plane == 0, own, other)
        second = jnp.where(plane == 0, other, own)
        hidden.append(jnp.concatenate([first, second], axis=1))
    for start in range(0, width, tile):
        here = slice(start, start + tile)
        term = 0.0
        for side, part in enumerate((down_own, down_other)):
            out = jnp.dot(hidden[side], part[:, here], preferred_element_type=jnp.float32)
            term += share_ref[side, :, :1] * wide(narrow(out))
        for out_ref, places in zip(out_refs, quarters):
            rows = [term[place * quarter : (place + 1) * quarter] for place in places]
            out_ref[:, here] = jnp.concatenate(rows, axis=0).astype(out_ref.dtype)


def run(kernel, operands, in_hbm, out_shape, scratch_shapes, flops, room=24, **sizes):
    held, fetched = pl.BlockSpec(memory_space=pltpu.VMEM), pl.BlockSpec(memory_space=pltpu.HBM)
    moved = sum(operand.size * operand.dtype.itemsize for operand in operands)
    return pl.pallas_call(
        functools.partial(kernel, **sizes),
        out_shape=out_shape,
        in_specs=[fetched if place in in_hbm else held for place in range(len(operands))],
        out_specs=jax.tree.map(lambda _: held, out_shape),
        scratch_shapes=scratch_shapes,
        compiler_params=pltpu.CompilerParams(vmem_limit_bytes=room * 1024 * 1024),
        cost_estimate=pl.CostEstimate(flops=flops, bytes_accessed=moved, transcendentals=0),
    )(*operands)


def pack(tokens, expert_ids, route_weights, experts):
    row_count, width = tokens.shape
    extra = -(-3 * experts // 128) * 128
    return run(
        pack_kernel,
        (tokens, expert_ids.T, route_weights.T),
        (0, 1, 2),
        jax.ShapeDtypeStruct((row_count, width + extra), jnp.bfloat16),
        [
            pltpu.VMEM(expert_ids.shape[::-1], jnp.int32),
            pltpu.VMEM(route_weights.shape[::-1], jnp.float32),
            pltpu.SemaphoreType.DMA((3,)),
        ],
        0,
        room=60,
        experts=experts,
    )


def fetch(arrays):
    rows = sum(array.shape[0] for array in arrays)
    return run(
        fetch_kernel,
        arrays,
        range(len(arrays)),
        jax.ShapeDtypeStruct((rows, arrays[0].shape[1]), arrays[0].dtype),
        [pltpu.SemaphoreType.DMA((len(arrays),))],
        0,
    )


def gate_up(parts, row_count, weights, experts):
    part_width, width = weights[0].shape[0] // 2, weights[0].shape[1]
    blocks, starts = zip(*(block for part in parts for block in part))
    total, chunks = len(blocks) * row_count, len(parts)
    outs = run(
        gate_up_kernel,
        (*blocks, *weights),
        (),
        [jax.ShapeDtypeStruct((2, total // chunks, part_width), jnp.bfloat16)] * chunks
        + [jax.ShapeDtypeStruct((2, total // chunks, 128), jnp.float32)] * chunks,
        [pltpu.VMEM((total, width), jnp.bfloat16)],
        8 * total * width * part_width,
        experts=experts,
        starts=starts,
        row_count=row_count,
        chunks=chunks,
    )
    return list(zip(outs[:chunks], outs[chunks:]))


def down(own, other, share, weights, quarters):
    total = own.shape[1]
    depth, width = weights[0].shape
    sizes = [(len(places) * total // 4, width) for places in quarters]
    return run(
        down_kernel,
        (own, other, share, *weights),
        (),
        [jax.ShapeDtypeStruct(sizes[0], jnp.float32)]
        + [jax.ShapeDtypeStruct(size, jnp.bfloat16) for size in sizes[1:]],
        [],
        4 * total * depth * width,
        quarters=quarters,
    )


def by_rows(tokens, expert_ids, route_weights, gate_local, up_local, down_local):
    row_count = tokens.shape[0]
    experts = lax.axis_size("node") * lax.axis_size("local")
    places = lax.axis_size("local")
    plane = lax.axis_index("rep")
    together = lax.optimization_barrier

    packed = pack(tokens, expert_ids, route_weights, experts)
    line_3, line_1, square_0, gates = together(
        (
            swap(packed, "local", 3),
            swap(packed, "local", 1),
            square(packed),
            fetch((gate_local, up_local)),
        )
    )
    other_gates = swap(gates, "node", 1)
    block_13 = jnp.concatenate([line_1, line_3], axis=0)
    side_13, other_13, line_2 = turn(block_13, True), turn(block_13, False), swap(line_3, "local", 1)
    line_2, side_13, other_13, downs = together((line_2, side_13, other_13, fetch((down_local,))))
    square_13 = [side_13, turn(side_13, False), other_13, block_13]

    def hidden_of(*parts):
        order = (3, 0, 2, 1)
        blocks = [(square[side], row) for side in order for square, row in parts]
        return gate_up((blocks,), row_count, (gates, other_gates), experts)[0]

    def exchanged(hidden, share):
        return hidden, swap(hidden, "rep", 1), share

    hidden_b = hidden_of((square_13, 0), (square_13, row_count))
    hidden_b, square_2, other_downs = together(
        (hidden_b, square(line_2), swap(downs, "node", 1))
    )
    weights = (downs, other_downs)
    hidden_a = hidden_of((square_0, 0), (square_2, 0))
    hidden_b, hidden_a = exchanged(*hidden_b), exchanged(*hidden_a)
    keep, send_y = down(*hidden_b, weights, ((0, 2), (1, 3)))
    back_y = swap(send_y, "node", 2)
    keep_a, send_y, send_x, send_across = down(*hidden_a, weights, ((0,), (1,), (2,), (3,)))
    across = swap(send_across, ("rep", "node"), lax.axis_size("node") | 2)
    along_x, along_y = swap(send_x, "rep", 1), swap(send_y, "node", 2)
    here, there = narrow(keep + wide(back_y)).reshape(2, 2 * row_count, -1)
    there = swap(there, ("rep", "local"), places | 1)
    here = swap(here, "local", 1)
    own = keep_a + wide(along_y) + wide(here)
    other = wide(along_x) + wide(across) + wide(there)
    total = jnp.stack([own, other]).reshape(2, 2, row_count, -1)
    own, other = narrow(total[:, 0] + wide(swap(narrow(total[:, 1]), "local", 2)))
    return jnp.where(
        plane == 0,
        jnp.concatenate([own, other], axis=1),
        jnp.concatenate([other, own], axis=1),
    )


def on_device(tokens, expert_ids, route_weights, gate_weight, up_weight, down_weight):
    row_count, top_count = expert_ids.shape
    expert_count = lax.axis_size("node") * lax.axis_size("local")
    slot_cap = min(row_count, max(2, 2 * row_count * top_count // expert_count))
    weights = (gate_weight[0], up_weight[0], down_weight[0])
    if slot_cap == row_count:
        return by_rows(tokens, expert_ids, route_weights, *weights)
    return by_slots(tokens, expert_ids, route_weights, *weights, slot_cap)


def solution(mesh):
    placed = (
        P(EVERY, None),
        P(EVERY, None),
        P(EVERY, None),
        P(PLANE, "rep", None),
        P(PLANE, "rep", None),
        P(PLANE, None, "rep"),
    )
    return jax.shard_map(
        on_device,
        mesh=mesh,
        in_specs=placed,
        out_specs=P(EVERY, None),
        check_vma=False,
    )
```

```python
import functools
import math

import jax
import jax.numpy as jnp
from jax import lax
from jax.experimental import pallas as pl
from jax.experimental.pallas import tpu as pltpu
from jax.sharding import PartitionSpec as P

PLANE = ("node", "local")
EVERY = ("rep", "node", "local")


def slot_table(expert_ids, expert_count, slot_cap):
    row_count, top_count = expert_ids.shape
    flat_ids = expert_ids.reshape(-1)
    hits = (flat_ids[:, None] == jnp.arange(expert_count, dtype=jnp.int32)[None, :]).astype(
        jnp.int32
    )
    before = jnp.cumsum(hits, axis=0) - hits
    rank_of = jnp.sum(before * hits, axis=1)
    return (flat_ids * slot_cap + rank_of).reshape(row_count, top_count)


def route_slots(blocks):
    return lax.all_to_all(blocks, PLANE, split_axis=1, concat_axis=1, tiled=True)


def by_slots(tokens, expert_ids, route_weights, gate_local, up_local, down_local, slot_cap):
    model_width = tokens.shape[1]
    plane_count = lax.axis_size("rep")
    expert_count = lax.axis_size("node") * lax.axis_size("local")
    slot_total = expert_count * slot_cap
    slot_of = slot_table(expert_ids, expert_count, slot_cap)
    slot_iota = jnp.arange(slot_total, dtype=jnp.int32)
    placed = jnp.any(slot_of[None, :, :] == slot_iota[:, None, None], axis=2).astype(jnp.bfloat16)
    outgoing = jnp.dot(placed, tokens, preferred_element_type=jnp.float32).astype(jnp.bfloat16)
    mixing = jnp.sum(
        jnp.where(slot_of[:, :, None] == slot_iota[None, None, :], route_weights[:, :, None], 0.0),
        axis=1,
    )
    arrived = route_slots(outgoing.reshape(1, expert_count, slot_cap, model_width))
    arrived = arrived.reshape(slot_total, model_width)
    shard_piece = lax.all_gather(arrived, "rep", axis=0, tiled=True)
    hidden_part = hidden_units(shard_piece, gate_local, up_local)
    expert_out = jnp.dot(
        lax.all_gather(hidden_part, "rep", axis=1, tiled=True),
        down_local,
        preferred_element_type=jnp.float32,
    ).astype(jnp.bfloat16)
    own_slots = lax.all_to_all(
        expert_out.reshape(plane_count, slot_total, down_local.shape[1]),
        "rep",
        split_axis=0,
        concat_axis=2,
        tiled=True,
    )
    returned = route_slots(own_slots.reshape(1, expert_count, slot_cap, model_width))
    back_rows = returned.reshape(slot_total, model_width).astype(jnp.float32)
    mixed_rows = jnp.dot(mixing, back_rows, precision=lax.Precision.HIGHEST)
    return mixed_rows.astype(jnp.bfloat16)


def hidden_units(rows, gate_local, up_local):
    feature_dims = (((1,), (1,)), ((), ()))
    gate = lax.dot_general(rows, gate_local, feature_dims, preferred_element_type=jnp.float32)
    up = lax.dot_general(rows, up_local, feature_dims, preferred_element_type=jnp.float32)
    return (jax.nn.silu(gate) * up).astype(jnp.bfloat16)


def swap(block, axes, mask):
    size = lax.axis_size(axes)
    return lax.ppermute(block, axes, [(place, place ^ mask) for place in range(size)])


def turn(block, first):
    nodes, size = lax.axis_size("node"), lax.axis_size(("rep", "node"))
    mask_of = [2 if (place % 2 == 0) == first else nodes for place in range(size)]
    pairs = [(place, place ^ mask) for place, mask in enumerate(mask_of)]
    return lax.ppermute(block, ("rep", "node"), pairs)


def square(block):
    side = turn(block, True)
    other_side = turn(block, False)
    return [side, turn(side, False), other_side, block]


def wide(block):
    return block.astype(jnp.float32)


def narrow(block):
    return block.astype(jnp.bfloat16)


def pack_kernel(tokens_in, ids_in, weights_in, out_ref, ids_ref, weights_ref, sems, *, experts):
    row_count, width = tokens_in.shape
    tokens_copy = pltpu.make_async_copy(tokens_in, out_ref.at[:, pl.ds(0, width)], sems.at[0])
    ids_copy = pltpu.make_async_copy(ids_in, ids_ref, sems.at[1])
    weights_copy = pltpu.make_async_copy(weights_in, weights_ref, sems.at[2])
    tokens_copy.start()
    ids_copy.start()
    weights_copy.start()
    extra = out_ref.shape[1] - width
    expert = lax.broadcasted_iota(jnp.int32, (extra, row_count), 0) % experts
    share = jnp.zeros(expert.shape, jnp.float32)
    ids_copy.wait()
    weights_copy.wait()
    for k in range(ids_ref.shape[0]):
        share += jnp.where(ids_ref[k : k + 1, :] == expert, weights_ref[k : k + 1, :], 0.0)
    share = jnp.concatenate([share, jnp.zeros((extra, extra - row_count), jnp.float32)], axis=1)
    share = share.T[:row_count]
    piece = lax.broadcasted_iota(jnp.int32, share.shape, 1) // experts
    high = wide(narrow(share))
    middle = wide(narrow(share - high))
    low = share - high - middle
    coded = jnp.where(piece == 0, high, jnp.where(piece == 1, middle, low))
    out_ref[:, width:] = narrow(jnp.where(piece < 3, coded, 0.0))
    tokens_copy.wait()


def fetch_kernel(*refs):
    *parts, out_ref, sems = refs
    row, copies = 0, []
    for place, part in enumerate(parts):
        rows = part.shape[0]
        there = out_ref.at[pl.ds(row, rows), :]
        copies.append(pltpu.make_async_copy(part, there, sems.at[place]))
        copies[-1].start()
        row += rows
    for copy in copies:
        copy.wait()


def gate_up_kernel(*refs, experts, starts, row_count, chunks):
    rows, out_refs = refs[-1], refs[-1 - 2 * chunks : -1]
    block_refs, weight_refs = refs[: len(starts)], refs[len(starts) : len(starts) + 2]
    part_width, width = weight_refs[0].shape[0] // 2, weight_refs[0].shape[1]
    own = lax.axis_index("node") * lax.axis_size("local") + lax.axis_index("local")
    other = own + lax.axis_size("local") * (1 - 2 * (lax.axis_index("node") % 2))
    lanes = lax.broadcasted_iota(jnp.int32, (row_count, block_refs[0].shape[1] - width), 1)
    coded = [
        (lanes % experts == expert) & (lanes < 3 * experts) for expert in (own, other)
    ]
    each = len(starts) // chunks
    core = lax.axis_index("node") % 2
    for place, (block, start) in enumerate(zip(block_refs, starts)):
        there = slice(start, start + row_count)
        chunk, (side, inner) = place // each, divmod(place % each, each // 4)
        if side in (1, 2):
            side = jnp.where(core == 0, side, 3 - side)
        first = pl.multiple_of((side * (each // 4) + inner) * row_count, row_count)
        rows[pl.ds(first + chunk * each * row_count, row_count), :] = block[there, :width]
        pieces = wide(block[there, width:])
        share_ref = out_refs[chunks + chunk]
        for expert in range(2):
            share = jnp.sum(jnp.where(coded[expert], pieces, 0.0), axis=1, keepdims=True)
            share = jnp.broadcast_to(share, (row_count, share_ref.shape[2]))
            share_ref[expert, pl.ds(first, row_count), :] = share
    feature_dims = (((1,), (1,)), ((), ()))
    for side, weights in enumerate(weight_refs):
        both = lax.dot_general(
            weights[...], rows[...], feature_dims, preferred_element_type=jnp.float32
        )
        gate, up = both[:part_width], both[part_width:]
        hidden = narrow((gate * up / (1.0 + jnp.exp(-gate))).T)
        for chunk, hidden_ref in enumerate(out_refs[:chunks]):
            total = hidden_ref.shape[1]
            hidden_ref[side] = hidden[chunk * total : (chunk + 1) * total]


def down_kernel(own_ref, other_ref, share_ref, down_own, down_other, *out_refs, quarters):
    plane = lax.axis_index("rep")
    width = down_own.shape[1]
    tile = math.gcd(width, 512)
    total = own_ref.shape[1]
    half, quarter = total // 2, total // 4
    hidden = []
    for side in range(2):
        own = own_ref[side]
        other = jnp.concatenate([other_ref[side, half:], other_ref[side, :half]], axis=0)
        first = jnp.where(plane == 0, own, other)
        second = jnp.where(plane == 0, other, own)
        hidden.append(jnp.concatenate([first, second], axis=1))
    for start in range(0, width, tile):
        here = slice(start, start + tile)
        term = 0.0
        for side, part in enumerate((down_own, down_other)):
            out = jnp.dot(hidden[side], part[:, here], preferred_element_type=jnp.float32)
            term += share_ref[side, :, :1] * wide(narrow(out))
        for out_ref, places in zip(out_refs, quarters):
            rows = [term[place * quarter : (place + 1) * quarter] for place in places]
            out_ref[:, here] = jnp.concatenate(rows, axis=0).astype(out_ref.dtype)


def run(kernel, operands, in_hbm, out_shape, scratch_shapes, flops, room=24, **sizes):
    held, fetched = pl.BlockSpec(memory_space=pltpu.VMEM), pl.BlockSpec(memory_space=pltpu.HBM)
    moved = sum(operand.size * operand.dtype.itemsize for operand in operands)
    return pl.pallas_call(
        functools.partial(kernel, **sizes),
        out_shape=out_shape,
        in_specs=[fetched if place in in_hbm else held for place in range(len(operands))],
        out_specs=jax.tree.map(lambda _: held, out_shape),
        scratch_shapes=scratch_shapes,
        compiler_params=pltpu.CompilerParams(vmem_limit_bytes=room * 1024 * 1024),
        cost_estimate=pl.CostEstimate(flops=flops, bytes_accessed=moved, transcendentals=0),
    )(*operands)


def pack(tokens, expert_ids, route_weights, experts):
    row_count, width = tokens.shape
    extra = -(-3 * experts // 128) * 128
    return run(
        pack_kernel,
        (tokens, expert_ids.T, route_weights.T),
        (0, 1, 2),
        jax.ShapeDtypeStruct((row_count, width + extra), jnp.bfloat16),
        [
            pltpu.VMEM(expert_ids.shape[::-1], jnp.int32),
            pltpu.VMEM(route_weights.shape[::-1], jnp.float32),
            pltpu.SemaphoreType.DMA((3,)),
        ],
        0,
        room=60,
        experts=experts,
    )


def fetch(arrays):
    rows = sum(array.shape[0] for array in arrays)
    return run(
        fetch_kernel,
        arrays,
        range(len(arrays)),
        jax.ShapeDtypeStruct((rows, arrays[0].shape[1]), arrays[0].dtype),
        [pltpu.SemaphoreType.DMA((len(arrays),))],
        0,
    )


def gate_up(parts, row_count, weights, experts):
    part_width, width = weights[0].shape[0] // 2, weights[0].shape[1]
    blocks, starts = zip(*(block for part in parts for block in part))
    total, chunks = len(blocks) * row_count, len(parts)
    outs = run(
        gate_up_kernel,
        (*blocks, *weights),
        (),
        [jax.ShapeDtypeStruct((2, total // chunks, part_width), jnp.bfloat16)] * chunks
        + [jax.ShapeDtypeStruct((2, total // chunks, 128), jnp.float32)] * chunks,
        [pltpu.VMEM((total, width), jnp.bfloat16)],
        8 * total * width * part_width,
        experts=experts,
        starts=starts,
        row_count=row_count,
        chunks=chunks,
    )
    return list(zip(outs[:chunks], outs[chunks:]))


def down(own, other, share, weights, quarters):
    total = own.shape[1]
    depth, width = weights[0].shape
    sizes = [(len(places) * total // 4, width) for places in quarters]
    return run(
        down_kernel,
        (own, other, share, *weights),
        (),
        [jax.ShapeDtypeStruct(sizes[0], jnp.float32)]
        + [jax.ShapeDtypeStruct(size, jnp.bfloat16) for size in sizes[1:]],
        [],
        4 * total * depth * width,
        quarters=quarters,
    )


def by_rows(tokens, expert_ids, route_weights, gate_local, up_local, down_local):
    row_count = tokens.shape[0]
    experts = lax.axis_size("node") * lax.axis_size("local")
    places = lax.axis_size("local")
    plane = lax.axis_index("rep")
    together = lax.optimization_barrier

    packed = pack(tokens, expert_ids, route_weights, experts)
    line_3, line_1, square_0, gates = together(
        (
            swap(packed, "local", 3),
            swap(packed, "local", 1),
            square(packed),
            fetch((gate_local, up_local)),
        )
    )
    other_gates = swap(gates, "node", 1)
    block_13 = jnp.concatenate([line_1, line_3], axis=0)
    side_13, other_13, line_2 = turn(block_13, True), turn(block_13, False), swap(line_3, "local", 1)
    line_2, side_13, other_13, downs = together((line_2, side_13, other_13, fetch((down_local,))))
    square_13 = [side_13, turn(side_13, False), other_13, block_13]

    def hidden_of(*parts):
        order = (3, 0, 2, 1)
        blocks = [(square[side], row) for side in order for square, row in parts]
        return gate_up((blocks,), row_count, (gates, other_gates), experts)[0]

    def exchanged(hidden, share):
        return hidden, swap(hidden, "rep", 1), share

    hidden_b = hidden_of((square_13, 0), (square_13, row_count))
    hidden_b, square_2, other_downs = together(
        (hidden_b, square(line_2), swap(downs, "node", 1))
    )
    weights = (downs, other_downs)
    hidden_a = hidden_of((square_0, 0), (square_2, 0))
    hidden_b, hidden_a = exchanged(*hidden_b), exchanged(*hidden_a)
    keep, send_y = down(*hidden_b, weights, ((0, 2), (1, 3)))
    back_y = swap(send_y, "node", 2)
    keep_a, send_y, send_x, send_across = down(*hidden_a, weights, ((0,), (1,), (2,), (3,)))
    across = swap(send_across, ("rep", "node"), lax.axis_size("node") | 2)
    along_x, along_y = swap(send_x, "rep", 1), swap(send_y, "node", 2)
    here, there = narrow(keep + wide(back_y)).reshape(2, 2 * row_count, -1)
    there = swap(there, ("rep", "local"), places | 1)
    here = swap(here, "local", 1)
    along_x, across, here, there = together((along_x, across, here, there))
    own = keep_a + wide(along_y) + wide(here)
    other = wide(along_x) + wide(across) + wide(there)
    total = jnp.stack([own, other]).reshape(2, 2, row_count, -1)
    own, other = narrow(total[:, 0] + wide(swap(narrow(total[:, 1]), "local", 2)))
    return jnp.where(
        plane == 0,
        jnp.concatenate([own, other], axis=1),
        jnp.concatenate([other, own], axis=1),
    )


def on_device(tokens, expert_ids, route_weights, gate_weight, up_weight, down_weight):
    row_count, top_count = expert_ids.shape
    expert_count = lax.axis_size("node") * lax.axis_size("local")
    slot_cap = min(row_count, max(2, 2 * row_count * top_count // expert_count))
    weights = (gate_weight[0], up_weight[0], down_weight[0])
    if slot_cap == row_count:
        return by_rows(tokens, expert_ids, route_weights, *weights)
    return by_slots(tokens, expert_ids, route_weights, *weights, slot_cap)


def solution(mesh):
    placed = (
        P(EVERY, None),
        P(EVERY, None),
        P(EVERY, None),
        P(PLANE, "rep", None),
        P(PLANE, "rep", None),
        P(PLANE, None, "rep"),
    )
    return jax.shard_map(
        on_device,
        mesh=mesh,
        in_specs=placed,
        out_specs=P(EVERY, None),
        check_vma=False,
    )
```

```python
import functools
import math

import jax
import jax.numpy as jnp
from jax import lax
from jax.experimental import pallas as pl
from jax.experimental.pallas import tpu as pltpu
from jax.sharding import PartitionSpec as P

PLANE = ("node", "local")
EVERY = ("rep", "node", "local")


def slot_table(expert_ids, expert_count, slot_cap):
    row_count, top_count = expert_ids.shape
    flat_ids = expert_ids.reshape(-1)
    hits = (flat_ids[:, None] == jnp.arange(expert_count, dtype=jnp.int32)[None, :]).astype(
        jnp.int32
    )
    before = jnp.cumsum(hits, axis=0) - hits
    rank_of = jnp.sum(before * hits, axis=1)
    return (flat_ids * slot_cap + rank_of).reshape(row_count, top_count)


def route_slots(blocks):
    return lax.all_to_all(blocks, PLANE, split_axis=1, concat_axis=1, tiled=True)


def by_slots(tokens, expert_ids, route_weights, gate_local, up_local, down_local, slot_cap):
    model_width = tokens.shape[1]
    plane_count = lax.axis_size("rep")
    expert_count = lax.axis_size("node") * lax.axis_size("local")
    slot_total = expert_count * slot_cap
    slot_of = slot_table(expert_ids, expert_count, slot_cap)
    slot_iota = jnp.arange(slot_total, dtype=jnp.int32)
    placed = jnp.any(slot_of[None, :, :] == slot_iota[:, None, None], axis=2).astype(jnp.bfloat16)
    outgoing = jnp.dot(placed, tokens, preferred_element_type=jnp.float32).astype(jnp.bfloat16)
    mixing = jnp.sum(
        jnp.where(slot_of[:, :, None] == slot_iota[None, None, :], route_weights[:, :, None], 0.0),
        axis=1,
    )
    arrived = route_slots(outgoing.reshape(1, expert_count, slot_cap, model_width))
    arrived = arrived.reshape(slot_total, model_width)
    shard_piece = lax.all_gather(arrived, "rep", axis=0, tiled=True)
    hidden_part = hidden_units(shard_piece, gate_local, up_local)
    expert_out = jnp.dot(
        lax.all_gather(hidden_part, "rep", axis=1, tiled=True),
        down_local,
        preferred_element_type=jnp.float32,
    ).astype(jnp.bfloat16)
    own_slots = lax.all_to_all(
        expert_out.reshape(plane_count, slot_total, down_local.shape[1]),
        "rep",
        split_axis=0,
        concat_axis=2,
        tiled=True,
    )
    returned = route_slots(own_slots.reshape(1, expert_count, slot_cap, model_width))
    back_rows = returned.reshape(slot_total, model_width).astype(jnp.float32)
    mixed_rows = jnp.dot(mixing, back_rows, precision=lax.Precision.HIGHEST)
    return mixed_rows.astype(jnp.bfloat16)


def hidden_units(rows, gate_local, up_local):
    feature_dims = (((1,), (1,)), ((), ()))
    gate = lax.dot_general(rows, gate_local, feature_dims, preferred_element_type=jnp.float32)
    up = lax.dot_general(rows, up_local, feature_dims, preferred_element_type=jnp.float32)
    return (jax.nn.silu(gate) * up).astype(jnp.bfloat16)


def swap(block, axes, mask):
    size = lax.axis_size(axes)
    return lax.ppermute(block, axes, [(place, place ^ mask) for place in range(size)])


def turn(block, first):
    nodes, size = lax.axis_size("node"), lax.axis_size(("rep", "node"))
    mask_of = [2 if (place % 2 == 0) == first else nodes for place in range(size)]
    pairs = [(place, place ^ mask) for place, mask in enumerate(mask_of)]
    return lax.ppermute(block, ("rep", "node"), pairs)


def square(block):
    side = turn(block, True)
    other_side = turn(block, False)
    return [side, turn(side, False), other_side, block]


def wide(block):
    return block.astype(jnp.float32)


def narrow(block):
    return block.astype(jnp.bfloat16)


def pack_kernel(tokens_in, ids_in, weights_in, out_ref, ids_ref, weights_ref, sems, *, experts):
    row_count, width = tokens_in.shape
    tokens_copy = pltpu.make_async_copy(tokens_in, out_ref.at[:, pl.ds(0, width)], sems.at[0])
    ids_copy = pltpu.make_async_copy(ids_in, ids_ref, sems.at[1])
    weights_copy = pltpu.make_async_copy(weights_in, weights_ref, sems.at[2])
    tokens_copy.start()
    ids_copy.start()
    weights_copy.start()
    extra = out_ref.shape[1] - width
    expert = lax.broadcasted_iota(jnp.int32, (extra, row_count), 0) % experts
    share = jnp.zeros(expert.shape, jnp.float32)
    ids_copy.wait()
    weights_copy.wait()
    for k in range(ids_ref.shape[0]):
        share += jnp.where(ids_ref[k : k + 1, :] == expert, weights_ref[k : k + 1, :], 0.0)
    share = jnp.concatenate([share, jnp.zeros((extra, extra - row_count), jnp.float32)], axis=1)
    share = share.T[:row_count]
    piece = lax.broadcasted_iota(jnp.int32, share.shape, 1) // experts
    high = wide(narrow(share))
    middle = wide(narrow(share - high))
    low = share - high - middle
    coded = jnp.where(piece == 0, high, jnp.where(piece == 1, middle, low))
    out_ref[:, width:] = narrow(jnp.where(piece < 3, coded, 0.0))
    tokens_copy.wait()


def fetch_kernel(*refs):
    *parts, out_ref, sems = refs
    row, copies = 0, []
    for place, part in enumerate(parts):
        rows = part.shape[0]
        there = out_ref.at[pl.ds(row, rows), :]
        copies.append(pltpu.make_async_copy(part, there, sems.at[place]))
        copies[-1].start()
        row += rows
    for copy in copies:
        copy.wait()


def gate_up_kernel(*refs, experts, starts, row_count, chunks):
    rows, out_refs = refs[-1], refs[-1 - 2 * chunks : -1]
    block_refs, weight_refs = refs[: len(starts)], refs[len(starts) : len(starts) + 2]
    part_width, width = weight_refs[0].shape[0] // 2, weight_refs[0].shape[1]
    own = lax.axis_index("node") * lax.axis_size("local") + lax.axis_index("local")
    other = own + lax.axis_size("local") * (1 - 2 * (lax.axis_index("node") % 2))
    lanes = lax.broadcasted_iota(jnp.int32, (row_count, block_refs[0].shape[1] - width), 1)
    coded = [
        (lanes % experts == expert) & (lanes < 3 * experts) for expert in (own, other)
    ]
    each = len(starts) // chunks
    core = lax.axis_index("node") % 2
    for place, (block, start) in enumerate(zip(block_refs, starts)):
        there = slice(start, start + row_count)
        chunk, (side, inner) = place // each, divmod(place % each, each // 4)
        if side in (1, 2):
            side = jnp.where(core == 0, side, 3 - side)
        first = pl.multiple_of((side * (each // 4) + inner) * row_count, row_count)
        rows[pl.ds(first + chunk * each * row_count, row_count), :] = block[there, :width]
        pieces = wide(block[there, width:])
        share_ref = out_refs[chunks + chunk]
        for expert in range(2):
            share = jnp.sum(jnp.where(coded[expert], pieces, 0.0), axis=1, keepdims=True)
            share = jnp.broadcast_to(share, (row_count, share_ref.shape[2]))
            share_ref[expert, pl.ds(first, row_count), :] = share
    feature_dims = (((1,), (1,)), ((), ()))
    for side, weights in enumerate(weight_refs):
        both = lax.dot_general(
            weights[...], rows[...], feature_dims, preferred_element_type=jnp.float32
        )
        gate, up = both[:part_width], both[part_width:]
        hidden = narrow((gate * up / (1.0 + jnp.exp(-gate))).T)
        for chunk, hidden_ref in enumerate(out_refs[:chunks]):
            total = hidden_ref.shape[1]
            hidden_ref[side] = hidden[chunk * total : (chunk + 1) * total]


def down_kernel(own_ref, other_ref, share_ref, down_own, down_other, *out_refs, quarters):
    plane = lax.axis_index("rep")
    width = down_own.shape[1]
    tile = math.gcd(width, 512)
    total = own_ref.shape[1]
    half, quarter = total // 2, total // 4
    hidden = []
    for side in range(2):
        own = own_ref[side]
        other = jnp.concatenate([other_ref[side, half:], other_ref[side, :half]], axis=0)
        first = jnp.where(plane == 0, own, other)
        second = jnp.where(plane == 0, other, own)
        hidden.append(jnp.concatenate([first, second], axis=1))
    for start in range(0, width, tile):
        here = slice(start, start + tile)
        term = 0.0
        for side, part in enumerate((down_own, down_other)):
            out = jnp.dot(hidden[side], part[:, here], preferred_element_type=jnp.float32)
            term += share_ref[side, :, :1] * wide(narrow(out))
        for out_ref, places in zip(out_refs, quarters):
            rows = [term[place * quarter : (place + 1) * quarter] for place in places]
            out_ref[:, here] = jnp.concatenate(rows, axis=0).astype(out_ref.dtype)


def run(kernel, operands, in_hbm, out_shape, scratch_shapes, flops, room=24, **sizes):
    held, fetched = pl.BlockSpec(memory_space=pltpu.VMEM), pl.BlockSpec(memory_space=pltpu.HBM)
    moved = sum(operand.size * operand.dtype.itemsize for operand in operands)
    return pl.pallas_call(
        functools.partial(kernel, **sizes),
        out_shape=out_shape,
        in_specs=[fetched if place in in_hbm else held for place in range(len(operands))],
        out_specs=jax.tree.map(lambda _: held, out_shape),
        scratch_shapes=scratch_shapes,
        compiler_params=pltpu.CompilerParams(vmem_limit_bytes=room * 1024 * 1024),
        cost_estimate=pl.CostEstimate(flops=flops, bytes_accessed=moved, transcendentals=0),
    )(*operands)


def pack(tokens, expert_ids, route_weights, experts):
    row_count, width = tokens.shape
    extra = -(-3 * experts // 128) * 128
    return run(
        pack_kernel,
        (tokens, expert_ids.T, route_weights.T),
        (0, 1, 2),
        jax.ShapeDtypeStruct((row_count, width + extra), jnp.bfloat16),
        [
            pltpu.VMEM(expert_ids.shape[::-1], jnp.int32),
            pltpu.VMEM(route_weights.shape[::-1], jnp.float32),
            pltpu.SemaphoreType.DMA((3,)),
        ],
        0,
        room=60,
        experts=experts,
    )


def fetch(arrays):
    rows = sum(array.shape[0] for array in arrays)
    return run(
        fetch_kernel,
        arrays,
        range(len(arrays)),
        jax.ShapeDtypeStruct((rows, arrays[0].shape[1]), arrays[0].dtype),
        [pltpu.SemaphoreType.DMA((len(arrays),))],
        0,
    )


def gate_up(parts, row_count, weights, experts):
    part_width, width = weights[0].shape[0] // 2, weights[0].shape[1]
    blocks, starts = zip(*(block for part in parts for block in part))
    total, chunks = len(blocks) * row_count, len(parts)
    outs = run(
        gate_up_kernel,
        (*blocks, *weights),
        (),
        [jax.ShapeDtypeStruct((2, total // chunks, part_width), jnp.bfloat16)] * chunks
        + [jax.ShapeDtypeStruct((2, total // chunks, 128), jnp.float32)] * chunks,
        [pltpu.VMEM((total, width), jnp.bfloat16)],
        8 * total * width * part_width,
        experts=experts,
        starts=starts,
        row_count=row_count,
        chunks=chunks,
    )
    return list(zip(outs[:chunks], outs[chunks:]))


def down(own, other, share, weights, quarters):
    total = own.shape[1]
    depth, width = weights[0].shape
    sizes = [(len(places) * total // 4, width) for places in quarters]
    return run(
        down_kernel,
        (own, other, share, *weights),
        (),
        [jax.ShapeDtypeStruct(sizes[0], jnp.float32)]
        + [jax.ShapeDtypeStruct(size, jnp.bfloat16) for size in sizes[1:]],
        [],
        4 * total * depth * width,
        quarters=quarters,
    )


def by_rows(tokens, expert_ids, route_weights, gate_local, up_local, down_local):
    row_count = tokens.shape[0]
    experts = lax.axis_size("node") * lax.axis_size("local")
    places = lax.axis_size("local")
    plane = lax.axis_index("rep")
    together = lax.optimization_barrier

    packed = pack(tokens, expert_ids, route_weights, experts)
    line_1, line_3, square_0, gates = together(
        (
            swap(packed, "local", 1),
            swap(packed, "local", 3),
            square(packed),
            fetch((gate_local, up_local)),
        )
    )
    other_gates = swap(gates, "node", 1)
    block_13 = jnp.concatenate([line_1, line_3], axis=0)
    side_13, other_13, line_2 = turn(block_13, True), turn(block_13, False), swap(line_3, "local", 1)
    line_2, side_13, other_13, downs = together((line_2, side_13, other_13, fetch((down_local,))))
    square_13 = [side_13, turn(side_13, False), other_13, block_13]

    def hidden_of(*parts):
        order = (3, 0, 2, 1)
        blocks = [(square[side], row) for side in order for square, row in parts]
        return gate_up((blocks,), row_count, (gates, other_gates), experts)[0]

    def exchanged(hidden, share):
        return hidden, swap(hidden, "rep", 1), share

    hidden_b = hidden_of((square_13, 0), (square_13, row_count))
    hidden_b, square_2, other_downs = together(
        (hidden_b, square(line_2), swap(downs, "node", 1))
    )
    weights = (downs, other_downs)
    hidden_a = hidden_of((square_0, 0), (square_2, 0))
    hidden_b, hidden_a = exchanged(*hidden_b), exchanged(*hidden_a)
    keep, send_y = down(*hidden_b, weights, ((0, 2), (1, 3)))
    back_y = swap(send_y, "node", 2)
    keep_a, send_y, send_x, send_across = down(*hidden_a, weights, ((0,), (1,), (2,), (3,)))
    across = swap(send_across, ("rep", "node"), lax.axis_size("node") | 2)
    along_x, along_y = swap(send_x, "rep", 1), swap(send_y, "node", 2)
    here, there = narrow(keep + wide(back_y)).reshape(2, 2 * row_count, -1)
    there = swap(there, ("rep", "local"), places | 1)
    here = swap(here, "local", 1)
    own = keep_a + wide(along_y) + wide(here)
    other = wide(along_x) + wide(across) + wide(there)
    total = jnp.stack([own, other]).reshape(2, 2, row_count, -1)
    own, other = narrow(total[:, 0] + wide(swap(narrow(total[:, 1]), "local", 2)))
    return jnp.where(
        plane == 0,
        jnp.concatenate([own, other], axis=1),
        jnp.concatenate([other, own], axis=1),
    )


def on_device(tokens, expert_ids, route_weights, gate_weight, up_weight, down_weight):
    row_count, top_count = expert_ids.shape
    expert_count = lax.axis_size("node") * lax.axis_size("local")
    slot_cap = min(row_count, max(2, 2 * row_count * top_count // expert_count))
    weights = (gate_weight[0], up_weight[0], down_weight[0])
    if slot_cap == row_count:
        return by_rows(tokens, expert_ids, route_weights, *weights)
    return by_slots(tokens, expert_ids, route_weights, *weights, slot_cap)


def solution(mesh):
    placed = (
        P(EVERY, None),
        P(EVERY, None),
        P(EVERY, None),
        P(PLANE, "rep", None),
        P(PLANE, "rep", None),
        P(PLANE, None, "rep"),
    )
    return jax.shard_map(
        on_device,
        mesh=mesh,
        in_specs=placed,
        out_specs=P(EVERY, None),
        check_vma=False,
    )
```

```python
import functools
import math

import jax
import jax.numpy as jnp
from jax import lax
from jax.experimental import pallas as pl
from jax.experimental.pallas import tpu as pltpu
from jax.sharding import PartitionSpec as P

PLANE = ("node", "local")
EVERY = ("rep", "node", "local")


def slot_table(expert_ids, expert_count, slot_cap):
    row_count, top_count = expert_ids.shape
    flat_ids = expert_ids.reshape(-1)
    hits = (flat_ids[:, None] == jnp.arange(expert_count, dtype=jnp.int32)[None, :]).astype(
        jnp.int32
    )
    before = jnp.cumsum(hits, axis=0) - hits
    rank_of = jnp.sum(before * hits, axis=1)
    return (flat_ids * slot_cap + rank_of).reshape(row_count, top_count)


def route_slots(blocks):
    return lax.all_to_all(blocks, PLANE, split_axis=1, concat_axis=1, tiled=True)


def by_slots(tokens, expert_ids, route_weights, gate_local, up_local, down_local, slot_cap):
    model_width = tokens.shape[1]
    plane_count = lax.axis_size("rep")
    expert_count = lax.axis_size("node") * lax.axis_size("local")
    slot_total = expert_count * slot_cap
    slot_of = slot_table(expert_ids, expert_count, slot_cap)
    slot_iota = jnp.arange(slot_total, dtype=jnp.int32)
    placed = jnp.any(slot_of[None, :, :] == slot_iota[:, None, None], axis=2).astype(jnp.bfloat16)
    outgoing = jnp.dot(placed, tokens, preferred_element_type=jnp.float32).astype(jnp.bfloat16)
    mixing = jnp.sum(
        jnp.where(slot_of[:, :, None] == slot_iota[None, None, :], route_weights[:, :, None], 0.0),
        axis=1,
    )
    arrived = route_slots(outgoing.reshape(1, expert_count, slot_cap, model_width))
    arrived = arrived.reshape(slot_total, model_width)
    shard_piece = lax.all_gather(arrived, "rep", axis=0, tiled=True)
    hidden_part = hidden_units(shard_piece, gate_local, up_local)
    expert_out = jnp.dot(
        lax.all_gather(hidden_part, "rep", axis=1, tiled=True),
        down_local,
        preferred_element_type=jnp.float32,
    ).astype(jnp.bfloat16)
    own_slots = lax.all_to_all(
        expert_out.reshape(plane_count, slot_total, down_local.shape[1]),
        "rep",
        split_axis=0,
        concat_axis=2,
        tiled=True,
    )
    returned = route_slots(own_slots.reshape(1, expert_count, slot_cap, model_width))
    back_rows = returned.reshape(slot_total, model_width).astype(jnp.float32)
    mixed_rows = jnp.dot(mixing, back_rows, precision=lax.Precision.HIGHEST)
    return mixed_rows.astype(jnp.bfloat16)


def hidden_units(rows, gate_local, up_local):
    feature_dims = (((1,), (1,)), ((), ()))
    gate = lax.dot_general(rows, gate_local, feature_dims, preferred_element_type=jnp.float32)
    up = lax.dot_general(rows, up_local, feature_dims, preferred_element_type=jnp.float32)
    return (jax.nn.silu(gate) * up).astype(jnp.bfloat16)


def swap(block, axes, mask):
    size = lax.axis_size(axes)
    return lax.ppermute(block, axes, [(place, place ^ mask) for place in range(size)])


def turn(block, first):
    nodes, size = lax.axis_size("node"), lax.axis_size(("rep", "node"))
    mask_of = [2 if (place % 2 == 0) == first else nodes for place in range(size)]
    pairs = [(place, place ^ mask) for place, mask in enumerate(mask_of)]
    return lax.ppermute(block, ("rep", "node"), pairs)


def square(block):
    side = turn(block, True)
    other_side = turn(block, False)
    return [side, turn(side, False), other_side, block]


def wide(block):
    return block.astype(jnp.float32)


def narrow(block):
    return block.astype(jnp.bfloat16)


def pack_kernel(tokens_in, ids_in, weights_in, out_ref, ids_ref, weights_ref, sems, *, experts):
    row_count, width = tokens_in.shape
    tokens_copy = pltpu.make_async_copy(tokens_in, out_ref.at[:, pl.ds(0, width)], sems.at[0])
    ids_copy = pltpu.make_async_copy(ids_in, ids_ref, sems.at[1])
    weights_copy = pltpu.make_async_copy(weights_in, weights_ref, sems.at[2])
    tokens_copy.start()
    ids_copy.start()
    weights_copy.start()
    extra = out_ref.shape[1] - width
    expert = lax.broadcasted_iota(jnp.int32, (extra, row_count), 0) % experts
    share = jnp.zeros(expert.shape, jnp.float32)
    ids_copy.wait()
    weights_copy.wait()
    for k in range(ids_ref.shape[0]):
        share += jnp.where(ids_ref[k : k + 1, :] == expert, weights_ref[k : k + 1, :], 0.0)
    share = jnp.concatenate([share, jnp.zeros((extra, extra - row_count), jnp.float32)], axis=1)
    share = share.T[:row_count]
    piece = lax.broadcasted_iota(jnp.int32, share.shape, 1) // experts
    high = wide(narrow(share))
    middle = wide(narrow(share - high))
    low = share - high - middle
    coded = jnp.where(piece == 0, high, jnp.where(piece == 1, middle, low))
    out_ref[:, width:] = narrow(jnp.where(piece < 3, coded, 0.0))
    tokens_copy.wait()


def fetch_kernel(*refs):
    *parts, out_ref, sems = refs
    row, copies = 0, []
    for place, part in enumerate(parts):
        rows = part.shape[0]
        there = out_ref.at[pl.ds(row, rows), :]
        copies.append(pltpu.make_async_copy(part, there, sems.at[place]))
        copies[-1].start()
        row += rows
    for copy in copies:
        copy.wait()


def gate_up_kernel(*refs, experts, starts, row_count, chunks):
    rows, out_refs = refs[-1], refs[-1 - 2 * chunks : -1]
    block_refs, weight_refs = refs[: len(starts)], refs[len(starts) : len(starts) + 2]
    part_width, width = weight_refs[0].shape[0] // 2, weight_refs[0].shape[1]
    own = lax.axis_index("node") * lax.axis_size("local") + lax.axis_index("local")
    other = own + lax.axis_size("local") * (1 - 2 * (lax.axis_index("node") % 2))
    lanes = lax.broadcasted_iota(jnp.int32, (row_count, block_refs[0].shape[1] - width), 1)
    coded = [
        (lanes % experts == expert) & (lanes < 3 * experts) for expert in (own, other)
    ]
    each = len(starts) // chunks
    core = lax.axis_index("node") % 2
    for place, (block, start) in enumerate(zip(block_refs, starts)):
        there = slice(start, start + row_count)
        chunk, (side, inner) = place // each, divmod(place % each, each // 4)
        if side in (1, 2):
            side = jnp.where(core == 0, side, 3 - side)
        first = pl.multiple_of((side * (each // 4) + inner) * row_count, row_count)
        rows[pl.ds(first + chunk * each * row_count, row_count), :] = block[there, :width]
        pieces = wide(block[there, width:])
        share_ref = out_refs[chunks + chunk]
        for expert in range(2):
            share = jnp.sum(jnp.where(coded[expert], pieces, 0.0), axis=1, keepdims=True)
            share = jnp.broadcast_to(share, (row_count, share_ref.shape[2]))
            share_ref[expert, pl.ds(first, row_count), :] = share
    feature_dims = (((1,), (1,)), ((), ()))
    for side, weights in enumerate(weight_refs):
        both = lax.dot_general(
            weights[...], rows[...], feature_dims, preferred_element_type=jnp.float32
        )
        gate, up = both[:part_width], both[part_width:]
        hidden = narrow((gate * up / (1.0 + jnp.exp(-gate))).T)
        for chunk, hidden_ref in enumerate(out_refs[:chunks]):
            total = hidden_ref.shape[1]
            hidden_ref[side] = hidden[chunk * total : (chunk + 1) * total]


def down_kernel(own_ref, other_ref, share_ref, down_own, down_other, *out_refs, quarters):
    plane = lax.axis_index("rep")
    width = down_own.shape[1]
    tile = math.gcd(width, 512)
    total = own_ref.shape[1]
    half, quarter = total // 2, total // 4
    hidden = []
    for side in range(2):
        own = own_ref[side]
        other = jnp.concatenate([other_ref[side, half:], other_ref[side, :half]], axis=0)
        first = jnp.where(plane == 0, own, other)
        second = jnp.where(plane == 0, other, own)
        hidden.append(jnp.concatenate([first, second], axis=1))
    for start in range(0, width, tile):
        here = slice(start, start + tile)
        term = 0.0
        for side, part in enumerate((down_own, down_other)):
            out = jnp.dot(hidden[side], part[:, here], preferred_element_type=jnp.float32)
            term += share_ref[side, :, :1] * wide(narrow(out))
        for out_ref, places in zip(out_refs, quarters):
            rows = [term[place * quarter : (place + 1) * quarter] for place in places]
            out_ref[:, here] = jnp.concatenate(rows, axis=0).astype(out_ref.dtype)


def run(kernel, operands, in_hbm, out_shape, scratch_shapes, flops, room=24, **sizes):
    held, fetched = pl.BlockSpec(memory_space=pltpu.VMEM), pl.BlockSpec(memory_space=pltpu.HBM)
    moved = sum(operand.size * operand.dtype.itemsize for operand in operands)
    return pl.pallas_call(
        functools.partial(kernel, **sizes),
        out_shape=out_shape,
        in_specs=[fetched if place in in_hbm else held for place in range(len(operands))],
        out_specs=jax.tree.map(lambda _: held, out_shape),
        scratch_shapes=scratch_shapes,
        compiler_params=pltpu.CompilerParams(vmem_limit_bytes=room * 1024 * 1024),
        cost_estimate=pl.CostEstimate(flops=flops, bytes_accessed=moved, transcendentals=0),
    )(*operands)


def pack(tokens, expert_ids, route_weights, experts):
    row_count, width = tokens.shape
    extra = -(-3 * experts // 128) * 128
    return run(
        pack_kernel,
        (tokens, expert_ids.T, route_weights.T),
        (0, 1, 2),
        jax.ShapeDtypeStruct((row_count, width + extra), jnp.bfloat16),
        [
            pltpu.VMEM(expert_ids.shape[::-1], jnp.int32),
            pltpu.VMEM(route_weights.shape[::-1], jnp.float32),
            pltpu.SemaphoreType.DMA((3,)),
        ],
        0,
        room=60,
        experts=experts,
    )


def fetch(arrays):
    rows = sum(array.shape[0] for array in arrays)
    return run(
        fetch_kernel,
        arrays,
        range(len(arrays)),
        jax.ShapeDtypeStruct((rows, arrays[0].shape[1]), arrays[0].dtype),
        [pltpu.SemaphoreType.DMA((len(arrays),))],
        0,
    )


def gate_up(parts, row_count, weights, experts):
    part_width, width = weights[0].shape[0] // 2, weights[0].shape[1]
    blocks, starts = zip(*(block for part in parts for block in part))
    total, chunks = len(blocks) * row_count, len(parts)
    outs = run(
        gate_up_kernel,
        (*blocks, *weights),
        (),
        [jax.ShapeDtypeStruct((2, total // chunks, part_width), jnp.bfloat16)] * chunks
        + [jax.ShapeDtypeStruct((2, total // chunks, 128), jnp.float32)] * chunks,
        [pltpu.VMEM((total, width), jnp.bfloat16)],
        8 * total * width * part_width,
        experts=experts,
        starts=starts,
        row_count=row_count,
        chunks=chunks,
    )
    return list(zip(outs[:chunks], outs[chunks:]))


def down(own, other, share, weights, quarters):
    total = own.shape[1]
    depth, width = weights[0].shape
    sizes = [(len(places) * total // 4, width) for places in quarters]
    return run(
        down_kernel,
        (own, other, share, *weights),
        (),
        [jax.ShapeDtypeStruct(sizes[0], jnp.float32)]
        + [jax.ShapeDtypeStruct(size, jnp.bfloat16) for size in sizes[1:]],
        [],
        4 * total * depth * width,
        quarters=quarters,
    )


def by_rows(tokens, expert_ids, route_weights, gate_local, up_local, down_local):
    row_count = tokens.shape[0]
    experts = lax.axis_size("node") * lax.axis_size("local")
    places = lax.axis_size("local")
    plane = lax.axis_index("rep")
    together = lax.optimization_barrier

    packed = pack(tokens, expert_ids, route_weights, experts)
    line_3, line_1, square_0, gates = together(
        (
            swap(packed, "local", 3),
            swap(packed, "local", 1),
            square(packed),
            fetch((gate_local, up_local)),
        )
    )
    other_gates = swap(gates, "node", 1)
    block_13 = jnp.concatenate([line_1, line_3], axis=0)
    side_13, other_13, line_2 = turn(block_13, True), turn(block_13, False), swap(line_3, "local", 1)
    line_2, side_13, other_13, downs = together((line_2, side_13, other_13, fetch((down_local,))))
    square_13 = [side_13, turn(side_13, False), other_13, block_13]

    def hidden_of(*parts):
        order = (3, 0, 2, 1)
        blocks = [(square[side], row) for side in order for square, row in parts]
        return gate_up((blocks,), row_count, (gates, other_gates), experts)[0]

    def exchanged(hidden, share):
        return hidden, swap(hidden, "rep", 1), share

    hidden_b = hidden_of((square_13, 0), (square_13, row_count))
    hidden_b, square_2, other_downs = together(
        (hidden_b, square(line_2), swap(downs, "node", 1))
    )
    weights = (downs, other_downs)
    hidden_a = hidden_of((square_0, 0), (square_2, 0))
    hidden_b, hidden_a = exchanged(*hidden_b), exchanged(*hidden_a)
    keep, send_y = down(*hidden_b, weights, ((0, 2), (1, 3)))
    back_y = swap(send_y, "node", 2)
    keep_a, send_y, send_x, send_across = down(*hidden_a, weights, ((0,), (1,), (2,), (3,)))
    across = swap(send_across, ("rep", "node"), lax.axis_size("node") | 2)
    along_x, along_y = swap(send_x, "rep", 1), swap(send_y, "node", 2)
    here, there = narrow(keep + wide(back_y)).reshape(2, 2 * row_count, -1)
    there = swap(there, ("rep", "local"), places | 1)
    here = swap(here, "local", 1)
    across, along_x, there = together((across, along_x, there))
    own = keep_a + wide(along_y) + wide(here)
    other = wide(along_x) + wide(across) + wide(there)
    total = jnp.stack([own, other]).reshape(2, 2, row_count, -1)
    own, other = narrow(total[:, 0] + wide(swap(narrow(total[:, 1]), "local", 2)))
    return jnp.where(
        plane == 0,
        jnp.concatenate([own, other], axis=1),
        jnp.concatenate([other, own], axis=1),
    )


def on_device(tokens, expert_ids, route_weights, gate_weight, up_weight, down_weight):
    row_count, top_count = expert_ids.shape
    expert_count = lax.axis_size("node") * lax.axis_size("local")
    slot_cap = min(row_count, max(2, 2 * row_count * top_count // expert_count))
    weights = (gate_weight[0], up_weight[0], down_weight[0])
    if slot_cap == row_count:
        return by_rows(tokens, expert_ids, route_weights, *weights)
    return by_slots(tokens, expert_ids, route_weights, *weights, slot_cap)


def solution(mesh):
    placed = (
        P(EVERY, None),
        P(EVERY, None),
        P(EVERY, None),
        P(PLANE, "rep", None),
        P(PLANE, "rep", None),
        P(PLANE, None, "rep"),
    )
    return jax.shard_map(
        on_device,
        mesh=mesh,
        in_specs=placed,
        out_specs=P(EVERY, None),
        check_vma=False,
    )
```

```python
import functools
import math

import jax
import jax.numpy as jnp
from jax import lax
from jax.experimental import pallas as pl
from jax.experimental.pallas import tpu as pltpu
from jax.sharding import PartitionSpec as P

PLANE = ("node", "local")
EVERY = ("rep", "node", "local")


def slot_table(expert_ids, expert_count, slot_cap):
    row_count, top_count = expert_ids.shape
    flat_ids = expert_ids.reshape(-1)
    hits = (flat_ids[:, None] == jnp.arange(expert_count, dtype=jnp.int32)[None, :]).astype(
        jnp.int32
    )
    before = jnp.cumsum(hits, axis=0) - hits
    rank_of = jnp.sum(before * hits, axis=1)
    return (flat_ids * slot_cap + rank_of).reshape(row_count, top_count)


def route_slots(blocks):
    return lax.all_to_all(blocks, PLANE, split_axis=1, concat_axis=1, tiled=True)


def by_slots(tokens, expert_ids, route_weights, gate_local, up_local, down_local, slot_cap):
    model_width = tokens.shape[1]
    plane_count = lax.axis_size("rep")
    expert_count = lax.axis_size("node") * lax.axis_size("local")
    slot_total = expert_count * slot_cap
    slot_of = slot_table(expert_ids, expert_count, slot_cap)
    slot_iota = jnp.arange(slot_total, dtype=jnp.int32)
    placed = jnp.any(slot_of[None, :, :] == slot_iota[:, None, None], axis=2).astype(jnp.bfloat16)
    outgoing = jnp.dot(placed, tokens, preferred_element_type=jnp.float32).astype(jnp.bfloat16)
    mixing = jnp.sum(
        jnp.where(slot_of[:, :, None] == slot_iota[None, None, :], route_weights[:, :, None], 0.0),
        axis=1,
    )
    arrived = route_slots(outgoing.reshape(1, expert_count, slot_cap, model_width))
    arrived = arrived.reshape(slot_total, model_width)
    shard_piece = lax.all_gather(arrived, "rep", axis=0, tiled=True)
    hidden_part = hidden_units(shard_piece, gate_local, up_local)
    expert_out = jnp.dot(
        lax.all_gather(hidden_part, "rep", axis=1, tiled=True),
        down_local,
        preferred_element_type=jnp.float32,
    ).astype(jnp.bfloat16)
    own_slots = lax.all_to_all(
        expert_out.reshape(plane_count, slot_total, down_local.shape[1]),
        "rep",
        split_axis=0,
        concat_axis=2,
        tiled=True,
    )
    returned = route_slots(own_slots.reshape(1, expert_count, slot_cap, model_width))
    back_rows = returned.reshape(slot_total, model_width).astype(jnp.float32)
    mixed_rows = jnp.dot(mixing, back_rows, precision=lax.Precision.HIGHEST)
    return mixed_rows.astype(jnp.bfloat16)


def hidden_units(rows, gate_local, up_local):
    feature_dims = (((1,), (1,)), ((), ()))
    gate = lax.dot_general(rows, gate_local, feature_dims, preferred_element_type=jnp.float32)
    up = lax.dot_general(rows, up_local, feature_dims, preferred_element_type=jnp.float32)
    return (jax.nn.silu(gate) * up).astype(jnp.bfloat16)


def swap(block, axes, mask):
    size = lax.axis_size(axes)
    return lax.ppermute(block, axes, [(place, place ^ mask) for place in range(size)])


def turn(block, first):
    nodes, size = lax.axis_size("node"), lax.axis_size(("rep", "node"))
    mask_of = [2 if (place % 2 == 0) == first else nodes for place in range(size)]
    pairs = [(place, place ^ mask) for place, mask in enumerate(mask_of)]
    return lax.ppermute(block, ("rep", "node"), pairs)


def square(block):
    side = turn(block, True)
    other_side = turn(block, False)
    return [side, turn(side, False), other_side, block]


def wide(block):
    return block.astype(jnp.float32)


def narrow(block):
    return block.astype(jnp.bfloat16)


def pack_kernel(tokens_in, ids_in, weights_in, out_ref, ids_ref, weights_ref, sems, *, experts):
    row_count, width = tokens_in.shape
    tokens_copy = pltpu.make_async_copy(tokens_in, out_ref.at[:, pl.ds(0, width)], sems.at[0])
    ids_copy = pltpu.make_async_copy(ids_in, ids_ref, sems.at[1])
    weights_copy = pltpu.make_async_copy(weights_in, weights_ref, sems.at[2])
    tokens_copy.start()
    ids_copy.start()
    weights_copy.start()
    extra = out_ref.shape[1] - width
    expert = lax.broadcasted_iota(jnp.int32, (extra, row_count), 0) % experts
    share = jnp.zeros(expert.shape, jnp.float32)
    ids_copy.wait()
    weights_copy.wait()
    for k in range(ids_ref.shape[0]):
        share += jnp.where(ids_ref[k : k + 1, :] == expert, weights_ref[k : k + 1, :], 0.0)
    share = jnp.concatenate([share, jnp.zeros((extra, extra - row_count), jnp.float32)], axis=1)
    share = share.T[:row_count]
    piece = lax.broadcasted_iota(jnp.int32, share.shape, 1) // experts
    high = wide(narrow(share))
    middle = wide(narrow(share - high))
    low = share - high - middle
    coded = jnp.where(piece == 0, high, jnp.where(piece == 1, middle, low))
    out_ref[:, width:] = narrow(jnp.where(piece < 3, coded, 0.0))
    tokens_copy.wait()


def fetch_kernel(*refs):
    *parts, out_ref, sems = refs
    row, copies = 0, []
    for place, part in enumerate(parts):
        rows = part.shape[0]
        there = out_ref.at[pl.ds(row, rows), :]
        copies.append(pltpu.make_async_copy(part, there, sems.at[place]))
        copies[-1].start()
        row += rows
    for copy in copies:
        copy.wait()


def gate_up_kernel(*refs, experts, starts, row_count, chunks):
    rows, out_refs = refs[-1], refs[-1 - 2 * chunks : -1]
    block_refs, weight_refs = refs[: len(starts)], refs[len(starts) : len(starts) + 2]
    part_width, width = weight_refs[0].shape[0] // 2, weight_refs[0].shape[1]
    own = lax.axis_index("node") * lax.axis_size("local") + lax.axis_index("local")
    other = own + lax.axis_size("local") * (1 - 2 * (lax.axis_index("node") % 2))
    lanes = lax.broadcasted_iota(jnp.int32, (row_count, block_refs[0].shape[1] - width), 1)
    coded = [
        (lanes % experts == expert) & (lanes < 3 * experts) for expert in (own, other)
    ]
    each = len(starts) // chunks
    core = lax.axis_index("node") % 2
    for place, (block, start) in enumerate(zip(block_refs, starts)):
        there = slice(start, start + row_count)
        chunk, (side, inner) = place // each, divmod(place % each, each // 4)
        if side in (1, 2):
            side = jnp.where(core == 0, side, 3 - side)
        first = pl.multiple_of((side * (each // 4) + inner) * row_count, row_count)
        rows[pl.ds(first + chunk * each * row_count, row_count), :] = block[there, :width]
        pieces = wide(block[there, width:])
        share_ref = out_refs[chunks + chunk]
        for expert in range(2):
            share = jnp.sum(jnp.where(coded[expert], pieces, 0.0), axis=1, keepdims=True)
            share = jnp.broadcast_to(share, (row_count, share_ref.shape[2]))
            share_ref[expert, pl.ds(first, row_count), :] = share
    feature_dims = (((1,), (1,)), ((), ()))
    for side, weights in enumerate(weight_refs):
        both = lax.dot_general(
            weights[...], rows[...], feature_dims, preferred_element_type=jnp.float32
        )
        gate, up = both[:part_width], both[part_width:]
        hidden = narrow((gate * up / (1.0 + jnp.exp(-gate))).T)
        for chunk, hidden_ref in enumerate(out_refs[:chunks]):
            total = hidden_ref.shape[1]
            hidden_ref[side] = hidden[chunk * total : (chunk + 1) * total]


def down_kernel(own_ref, other_ref, share_ref, down_own, down_other, *out_refs, quarters):
    plane = lax.axis_index("rep")
    width = down_own.shape[1]
    tile = math.gcd(width, 1024)
    total = own_ref.shape[1]
    half, quarter = total // 2, total // 4
    hidden = []
    for side in range(2):
        own = own_ref[side]
        other = jnp.concatenate([other_ref[side, half:], other_ref[side, :half]], axis=0)
        first = jnp.where(plane == 0, own, other)
        second = jnp.where(plane == 0, other, own)
        hidden.append(jnp.concatenate([first, second], axis=1))
    for start in range(0, width, tile):
        here = slice(start, start + tile)
        term = 0.0
        for side, part in enumerate((down_own, down_other)):
            out = jnp.dot(hidden[side], part[:, here], preferred_element_type=jnp.float32)
            term += share_ref[side, :, :1] * wide(narrow(out))
        for out_ref, places in zip(out_refs, quarters):
            rows = [term[place * quarter : (place + 1) * quarter] for place in places]
            out_ref[:, here] = jnp.concatenate(rows, axis=0).astype(out_ref.dtype)


def run(kernel, operands, in_hbm, out_shape, scratch_shapes, flops, room=24, **sizes):
    held, fetched = pl.BlockSpec(memory_space=pltpu.VMEM), pl.BlockSpec(memory_space=pltpu.HBM)
    moved = sum(operand.size * operand.dtype.itemsize for operand in operands)
    return pl.pallas_call(
        functools.partial(kernel, **sizes),
        out_shape=out_shape,
        in_specs=[fetched if place in in_hbm else held for place in range(len(operands))],
        out_specs=jax.tree.map(lambda _: held, out_shape),
        scratch_shapes=scratch_shapes,
        compiler_params=pltpu.CompilerParams(vmem_limit_bytes=room * 1024 * 1024),
        cost_estimate=pl.CostEstimate(flops=flops, bytes_accessed=moved, transcendentals=0),
    )(*operands)


def pack(tokens, expert_ids, route_weights, experts):
    row_count, width = tokens.shape
    extra = -(-3 * experts // 128) * 128
    return run(
        pack_kernel,
        (tokens, expert_ids.T, route_weights.T),
        (0, 1, 2),
        jax.ShapeDtypeStruct((row_count, width + extra), jnp.bfloat16),
        [
            pltpu.VMEM(expert_ids.shape[::-1], jnp.int32),
            pltpu.VMEM(route_weights.shape[::-1], jnp.float32),
            pltpu.SemaphoreType.DMA((3,)),
        ],
        0,
        room=60,
        experts=experts,
    )


def fetch(arrays):
    rows = sum(array.shape[0] for array in arrays)
    return run(
        fetch_kernel,
        arrays,
        range(len(arrays)),
        jax.ShapeDtypeStruct((rows, arrays[0].shape[1]), arrays[0].dtype),
        [pltpu.SemaphoreType.DMA((len(arrays),))],
        0,
    )


def gate_up(parts, row_count, weights, experts):
    part_width, width = weights[0].shape[0] // 2, weights[0].shape[1]
    blocks, starts = zip(*(block for part in parts for block in part))
    total, chunks = len(blocks) * row_count, len(parts)
    outs = run(
        gate_up_kernel,
        (*blocks, *weights),
        (),
        [jax.ShapeDtypeStruct((2, total // chunks, part_width), jnp.bfloat16)] * chunks
        + [jax.ShapeDtypeStruct((2, total // chunks, 128), jnp.float32)] * chunks,
        [pltpu.VMEM((total, width), jnp.bfloat16)],
        8 * total * width * part_width,
        experts=experts,
        starts=starts,
        row_count=row_count,
        chunks=chunks,
    )
    return list(zip(outs[:chunks], outs[chunks:]))


def down(own, other, share, weights, quarters):
    total = own.shape[1]
    depth, width = weights[0].shape
    sizes = [(len(places) * total // 4, width) for places in quarters]
    return run(
        down_kernel,
        (own, other, share, *weights),
        (),
        [jax.ShapeDtypeStruct(sizes[0], jnp.float32)]
        + [jax.ShapeDtypeStruct(size, jnp.bfloat16) for size in sizes[1:]],
        [],
        4 * total * depth * width,
        quarters=quarters,
    )


def by_rows(tokens, expert_ids, route_weights, gate_local, up_local, down_local):
    row_count = tokens.shape[0]
    experts = lax.axis_size("node") * lax.axis_size("local")
    places = lax.axis_size("local")
    plane = lax.axis_index("rep")
    together = lax.optimization_barrier

    packed = pack(tokens, expert_ids, route_weights, experts)
    line_3, line_1, square_0, gates = together(
        (
            swap(packed, "local", 3),
            swap(packed, "local", 1),
            square(packed),
            fetch((gate_local, up_local)),
        )
    )
    other_gates = swap(gates, "node", 1)
    block_13 = jnp.concatenate([line_1, line_3], axis=0)
    side_13, other_13, line_2 = turn(block_13, True), turn(block_13, False), swap(line_3, "local", 1)
    line_2, side_13, other_13, downs = together((line_2, side_13, other_13, fetch((down_local,))))
    square_13 = [side_13, turn(side_13, False), other_13, block_13]

    def hidden_of(*parts):
        order = (3, 0, 2, 1)
        blocks = [(square[side], row) for side in order for square, row in parts]
        return gate_up((blocks,), row_count, (gates, other_gates), experts)[0]

    def exchanged(hidden, share):
        return hidden, swap(hidden, "rep", 1), share

    hidden_b = hidden_of((square_13, 0), (square_13, row_count))
    hidden_b, square_2, other_downs = together(
        (hidden_b, square(line_2), swap(downs, "node", 1))
    )
    weights = (downs, other_downs)
    hidden_a = hidden_of((square_0, 0), (square_2, 0))
    hidden_b, hidden_a = exchanged(*hidden_b), exchanged(*hidden_a)
    keep, send_y = down(*hidden_b, weights, ((0, 2), (1, 3)))
    back_y = swap(send_y, "node", 2)
    keep_a, send_y, send_x, send_across = down(*hidden_a, weights, ((0,), (1,), (2,), (3,)))
    across = swap(send_across, ("rep", "node"), lax.axis_size("node") | 2)
    along_x, along_y = swap(send_x, "rep", 1), swap(send_y, "node", 2)
    here, there = narrow(keep + wide(back_y)).reshape(2, 2 * row_count, -1)
    there = swap(there, ("rep", "local"), places | 1)
    here = swap(here, "local", 1)
    own = keep_a + wide(along_y) + wide(here)
    other = wide(along_x) + wide(across) + wide(there)
    total = jnp.stack([own, other]).reshape(2, 2, row_count, -1)
    own, other = narrow(total[:, 0] + wide(swap(narrow(total[:, 1]), "local", 2)))
    return jnp.where(
        plane == 0,
        jnp.concatenate([own, other], axis=1),
        jnp.concatenate([other, own], axis=1),
    )


def on_device(tokens, expert_ids, route_weights, gate_weight, up_weight, down_weight):
    row_count, top_count = expert_ids.shape
    expert_count = lax.axis_size("node") * lax.axis_size("local")
    slot_cap = min(row_count, max(2, 2 * row_count * top_count // expert_count))
    weights = (gate_weight[0], up_weight[0], down_weight[0])
    if slot_cap == row_count:
        return by_rows(tokens, expert_ids, route_weights, *weights)
    return by_slots(tokens, expert_ids, route_weights, *weights, slot_cap)


def solution(mesh):
    placed = (
        P(EVERY, None),
        P(EVERY, None),
        P(EVERY, None),
        P(PLANE, "rep", None),
        P(PLANE, "rep", None),
        P(PLANE, None, "rep"),
    )
    return jax.shard_map(
        on_device,
        mesh=mesh,
        in_specs=placed,
        out_specs=P(EVERY, None),
        check_vma=False,
    )
```
